256 devices in a mesh: pop: 32 (over x_hi, z, core), wa: 8 (over x_lo, y).
Axes of the slice: x: 4 (x_hi: 2, x_lo: 2; x = x_hi * 2 + x_lo), y: 4, z: 8, core: 2. Of those that a mesh axis runs over, the one named last changes fastest.
Arguments:
- inputs: bfloat16 [8192, 24, 4096], P('pop', 'wa'), may hold values from -6 to 6
- weight: bfloat16 [2048, 4096], P(None, 'wa'), may hold values from -0.09375 to 0.09375
- factor_in: bfloat16 [8192, 4096], P('pop'), may hold values from -0.09375 to 0.09375
- factor_out: bfloat16 [8192, 2048], P('pop'), may hold values from -6 to 6
- readout: float32 [2048], replicated, may hold values from -0.125 to 0.125
Outputs:
- weight_step: float32 [2048, 4096], P('pop', 'wa')
- utilities: float32 [8192], P('pop')
The draws below stay inside these ranges and needn't reach their ends.
All inputs are finite; a program needn't handle non-finite values.
Results may differ from the reference program's by a relative error of at most 0.0029.
Values may be sent and summed in bfloat16 or wider, within the bound.
No kernel may reach another device: no remote copies, remote signals or barrier semaphores. Data moves between devices by JAX's collectives and lax.ppermute only.
A program may use at most 128 MiB of HBM per device.

```python
import jax
import jax.numpy as jnp
from jax import lax

D = 4096
OUT = 2048
MEM_DEV = 256
MEMBERS = 8192
ROWS = 24


def level_of(stream_key, shape, shards, smallest, largest):
    def one(axis_at, parts):
        heights = jax.random.uniform(jax.random.fold_in(jax.random.fold_in(stream_key, 6), axis_at), (parts,), jnp.float32, smallest / len(shards), largest / len(shards))
        return jnp.repeat(jnp.exp(heights), shape[axis_at] // parts).reshape((-1,) + (1,) * (len(shape) - axis_at - 1))

    loudness = one(*shards[0])
    for cut in shards[1:]:
        loudness = loudness * one(*cut)
    return loudness


def bell_draw(own_key, shape, deviation, bound, pieces=(), dtype=jnp.bfloat16):
    drawn = jax.random.normal(own_key, shape, jnp.float32) * deviation
    if len(pieces) > 0:
        drawn = level_of(own_key, shape, pieces, -0.22, 0.18) * drawn
    return jnp.clip(drawn, min=-bound, max=bound).astype(dtype)


def setup_inputs(seed: int = 0) -> dict:
    key_of = jax.random.split(jax.random.key(seed), 6)
    inputs = bell_draw(key_of[0], (MEMBERS, ROWS, D), 1.0, 6.0, ((0, 32), (1, 8)))
    weight = bell_draw(key_of[1], (OUT, D), D ** -0.5, 0.09375, ((1, 8),))
    factor_in = bell_draw(key_of[2], (MEMBERS, D), D ** -0.5, 0.09375, ((0, 32),))
    factor_out = bell_draw(key_of[3], (MEMBERS, OUT), 1.0, 6.0, ((0, 32),))
    readout = bell_draw(key_of[4], (OUT,), OUT ** -0.5, 0.125, (), jnp.float32)
    return dict(inputs=inputs, weight=weight, factor_in=factor_in, factor_out=factor_out, readout=readout)


perturb_scale = 0.5
epsilon = 1e-05

def reference(inputs, weight, factor_in, factor_out, readout):
    blocks = MEMBERS // MEM_DEV

    def fitness_block(packed):
        rows_blk, in_blk, out_blk = packed
        count = rows_blk.shape[0]
        flat = rows_blk.reshape(count * ROWS, D)
        proj = lax.dot_general(flat, weight, (((1,), (1,)), ((), ())), preferred_element_type=jnp.float32)
        proj = proj.reshape(count, ROWS, OUT)
        low = jnp.einsum('mrd,md->mr', rows_blk.astype(jnp.float32), in_blk.astype(jnp.float32))
        pert = proj + perturb_scale * low[:, :, None] * out_blk.astype(jnp.float32)[:, None, :]
        return lax.optimization_barrier(jnp.sum(jnp.tanh(pert) * readout, axis=(1, 2))) / ROWS
    fitness = lax.map(fitness_block, (inputs.reshape(blocks, MEM_DEV, ROWS, D), factor_in.reshape(blocks, MEM_DEV, D), factor_out.reshape(blocks, MEM_DEV, OUT))).reshape(MEMBERS)
    mean = jnp.sum(fitness) / MEMBERS
    spread = jnp.sum((fitness - mean) ** 2) / MEMBERS
    utilities = (fitness - mean) / jnp.sqrt(spread + epsilon)
    scaled = (utilities[:, None] * factor_out.astype(jnp.float32)).astype(jnp.bfloat16)
    summed = jnp.dot(scaled.T, factor_in, preferred_element_type=jnp.float32)
    weight_step = summed / jnp.sqrt(jnp.float32(MEMBERS))
    return (weight_step, utilities)
```

```python
import functools

import jax
import jax.numpy as jnp
import numpy as np
from jax import lax
from jax.experimental import pallas as pl
from jax.experimental.pallas import tpu as pltpu
from jax.sharding import Mesh, PartitionSpec as P

perturb_scale = 0.5
epsilon = 1e-05

XH, Z, CORE, XL, Y = 2, 8, 2, 2, 4
AXES = ("xh", "z", "core", "xl", "y")
SIZES = (XH, Z, CORE, XL, Y)
WA = XL * Y
ROWS_ALL = 24
VMEM_BYTES = 48 * 1024 * 1024


def permutation(move):
    pairs = []
    for i in range(int(np.prod(SIZES))):
        at = [int(v) for v in np.unravel_index(i, SIZES)]
        to = move(*at)
        pairs.append((i, int(np.ravel_multi_index(to, SIZES))))
    return pairs


def go_y(step):
    def move(xh, z, c, xl, y):
        s = step if c == 0 else -step
        return (xh, z, c, xl, (y + s) % Y)

    return permutation(move)


def go_x():
    def move(xh, z, c, xl, y):
        x = xh * 2 + xl
        if c == 0:
            x = x ^ 1
        else:
            x = (x + 1) % 4 if x % 2 else (x - 1) % 4
        return (x // 2, z, c, x % 2, y)

    return permutation(move)


def go_core():
    return permutation(lambda xh, z, c, xl, y: (xh, z, 1 - c, xl, y))


def nt_dot(a, b):
    return lax.dot_general(a, b, (((1,), (1,)), ((), ())), preferred_element_type=jnp.float32)


def group_kernel(count, has_acc, kidx, *refs):
    x_own = refs[:count]
    x_oth = refs[count : 2 * count]
    ws = refs[2 * count : 3 * count]
    rest = refs[3 * count :]
    acc_in = rest[0] if has_acc else None
    out = rest[-1]
    tile = out.shape[2]
    width = out.shape[3]
    for side, xs in ((0, x_own), (1, x_oth)):
        total = None
        for x, w in zip(xs, ws):
            part = nt_dot(x[...].reshape(3 * tile, x.shape[2]), w[...])
            total = part if total is None else total + part
        total = total.reshape(3, tile, width)
        if has_acc:
            total = total + acc_in[side]
        out[side] = total


def group_matmul(kidx, x_own, x_oth, ws, acc, tile=128):
    count = len(ws)
    members = x_own.shape[1]
    block = ws[0].shape[1]
    width = ws[0].shape[0]

    def x_spec(s):
        return pl.BlockSpec((3, tile, block), lambda i, k, s=s: (0, i, k[s]))

    specs = [x_spec(s) for s in range(count)] * 2
    specs += [pl.BlockSpec((width, block), lambda i, k: (0, 0))] * count
    acc_spec = pl.BlockSpec((2, 3, tile, width), lambda i, k: (0, 0, i, 0))
    args = [x_own] * count + [x_oth] * count + list(ws)
    alias = {}
    if acc is not None:
        specs.append(acc_spec)
        args.append(acc)
        alias = {len(args): 0}
    flops = 2 * 2 * 3 * members * width * block * count
    return pl.pallas_call(
        functools.partial(group_kernel, count, acc is not None),
        out_shape=jax.ShapeDtypeStruct((2, 3, members, width), jnp.float32),
        grid_spec=pltpu.PrefetchScalarGridSpec(
            num_scalar_prefetch=1,
            grid=(members // tile,),
            in_specs=specs,
            out_specs=acc_spec,
        ),
        input_output_aliases=alias,
        compiler_params=pltpu.CompilerParams(vmem_limit_bytes=VMEM_BYTES),
        cost_estimate=pl.CostEstimate(flops=flops, bytes_accessed=16 * 1024 * 1024, transcendentals=0),
    )(kidx, *args)


def last_kernel(kidx, x_own, x_oth, w, acc, low, fout, readout, out):
    tile = acc.shape[2]
    width = acc.shape[3]
    chunk = 256
    ones = jnp.ones((8, 128), jnp.float32)
    for side, x in ((0, x_own), (1, x_oth)):
        total = jnp.zeros((tile, 128), jnp.float32)
        flat = x[...].reshape(3 * tile, x.shape[2])
        for j in range(0, width, chunk):
            cols = pl.ds(j, chunk)
            part = nt_dot(flat, w[cols, :]).reshape(3, tile, chunk)
            shift = fout[side, :, cols].astype(jnp.float32)
            read = readout[:, cols]
            summed = None
            for r in range(3):
                pert = part[r] + acc[side, r, :, cols] + low[side, r] * shift
                term = jnp.tanh(pert)
                summed = term if summed is None else summed + term
            summed = summed * read
            for h in range(0, chunk, 128):
                total = total + summed[:, h : h + 128]
        out[side] = lax.dot_general(
            ones,
            total,
            (((1,), (1,)), ((), ())),
            preferred_element_type=jnp.float32,
            precision=lax.Precision.HIGHEST,
        )


def last_matmul(kidx, x_own, x_oth, w, acc, low, fout, readout, tile=128):
    members = x_own.shape[1]
    width, block = w.shape
    x_spec = pl.BlockSpec((3, tile, block), lambda i, k: (0, i, k[0]))
    return pl.pallas_call(
        last_kernel,
        out_shape=jax.ShapeDtypeStruct((2, 8, members), jnp.float32),
        grid_spec=pltpu.PrefetchScalarGridSpec(
            num_scalar_prefetch=1,
            grid=(members // tile,),
            in_specs=[
                x_spec,
                x_spec,
                pl.BlockSpec((width, block), lambda i, k: (0, 0)),
                pl.BlockSpec((2, 3, tile, width), lambda i, k: (0, 0, i, 0)),
                pl.BlockSpec((2, 3, tile, 1), lambda i, k: (0, 0, i, 0)),
                pl.BlockSpec((2, tile, width), lambda i, k: (0, i, 0)),
                pl.BlockSpec((1, width), lambda i, k: (0, 0)),
            ],
            out_specs=pl.BlockSpec((2, 8, tile), lambda i, k: (0, 0, i)),
        ),
        compiler_params=pltpu.CompilerParams(vmem_limit_bytes=VMEM_BYTES),
        cost_estimate=pl.CostEstimate(
            flops=2 * 6 * members * width * block,
            bytes_accessed=12 * 1024 * 1024,
            transcendentals=6 * members * width,
        ),
    )(kidx, x_own, x_oth, w, acc, low, fout, readout)


def step_kernel(place, fit, fout_t, fin, part, util):
    values = fit[...]
    count = values.shape[0] * values.shape[1]
    mean = jnp.sum(values) / count
    spread = jnp.sum((values - mean) ** 2) / count
    root = jnp.sqrt(jnp.full((1, 1), spread + epsilon, jnp.float32))
    xh, z, c = place[0], place[1], place[2]
    util[...] = (fit[pl.ds(xh * 16 + z * 2 + c, 1), :] - mean) / root
    total = None
    members = fin.shape[1]
    for k in range(Z):
        row = (fit[pl.ds(xh * 16 + k * 2 + c, 1), :] - mean) / root
        scaled = (fout_t[:, k * members : (k + 1) * members].astype(jnp.float32) * row).astype(jnp.bfloat16)
        one = jnp.dot(scaled, fin[k], preferred_element_type=jnp.float32)
        total = one if total is None else total + one
    part[...] = total * (1.0 / np.sqrt(float(count)))


def weight_part(place, fit, fout_t, fin):
    rows = fout_t.shape[0]
    members, cols = fin.shape[1], fin.shape[2]
    vmem = pl.BlockSpec(memory_space=pltpu.VMEM)
    return pl.pallas_call(
        step_kernel,
        out_shape=(
            jax.ShapeDtypeStruct((rows, cols), jnp.float32),
            jax.ShapeDtypeStruct((1, members), jnp.float32),
        ),
        in_specs=[pl.BlockSpec(memory_space=pltpu.SMEM), vmem, vmem, vmem],
        out_specs=(vmem, vmem),
        compiler_params=pltpu.CompilerParams(vmem_limit_bytes=VMEM_BYTES),
        cost_estimate=pl.CostEstimate(
            flops=2 * rows * Z * members * cols, bytes_accessed=4 * 1024 * 1024, transcendentals=0
        ),
    )(place, fit, fout_t, fin)


def share(x, axes, count):
    return lax.all_to_all(jnp.broadcast_to(x[None], (count,) + x.shape), axes, 0, 0, tiled=True)


def shards(inputs, weight, factor_in, factor_out, readout):
    members, rows_here, width = inputs.shape
    out_width, block = weight.shape
    half = out_width // 2
    xh, z, c, xl, y = (lax.axis_index(a) for a in AXES)
    wa = xl * Y + y
    sign = 1 - 2 * c
    y_fwd, y_bwd, x_go, core_go = go_y(1), go_y(-1), go_x(), go_core()

    def send(v, pairs):
        return lax.ppermute(v, AXES, pairs)

    def col(xl_at, off):
        return xl_at * Y + lax.rem(y + off + Y, Y)

    xo = 1 - xl
    k_own, k_a, k_b, k_c = col(xl, 0), col(xl, -sign), col(xl, sign), col(xl, 2)
    k_d, k_e, k_f, k_g = col(xo, 0), col(xo, -sign), col(xo, sign), col(xo, 2)

    x_own = inputs.transpose(1, 0, 2)
    w_own = lax.dynamic_slice_in_dim(weight, c * half, half, 0)

    w_a = send(w_own, y_fwd)
    w_d = send(w_own, x_go)
    x_oth = send(x_own, core_go)

    fin_here = lax.dynamic_slice_in_dim(factor_in, wa * block, block, 1)
    fin_all = lax.all_gather(fin_here, "z", axis=0)
    m_slice = members // WA
    fout_here = lax.dynamic_slice_in_dim(factor_out, wa * m_slice, m_slice, 0)
    pieces = fout_here.reshape(m_slice, XH, Z, CORE, out_width // (XH * Z * CORE))
    pieces = pieces.transpose(2, 0, 1, 3, 4).reshape(Z, m_slice, out_width // Z)
    pieces = lax.all_to_all(pieces, "z", 0, 0, tiled=True)
    fout_all = lax.all_gather(pieces, ("xl", "y"), axis=0)
    fout_t = fout_all.transpose(3, 1, 0, 2).reshape(out_width // Z, Z * members)

    low_own = perturb_scale * jnp.sum(
        x_own.astype(jnp.float32) * factor_in.astype(jnp.float32)[None], axis=-1
    )
    read_mine = lax.dynamic_slice_in_dim(readout, c * half, half, 0)[None]
    fout_mine = lax.dynamic_slice_in_dim(factor_out, c * half, half, 1)
    fout_theirs = lax.dynamic_slice_in_dim(factor_out, (1 - c) * half, half, 1)
    low_oth = send(low_own, core_go)
    fout_oth = send(fout_theirs, core_go)
    low = jnp.stack([low_own, low_oth])[..., None]
    fout = jnp.stack([fout_mine, fout_oth])

    def idx(*ks):
        return jnp.stack(ks).astype(jnp.int32)

    w_b = send(w_own, y_bwd)
    w_e = send(w_a, x_go)
    acc = group_matmul(idx(k_own, k_a, k_d), x_own, x_oth, [w_own, w_a, w_d], None)
    w_f = send(w_b, x_go)
    w_c = send(w_a, y_fwd)
    acc = group_matmul(idx(k_b, k_e), x_own, x_oth, [w_b, w_e], acc)
    quarter = half // 2
    w_g0 = send(w_c[:quarter], x_go)
    w_g1 = send(w_e[quarter:], y_fwd)
    acc = group_matmul(idx(k_f, k_c), x_own, x_oth, [w_f, w_c], acc)
    w_g = jnp.concatenate([w_g0, w_g1], axis=0)
    partial = last_matmul(idx(k_g), x_own, x_oth, w_g, acc, low, fout, read_mine)[:, 0, :]

    by_core = jnp.where(c == 0, partial, partial[::-1])
    spread_out = share(by_core.reshape(2 * members), ("core", "xl", "y"), CORE * WA)
    fit_chip = jnp.sum(spread_out.reshape(CORE * WA, 2 * members), axis=0) / ROWS_ALL
    fit = share(fit_chip, ("xh", "z"), XH * Z).reshape(XH * Z * CORE, members)

    part, util = weight_part(idx(xh, z, c), fit, fout_t, fin_all)
    out_rows = part.shape[0] // (XH * CORE)
    swapped = lax.all_to_all(part.reshape(XH * CORE, out_rows, block), ("xh", "core"), 0, 0, tiled=True)
    return jnp.sum(swapped, axis=0), util.reshape(members)


def solution(mesh):
    fine = Mesh(mesh.devices.reshape(SIZES), AXES)
    pop, wa = ("xh", "z", "core"), ("xl", "y")
    placed = (P(pop, wa, None), P(None, wa), P(pop, None), P(pop, None), P())
    return jax.shard_map(
        shards, mesh=fine, in_specs=placed, out_specs=(P(pop, wa), P(pop)), check_vma=False
    )
```

```python
import functools

import jax
import jax.numpy as jnp
import numpy as np
from jax import lax
from jax.experimental import pallas as pl
from jax.experimental.pallas import tpu as pltpu
from jax.sharding import Mesh, PartitionSpec as P

perturb_scale = 0.5
epsilon = 1e-05

XH, Z, CORE, XL, Y = 2, 8, 2, 2, 4
AXES = ("xh", "z", "core", "xl", "y")
SIZES = (XH, Z, CORE, XL, Y)
WA = XL * Y
ROWS_ALL = 24
VMEM_BYTES = 24 * 1024 * 1024


def permutation(move):
    pairs = []
    for i in range(int(np.prod(SIZES))):
        at = [int(v) for v in np.unravel_index(i, SIZES)]
        to = move(*at)
        pairs.append((i, int(np.ravel_multi_index(to, SIZES))))
    return pairs


def go_y(step):
    def move(xh, z, c, xl, y):
        s = step if c == 0 else -step
        return (xh, z, c, xl, (y + s) % Y)

    return permutation(move)


def go_x():
    def move(xh, z, c, xl, y):
        x = xh * 2 + xl
        if c == 0:
            x = x ^ 1
        else:
            x = (x + 1) % 4 if x % 2 else (x - 1) % 4
        return (x // 2, z, c, x % 2, y)

    return permutation(move)


def go_core():
    return permutation(lambda xh, z, c, xl, y: (xh, z, 1 - c, xl, y))


def go_xh():
    return permutation(lambda xh, z, c, xl, y: (1 - xh, z, c, xl, y))


def nt_dot(a, b):
    return lax.dot_general(a, b, (((1,), (1,)), ((), ())), preferred_element_type=jnp.float32)


def fetch_columns(kidx, count, block, sources, buffers, sems):
    copies = []
    for s in range(count):
        cols = pl.ds(pl.multiple_of(kidx[s] * block, block), block)
        for side in range(2):
            copy = pltpu.make_async_copy(
                sources[side].at[:, :, cols], buffers.at[s, side], sems.at[s, side]
            )
            copy.start()
            copies.append(copy)
    return copies


def group_kernel(count, has_acc, kidx, x_own, x_oth, *refs):
    ws = refs[:count]
    acc_in = refs[count] if has_acc else None
    out, token, buffers, sems = refs[-4:]
    members, width = out.shape[2], out.shape[3]
    block = ws[0].shape[1]
    copies = fetch_columns(kidx, count, block, (x_own, x_oth), buffers, sems)
    token[...] = jnp.zeros_like(token)
    chunk = 512
    for side in range(2):
        for s in range(count):
            copies[2 * s + side].wait()
        for j in range(0, width, chunk):
            cols = pl.ds(j, chunk)
            total = None
            for s, w in enumerate(ws):
                part = nt_dot(buffers[s, side].reshape(3 * members, block), w[cols, :])
                total = part if total is None else total + part
            total = total.reshape(3, members, chunk)
            if has_acc:
                total = total + acc_in[side, :, :, cols]
            out[side, :, :, cols] = total


def group_matmul(kidx, x_own, x_oth, ws, acc):
    count = len(ws)
    members = x_own.shape[1]
    width, block = ws[0].shape
    smem = pl.BlockSpec(memory_space=pltpu.SMEM)
    vmem = pl.BlockSpec(memory_space=pltpu.VMEM)
    hbm = pl.BlockSpec(memory_space=pl.ANY)
    args = [x_own, x_oth] + list(ws)
    specs = [smem, hbm, hbm] + [vmem] * count
    alias = {}
    if acc is not None:
        specs.append(vmem)
        args.append(acc)
        alias = {len(args): 0}
    flops = 2 * 2 * 3 * members * width * block * count
    return pl.pallas_call(
        functools.partial(group_kernel, count, acc is not None),
        out_shape=(
            jax.ShapeDtypeStruct((2, 3, members, width), jnp.float32),
            jax.ShapeDtypeStruct((8, 128), jnp.float32),
        ),
        in_specs=specs,
        out_specs=(vmem, vmem),
        scratch_shapes=[
            pltpu.VMEM((count, 2, 3, members, block), jnp.bfloat16),
            pltpu.SemaphoreType.DMA((count, 2)),
        ],
        input_output_aliases=alias,
        compiler_params=pltpu.CompilerParams(vmem_limit_bytes=VMEM_BYTES),
        cost_estimate=pl.CostEstimate(flops=flops, bytes_accessed=16 * 1024 * 1024, transcendentals=0),
    )(kidx, *args)


def last_kernel(kidx, x_own, x_oth, w, acc, low_own, low_oth, fout_own, fout_oth, readout, out, buffers, sems):
    members, width = acc.shape[2], acc.shape[3]
    block = w.shape[1]
    copies = fetch_columns(kidx, 1, block, (x_own, x_oth), buffers, sems)
    chunk = 256
    ones = jnp.ones((8, 128), jnp.float32)
    for side, low, fout in ((0, low_own, fout_own), (1, low_oth, fout_oth)):
        copies[side].wait()
        total = jnp.zeros((members, 128), jnp.float32)
        for j in range(0, width, chunk):
            cols = pl.ds(j, chunk)
            part = nt_dot(buffers[0, side].reshape(3 * members, block), w[cols, :])
            part = part.reshape(3, members, chunk)
            shift = fout[:, cols].astype(jnp.float32)
            summed = None
            for r in range(3):
                pert = part[r] + acc[side, r, :, cols] + low[r] * shift
                term = jnp.tanh(pert)
                summed = term if summed is None else summed + term
            summed = summed * readout[:, cols]
            for h in range(0, chunk, 128):
                total = total + summed[:, h : h + 128]
        row = lax.dot_general(
            ones,
            total,
            (((1,), (1,)), ((), ())),
            preferred_element_type=jnp.float32,
            precision=lax.Precision.HIGHEST,
        )
        out[jnp.bitwise_xor(kidx[1], side)] = row


def last_matmul(kidx, x_own, x_oth, w, acc, low_own, low_oth, fout_own, fout_oth, readout):
    members = x_own.shape[1]
    width, block = w.shape
    smem = pl.BlockSpec(memory_space=pltpu.SMEM)
    vmem = pl.BlockSpec(memory_space=pltpu.VMEM)
    hbm = pl.BlockSpec(memory_space=pl.ANY)
    return pl.pallas_call(
        last_kernel,
        out_shape=jax.ShapeDtypeStruct((2, 8, members), jnp.float32),
        in_specs=[smem, hbm, hbm] + [vmem] * 7,
        out_specs=vmem,
        scratch_shapes=[
            pltpu.VMEM((1, 2, 3, members, block), jnp.bfloat16),
            pltpu.SemaphoreType.DMA((1, 2)),
        ],
        compiler_params=pltpu.CompilerParams(vmem_limit_bytes=VMEM_BYTES),
        cost_estimate=pl.CostEstimate(
            flops=2 * 6 * members * width * block,
            bytes_accessed=12 * 1024 * 1024,
            transcendentals=6 * members * width,
        ),
    )(kidx, x_own, x_oth, w, acc, low_own, low_oth, fout_own, fout_oth, readout)


def low_kernel(x, fin, out):
    width = fin.shape[1]
    chunk = 128
    totals = [None] * 3
    for j in range(0, width, chunk):
        cols = pl.ds(j, chunk)
        f = fin[:, cols].astype(jnp.float32)
        for r in range(3):
            term = x[r, :, cols].astype(jnp.float32) * f
            totals[r] = term if totals[r] is None else totals[r] + term
    for r in range(3):
        out[r] = perturb_scale * jnp.sum(totals[r], axis=1, keepdims=True)


def low_term(x, fin):
    rows, members, width = x.shape
    tile = 64
    return pl.pallas_call(
        low_kernel,
        out_shape=jax.ShapeDtypeStruct((rows, members, 1), jnp.float32),
        grid=(members // tile,),
        in_specs=[
            pl.BlockSpec((rows, tile, width), lambda i: (0, i, 0)),
            pl.BlockSpec((tile, width), lambda i: (i, 0)),
        ],
        out_specs=pl.BlockSpec((rows, tile, 1), lambda i: (0, i, 0)),
        compiler_params=pltpu.CompilerParams(vmem_limit_bytes=VMEM_BYTES),
        cost_estimate=pl.CostEstimate(
            flops=2 * rows * members * width, bytes_accessed=9 * 1024 * 1024, transcendentals=0
        ),
    )(x, fin)


def step_kernel(place, fit, fout_t, fin, keep, give, util):
    values = fit[...]
    count = values.shape[0] * values.shape[1]
    mean = jnp.sum(values) / count
    spread = jnp.sum((values - mean) ** 2) / count
    root = jnp.sqrt(jnp.full((1, 1), spread + epsilon, jnp.float32))
    xh, z, c = place[0], place[1], place[2]
    util[...] = (fit[pl.ds(xh * 16 + z * 2 + c, 1), :] - mean) / root
    total = None
    members = fin.shape[1]
    for k in range(Z):
        row = (fit[pl.ds(xh * 16 + k * 2 + c, 1), :] - mean) / root
        scaled = (fout_t[:, k * members : (k + 1) * members].astype(jnp.float32) * row).astype(jnp.bfloat16)
        one = jnp.dot(scaled, fin[k], preferred_element_type=jnp.float32)
        total = one if total is None else total + one
    total = total * (1.0 / np.sqrt(float(count)))
    rows = keep.shape[1]
    total = total.reshape(XH, CORE, rows, total.shape[1])
    for h in range(XH):
        at = jnp.bitwise_xor(xh, h)
        keep[at] = jnp.where(c == 0, total[h, 0], total[h, 1])
        give[at] = jnp.where(c == 0, total[h, 1], total[h, 0])


def weight_part(place, fit, fout_t, fin):
    rows = fout_t.shape[0]
    members, cols = fin.shape[1], fin.shape[2]
    vmem = pl.BlockSpec(memory_space=pltpu.VMEM)
    return pl.pallas_call(
        step_kernel,
        out_shape=(
            jax.ShapeDtypeStruct((XH, rows // (XH * CORE), cols), jnp.float32),
            jax.ShapeDtypeStruct((XH, rows // (XH * CORE), cols), jnp.float32),
            jax.ShapeDtypeStruct((1, members), jnp.float32),
        ),
        in_specs=[pl.BlockSpec(memory_space=pltpu.SMEM), vmem, vmem, vmem],
        out_specs=(vmem, vmem, vmem),
        compiler_params=pltpu.CompilerParams(vmem_limit_bytes=VMEM_BYTES),
        cost_estimate=pl.CostEstimate(
            flops=2 * rows * Z * members * cols, bytes_accessed=4 * 1024 * 1024, transcendentals=0
        ),
    )(place, fit, fout_t, fin)


def share(x, axes, count):
    return lax.all_to_all(jnp.broadcast_to(x[None], (count,) + x.shape), axes, 0, 0, tiled=True)


def shards(inputs, weight, factor_in, factor_out, readout):
    members, rows_here, width = inputs.shape
    out_width, block = weight.shape
    half = out_width // 2
    xh, z, c, xl, y = (lax.axis_index(a) for a in AXES)
    wa = xl * Y + y
    sign = 1 - 2 * c
    y_fwd, y_bwd, x_go, core_go = go_y(1), go_y(-1), go_x(), go_core()

    def send(v, pairs):
        return lax.ppermute(v, AXES, pairs)

    def col(xl_at, off):
        return xl_at * Y + lax.rem(y + off + Y, Y)

    xo = 1 - xl
    k_own, k_a, k_b, k_c = col(xl, 0), col(xl, -sign), col(xl, sign), col(xl, 2)
    k_d, k_e, k_f, k_g = col(xo, 0), col(xo, -sign), col(xo, sign), col(xo, 2)

    x_own = inputs.transpose(1, 0, 2)
    w_own = lax.dynamic_slice_in_dim(weight, c * half, half, 0)

    def idx(*ks):
        return jnp.stack(ks).astype(jnp.int32)

    def after(values, *done):
        return lax.optimization_barrier((tuple(values), done))[0]

    w_a = send(w_own, y_fwd)
    w_d = send(w_own, x_go)
    x_oth = send(x_own, core_go)

    fin_here = lax.dynamic_slice_in_dim(factor_in, wa * block, block, 1)
    fin_all = lax.all_gather(fin_here, "z", axis=0)
    rows_out = out_width // (XH * Z * CORE)
    pieces = factor_out.reshape(members, XH, Z, CORE, rows_out)
    pieces = pieces.transpose(2, 0, 1, 3, 4).reshape(Z, members, out_width // Z)
    pieces = lax.all_to_all(pieces, "z", 0, 0, tiled=True)

    w_a, w_d, w_own2 = after((w_a, w_d, w_own))
    w_b = send(w_own2, y_bwd)
    w_e = send(w_a, x_go)
    acc, token = group_matmul(idx(k_own, k_a, k_d), x_own, x_oth, [w_own, w_a, w_d], None)

    x_low, fin_low, fout_low = after((x_own, factor_in, factor_out), w_a, w_d)
    low_own = low_term(x_low, fin_low)
    read_mine = lax.dynamic_slice_in_dim(readout, c * half, half, 0)[None]
    fout_mine = lax.dynamic_slice_in_dim(fout_low, c * half, half, 1)
    fout_theirs = lax.dynamic_slice_in_dim(fout_low, (1 - c) * half, half, 1)
    fout_oth = send(fout_theirs, core_go)

    w_a3, w_b3 = after((w_a, w_b), w_e, token)
    w_f = send(w_b3, x_go)
    w_c = send(w_a3, y_fwd)
    low_oth = send(low_own, core_go)
    acc, token = group_matmul(idx(k_b, k_e), x_own, x_oth, [w_b, w_e], acc)

    quarter = half // 2
    w_c4, w_e4 = after((w_c, w_e), w_f, token)
    w_g0 = send(w_c4[:quarter], x_go)
    w_g1 = send(w_e4[quarter:], y_fwd)
    acc, token = group_matmul(idx(k_f, k_c), x_own, x_oth, [w_f, w_c], acc)
    w_g = jnp.concatenate([w_g0, w_g1], axis=0)
    partial = last_matmul(
        idx(k_g, c), x_own, x_oth, w_g, acc, low_own, low_oth, fout_mine, fout_oth, read_mine
    )[:, 0, :]

    spread_out = share(partial.reshape(2 * members), ("core", "xl", "y"), CORE * WA)
    fit_chip = jnp.sum(spread_out.reshape(CORE * WA, 2 * members), axis=0) / ROWS_ALL
    fit = share(fit_chip, ("xh", "z"), XH * Z).reshape(XH * Z * CORE, members)

    pieces = after((pieces,), partial)[0]
    fout_t = pieces.transpose(2, 0, 1).reshape(out_width // Z, Z * members)
    keep, give, util = weight_part(idx(xh, z, c), fit, fout_t, fin_all)
    summed = keep + send(give, core_go)
    weight_step = summed[0] + send(summed[1], go_xh())
    return weight_step, util.reshape(members)


def solution(mesh):
    fine = Mesh(mesh.devices.reshape(SIZES), AXES)
    pop, wa = ("xh", "z", "core"), ("xl", "y")
    placed = (P(pop, wa, None), P(None, wa), P(pop, None), P(pop, None), P())
    return jax.shard_map(
        shards, mesh=fine, in_specs=placed, out_specs=(P(pop, wa), P(pop)), check_vma=False
    )
```

```python
import functools

import jax
import jax.numpy as jnp
import numpy as np
from jax import lax
from jax.experimental import pallas as pl
from jax.experimental.pallas import tpu as pltpu
from jax.sharding import Mesh, PartitionSpec as P

perturb_scale = 0.5
epsilon = 1e-05

XH, Z, CORE, XL, Y = 2, 8, 2, 2, 4
AXES = ("xh", "z", "core", "xl", "y")
SIZES = (XH, Z, CORE, XL, Y)
WA = XL * Y
CHAINS = 2
ROWS_ALL = 24
VMEM_BYTES = 55 * 1024 * 1024
SMALL_BYTES = 1024 * 1024


def permutation(move):
    pairs = []
    for i in range(int(np.prod(SIZES))):
        at = [int(v) for v in np.unravel_index(i, SIZES)]
        to = move(*at)
        pairs.append((i, int(np.ravel_multi_index(to, SIZES))))
    return pairs


def go_y(step):
    def move(xh, z, c, xl, y):
        s = step if c == 0 else -step
        return (xh, z, c, xl, (y + s) % Y)

    return permutation(move)


def go_x():
    def move(xh, z, c, xl, y):
        x = xh * 2 + xl
        if c == 0:
            x = x ^ 1
        else:
            x = (x + 1) % 4 if x % 2 else (x - 1) % 4
        return (x // 2, z, c, x % 2, y)

    return permutation(move)


def go_core():
    return permutation(lambda xh, z, c, xl, y: (xh, z, 1 - c, xl, y))


def go_xh():
    return permutation(lambda xh, z, c, xl, y: (1 - xh, z, c, xl, y))


def nt_dot(a, b):
    return lax.dot_general(a, b, (((1,), (1,)), ((), ())), preferred_element_type=jnp.float32)


def fetch_columns(kidx, count, block, sources, buffers, sems):
    copies = []
    for s in range(count):
        cols = pl.ds(pl.multiple_of(kidx[s] * block, block), block)
        for side in range(2):
            copy = pltpu.make_async_copy(
                sources[side].at[:, :, cols], buffers.at[s, side], sems.at[s, side]
            )
            copy.start()
            copies.append(copy)
    return copies


def fetch_weights(sent, ws, sems):
    copies = []
    for s, w in enumerate(sent):
        copy = pltpu.make_async_copy(w, ws.at[s], sems.at[s])
        copy.start()
        copies.append(copy)
    return copies


def group_kernel(count, has_acc, extra, kidx, x_own, x_oth, *refs):
    refs = refs[extra:]
    sent = refs[:count]
    acc_in = refs[count] if has_acc else None
    out, token, ws, w_sems, buffers, sems = refs[-6:]
    members, width = out.shape[2], out.shape[3]
    block = sent[0].shape[1]
    copies = fetch_columns(kidx, count, block, (x_own, x_oth), buffers, sems)
    fetched = fetch_weights(sent, ws, w_sems)
    token[...] = jnp.zeros_like(token)
    chunk = 512
    for side in range(2):
        for s in range(count):
            copies[2 * s + side].wait()
            if side == 0:
                fetched[s].wait()
        for j in range(0, width, chunk):
            cols = pl.ds(j, chunk)
            total = None
            for s in range(count):
                part = nt_dot(buffers[s, side].reshape(3 * members, block), ws[s, cols, :])
                total = part if total is None else total + part
            total = total.reshape(3, members, chunk)
            if has_acc:
                total = total + acc_in[side, :, :, cols]
            out[side, :, :, cols] = total


def group_matmul(kidx, x_own, x_oth, ws, acc, extra=()):
    count = len(ws)
    members = x_own.shape[1]
    width, block = ws[0].shape
    smem = pl.BlockSpec(memory_space=pltpu.SMEM)
    vmem = pl.BlockSpec(memory_space=pltpu.VMEM)
    hbm = pl.BlockSpec(memory_space=pltpu.HBM)
    args = [x_own, x_oth, *extra] + list(ws)
    specs = [smem, hbm, hbm] + [hbm] * len(extra) + [hbm] * count
    alias = {}
    if acc is not None:
        specs.append(vmem)
        args.append(acc)
        alias = {len(args): 0}
    flops = 2 * 2 * 3 * members * width * block * count
    return pl.pallas_call(
        functools.partial(group_kernel, count, acc is not None, len(extra)),
        out_shape=(
            jax.ShapeDtypeStruct((2, 3, members, width), jnp.float32),
            jax.ShapeDtypeStruct((8, 128), jnp.float32),
        ),
        in_specs=specs,
        out_specs=(vmem, vmem),
        scratch_shapes=[
            pltpu.VMEM((count, width, block), jnp.bfloat16),
            pltpu.SemaphoreType.DMA((count,)),
            pltpu.VMEM((count, 2, 3, members, block), jnp.bfloat16),
            pltpu.SemaphoreType.DMA((count, 2)),
        ],
        input_output_aliases=alias,
        compiler_params=pltpu.CompilerParams(vmem_limit_bytes=VMEM_BYTES),
        cost_estimate=pl.CostEstimate(flops=flops, bytes_accessed=16 * 1024 * 1024, transcendentals=0),
    )(kidx, *args)


def last_kernel(first, kidx, x_own, x_oth, sent, pieces, acc, low_own, low_oth, fout_own, fout_oth, readout, *refs):
    before = refs[0] if len(refs) == 6 else None
    out, w, w_sems, buffers, sems = refs[-5:]
    members, width = acc.shape[2], acc.shape[3]
    block = sent.shape[1]
    fetched = fetch_weights([sent], w, w_sems)
    copies = fetch_columns(kidx, 1, block, (x_own, x_oth), buffers, sems)
    fetched[0].wait()
    chunk = 256
    ones = jnp.ones((8, 128), jnp.float32)
    for side, low, fout in ((0, low_own, fout_own), (1, low_oth, fout_oth)):
        copies[side].wait()
        total = jnp.zeros((members, 128), jnp.float32)
        for j in range(0, width, chunk):
            cols = pl.ds(j, chunk)
            part = nt_dot(buffers[0, side].reshape(3 * members, block), w[0, cols, :])
            part = part.reshape(3, members, chunk)
            shift = fout[:, pl.ds(first + j, chunk)].astype(jnp.float32)
            summed = None
            for r in range(3):
                pert = part[r] + acc[side, r, :, cols] + low[r] * shift
                term = jnp.tanh(pert)
                summed = term if summed is None else summed + term
            summed = summed * readout[:, pl.ds(first + j, chunk)]
            for h in range(0, chunk, 128):
                total = total + summed[:, h : h + 128]
        row = lax.dot_general(
            ones,
            total,
            (((1,), (1,)), ((), ())),
            preferred_element_type=jnp.float32,
            precision=lax.Precision.HIGHEST,
        )[0:1]
        at = pl.ds(pl.multiple_of(jnp.bitwise_xor(kidx[1], side) * members, members), members)
        if before is not None:
            row = row + before[0, :, at]
        for k in range(out.shape[0]):
            out[k, :, at] = row


def last_matmul(first, kidx, x_own, x_oth, w, pieces, acc, low_own, low_oth, fout_own, fout_oth, readout, before):
    members = x_own.shape[1]
    width, block = w.shape
    smem = pl.BlockSpec(memory_space=pltpu.SMEM)
    vmem = pl.BlockSpec(memory_space=pltpu.VMEM)
    hbm = pl.BlockSpec(memory_space=pltpu.HBM)
    args = [acc, low_own, low_oth, fout_own, fout_oth, readout]
    if before is not None:
        args.append(before)
    return pl.pallas_call(
        functools.partial(last_kernel, first),
        out_shape=jax.ShapeDtypeStruct((CORE * WA, 1, 2 * members), jnp.float32),
        in_specs=[smem, hbm, hbm, hbm, hbm] + [vmem] * len(args),
        out_specs=vmem,
        scratch_shapes=[
            pltpu.VMEM((1, width, block), jnp.bfloat16),
            pltpu.SemaphoreType.DMA((1,)),
            pltpu.VMEM((1, 2, 3, members, block), jnp.bfloat16),
            pltpu.SemaphoreType.DMA((1, 2)),
        ],
        compiler_params=pltpu.CompilerParams(vmem_limit_bytes=VMEM_BYTES),
        cost_estimate=pl.CostEstimate(
            flops=2 * 6 * members * width * block,
            bytes_accessed=6 * 1024 * 1024,
            transcendentals=6 * members * width,
        ),
    )(kidx, x_own, x_oth, w, pieces, *args)


def after_kernel(*refs):
    pass


def after(values, *done):
    hbm = pl.BlockSpec(memory_space=pltpu.HBM)
    count = len(values)
    return pl.pallas_call(
        after_kernel,
        out_shape=tuple(jax.ShapeDtypeStruct(v.shape, v.dtype) for v in values),
        in_specs=[hbm] * (count + len(done)),
        out_specs=(hbm,) * count,
        input_output_aliases={i: i for i in range(count)},
        compiler_params=pltpu.CompilerParams(vmem_limit_bytes=SMALL_BYTES),
    )(*values, *done)


def sum_kernel(got, out):
    out[...] = jnp.broadcast_to(jnp.sum(got[...], axis=0, keepdims=True) / ROWS_ALL, out.shape)


def sum_and_copy(got):
    vmem = pl.BlockSpec(memory_space=pltpu.VMEM)
    return pl.pallas_call(
        sum_kernel,
        out_shape=jax.ShapeDtypeStruct((XH * Z,) + got.shape[1:], jnp.float32),
        in_specs=[vmem],
        out_specs=vmem,
        compiler_params=pltpu.CompilerParams(vmem_limit_bytes=SMALL_BYTES),
    )(got)


def low_kernel(x, fin, out, x_buf, f_buf, sems):
    tiles, rows, tile, width = x_buf.shape
    copies = []
    for t in range(tiles):
        span = pl.ds(t * tile, tile)
        pair = (
            pltpu.make_async_copy(x.at[:, span, :], x_buf.at[t], sems.at[t, 0]),
            pltpu.make_async_copy(fin.at[span, :], f_buf.at[t], sems.at[t, 1]),
        )
        for copy in pair:
            copy.start()
        copies.append(pair)
    chunk = 128
    for t in range(tiles):
        for copy in copies[t]:
            copy.wait()
        totals = [None] * rows
        for j in range(0, width, chunk):
            cols = pl.ds(j, chunk)
            f = f_buf[t, :, cols].astype(jnp.float32)
            for r in range(rows):
                term = x_buf[t, r, :, cols].astype(jnp.float32) * f
                totals[r] = term if totals[r] is None else totals[r] + term
        for r in range(rows):
            out[r, pl.ds(t * tile, tile), :] = perturb_scale * jnp.sum(totals[r], axis=1, keepdims=True)


def low_term(x, fin):
    rows, members, width = x.shape
    tile = 64
    tiles = members // tile
    hbm = pl.BlockSpec(memory_space=pltpu.HBM)
    return pl.pallas_call(
        low_kernel,
        out_shape=jax.ShapeDtypeStruct((rows, members, 1), jnp.float32),
        in_specs=[hbm, hbm],
        out_specs=pl.BlockSpec(memory_space=pltpu.VMEM),
        scratch_shapes=[
            pltpu.VMEM((tiles, rows, tile, width), jnp.bfloat16),
            pltpu.VMEM((tiles, tile, width), jnp.bfloat16),
            pltpu.SemaphoreType.DMA((tiles, 2)),
        ],
        compiler_params=pltpu.CompilerParams(vmem_limit_bytes=VMEM_BYTES),
        cost_estimate=pl.CostEstimate(
            flops=2 * rows * members * width, bytes_accessed=9 * 1024 * 1024, transcendentals=0
        ),
    )(x, fin)


def step_kernel(place, fit, fout, fin, keep, give, util, rows_ref):
    values = fit[...]
    members = fin.shape[1]
    count = values.shape[0] * values.shape[2]
    mean = jnp.sum(values) / count
    spread = jnp.sum((values - mean) ** 2) / count
    root = jnp.sqrt(jnp.full((1, 1), spread + epsilon, jnp.float32))
    xh, z, c = place[0], place[1], place[2]
    at = pl.ds(pl.multiple_of(c * members, members), members)
    util[...] = (fit[xh * Z + z, :, at] - mean) / root
    for k in range(Z):
        rows_ref[k : k + 1, :] = fit[xh * Z + k, :, at]
    columns = (jnp.transpose(rows_ref[...]) - mean) / root
    total = None
    for k in range(Z):
        scaled = (fout[k].astype(jnp.float32) * columns[:, k : k + 1]).astype(jnp.bfloat16)
        one = lax.dot_general(
            scaled, fin[k], (((0,), (0,)), ((), ())), preferred_element_type=jnp.float32
        )
        total = one if total is None else total + one
    total = total * (1.0 / np.sqrt(float(count)))
    rows = keep.shape[1]
    total = total.reshape(XH, CORE, rows, total.shape[1])
    for h in range(XH):
        to = jnp.bitwise_xor(xh, h)
        keep[to] = jnp.where(c == 0, total[h, 0], total[h, 1])
        give[to] = jnp.where(c == 0, total[h, 1], total[h, 0])


def weight_part(place, fit, fout, fin):
    members, rows = fout.shape[1], fout.shape[2]
    cols = fin.shape[2]
    vmem = pl.BlockSpec(memory_space=pltpu.VMEM)
    block = jax.ShapeDtypeStruct((XH, rows // (XH * CORE), cols), jnp.float32)
    return pl.pallas_call(
        step_kernel,
        out_shape=(block, block, jax.ShapeDtypeStruct((1, members), jnp.float32)),
        in_specs=[pl.BlockSpec(memory_space=pltpu.SMEM), vmem, vmem, vmem],
        out_specs=(vmem, vmem, vmem),
        scratch_shapes=[pltpu.VMEM((Z, members), jnp.float32)],
        compiler_params=pltpu.CompilerParams(vmem_limit_bytes=VMEM_BYTES),
        cost_estimate=pl.CostEstimate(
            flops=2 * rows * Z * members * cols, bytes_accessed=4 * 1024 * 1024, transcendentals=0
        ),
    )(place, fit, fout, fin)


def share(x, axes):
    return lax.all_to_all(x, axes, 0, 0, tiled=True)


def shards(inputs, weight, factor_in, factor_out, readout):
    members, rows_here, width = inputs.shape
    out_width, block = weight.shape
    half = out_width // 2
    xh, z, c, xl, y = (lax.axis_index(a) for a in AXES)
    wa = xl * Y + y
    sign = 1 - 2 * c
    y_fwd, y_bwd, x_go, core_go = go_y(1), go_y(-1), go_x(), go_core()

    def send(v, pairs):
        return lax.ppermute(v, AXES, pairs)

    def col(xl_at, off):
        return xl_at * Y + lax.rem(y + off + Y, Y)

    xo = 1 - xl
    k_own, k_a, k_b, k_c = col(xl, 0), col(xl, -sign), col(xl, sign), col(xl, 2)
    k_d, k_e, k_f, k_g = col(xo, 0), col(xo, -sign), col(xo, sign), col(xo, 2)

    x_own = inputs.transpose(1, 0, 2)
    def col(xl_at, off):
        return xl_at * Y + lax.rem(y + off + Y, Y)

    xo = 1 - xl
    k_own, k_a, k_b, k_c = col(xl, 0), col(xl, -sign), col(xl, sign), col(xl, 2)
    k_d, k_e, k_f, k_g = col(xo, 0), col(xo, -sign), col(xo, sign), col(xo, 2)

    x_own = inputs.transpose(1, 0, 2)
    w_own = lax.dynamic_slice_in_dim(weight, c * half, half, 0)

    def idx(*ks):
        return jnp.stack(ks).astype(jnp.int32)

    fin_here = lax.dynamic_slice_in_dim(factor_in, wa * block, block, 1)
    fin_all = lax.all_gather(fin_here, "z", axis=0)
    rows_out = out_width // (XH * Z * CORE)
    pieces = factor_out.reshape(members, XH, Z, CORE, rows_out)
    pieces = pieces.transpose(2, 0, 1, 3, 4).reshape(Z, members, out_width // Z)
    pieces = lax.all_to_all(pieces, "z", 0, 0, tiled=True)

    part = half // CHAINS
    chains = range(CHAINS)
    starts = [c * half + h * part for h in chains]
    own = [lax.dynamic_slice_in_dim(weight, at, part, 0) for at in starts]
    w_a = [send(w, y_fwd) for w in own]
    w_d = [send(w, x_go) for w in own]
    x_oth = send(x_own, core_go)

    low_own = low_term(x_own, factor_in)
    low_oth = send(low_own, core_go)
    fout_theirs = lax.dynamic_slice_in_dim(factor_out, (1 - c) * half, half, 1)
    fout_got = send(fout_theirs, core_go)
    fout_mine = lax.dynamic_slice_in_dim(factor_out, c * half, half, 1)
    read_mine = lax.dynamic_slice_in_dim(readout, c * half, half, 0)[None]

    w_b, w_e, w_c, w_f, acc, token = ([None] * CHAINS for _ in range(6))
    for h in chains:
        own[h], w_a[h], w_d[h] = after((own[h], w_a[h], w_d[h]))
        w_b[h] = send(own[h], y_bwd)
        w_e[h] = send(w_a[h], x_go)
        acc[h], token[h] = group_matmul(
            idx(k_own, k_a, k_d), x_own, x_oth, [own[h], w_a[h], w_d[h]], None, (low_own, fout_mine)
        )
    for h in chains:
        w_a[h], w_b[h], w_e[h] = after((w_a[h], w_b[h], w_e[h]), token[h])
        w_c[h] = send(w_a[h], y_fwd)
        w_f[h] = send(w_b[h], x_go)
        acc[h], token[h] = group_matmul(
            idx(k_b, k_e), x_own, x_oth, [w_b[h], w_e[h]], acc[h], (low_oth, fout_got)
        )
    w_g = [None] * CHAINS
    for h in chains:
        w_c[h], w_f[h], w_e[h] = after((w_c[h], w_f[h], w_e[h]), token[h])
        w_g[h] = send(w_c[h], x_go) if h == 0 else send(w_e[h], y_fwd)
        acc[h], token[h] = group_matmul(
            idx(k_f, k_c), x_own, x_oth, [w_f[h], w_c[h]], acc[h]
        )
    partial = None
    for h in chains:
        partial = last_matmul(
            h * part, idx(k_g, c), x_own, x_oth, w_g[h], pieces if h == 1 else w_g[h], acc[h],
            low_own, low_oth, fout_mine, fout_got, read_mine, partial,
        )

    fit = share(sum_and_copy(share(partial, ("core", "xl", "y"))), ("xh", "z"))

    keep, give, util = weight_part(idx(xh, z, c), fit, pieces, fin_all)
    summed = keep + send(give, core_go)
    weight_step = summed[0] + send(summed[1], go_xh())
    return weight_step, util.reshape(members)


def solution(mesh):
    fine = Mesh(mesh.devices.reshape(SIZES), AXES)
    pop, wa = ("xh", "z", "core"), ("xl", "y")
    placed = (P(pop, wa, None), P(None, wa), P(pop, None), P(pop, None), P())
    return jax.shard_map(
        shards, mesh=fine, in_specs=placed, out_specs=(P(pop, wa), P(pop)), check_vma=False
    )
```

```python
import functools

import jax
import jax.numpy as jnp
import numpy as np
from jax import lax
from jax.experimental import pallas as pl
from jax.experimental.pallas import tpu as pltpu
from jax.sharding import Mesh, PartitionSpec as P

perturb_scale = 0.5
epsilon = 1e-05

XH, Z, CORE, XL, Y = 2, 8, 2, 2, 4
AXES = ("xh", "z", "core", "xl", "y")
SIZES = (XH, Z, CORE, XL, Y)
WA = XL * Y
CHAINS = 2
ROWS_ALL = 24
VMEM_BYTES = 46 * 1024 * 1024
SMALL_BYTES = 1024 * 1024


def permutation(move):
    pairs = []
    for i in range(int(np.prod(SIZES))):
        at = [int(v) for v in np.unravel_index(i, SIZES)]
        to = move(*at)
        pairs.append((i, int(np.ravel_multi_index(to, SIZES))))
    return pairs


def go_y(step):
    def move(xh, z, c, xl, y):
        s = step if c == 0 else -step
        return (xh, z, c, xl, (y + s) % Y)

    return permutation(move)


def go_x():
    def move(xh, z, c, xl, y):
        x = xh * 2 + xl
        if c == 0:
            x = x ^ 1
        else:
            x = (x + 1) % 4 if x % 2 else (x - 1) % 4
        return (x // 2, z, c, x % 2, y)

    return permutation(move)


def go_core():
    return permutation(lambda xh, z, c, xl, y: (xh, z, 1 - c, xl, y))


def go_xh():
    return permutation(lambda xh, z, c, xl, y: (1 - xh, z, c, xl, y))


def nt_dot(a, b):
    return lax.dot_general(a, b, (((1,), (1,)), ((), ())), preferred_element_type=jnp.float32)


def fetch_columns(kidx, base, count, block, sources, buffers, sems):
    copies = []
    for s in range(count):
        cols = pl.ds(pl.multiple_of(kidx[base + s] * block, block), block)
        for side in range(2):
            copy = pltpu.make_async_copy(
                sources[side].at[:, :, cols], buffers.at[s, side], sems.at[s, side]
            )
            copy.start()
            copies.append(copy)
    return copies


def fetch_weights(sent, ws, sems):
    copies = []
    for s, w in enumerate(sent):
        copy = pltpu.make_async_copy(w, ws.at[s], sems.at[s])
        copy.start()
        copies.append(copy)
    return copies


def group_kernel(base, count, has_acc, extra, kidx, x_own, x_oth, *refs):
    refs = refs[extra:]
    sent = refs[:count]
    acc_in = refs[count] if has_acc else None
    out, token, ws, w_sems, buffers, sems = refs[-6:]
    members, width = out.shape[2], out.shape[3]
    block = sent[0].shape[1]
    copies = fetch_columns(kidx, base, count, block, (x_own, x_oth), buffers, sems)
    fetched = fetch_weights(sent, ws, w_sems)
    token[...] = jnp.zeros_like(token)
    chunk = 512
    for side in range(2):
        for s in range(count):
            copies[2 * s + side].wait()
            if side == 0:
                fetched[s].wait()
        for j in range(0, width, chunk):
            cols = pl.ds(j, chunk)
            total = None
            for s in range(count):
                part = nt_dot(buffers[s, side].reshape(3 * members, block), ws[s, cols, :])
                total = part if total is None else total + part
            total = total.reshape(3, members, chunk)
            if has_acc:
                total = total + acc_in[side, :, :, cols]
            out[side, :, :, cols] = total


def group_matmul(base, kidx, x_own, x_oth, ws, acc, extra=()):
    count = len(ws)
    members = x_own.shape[1]
    width, block = ws[0].shape
    smem = pl.BlockSpec(memory_space=pltpu.SMEM)
    vmem = pl.BlockSpec(memory_space=pltpu.VMEM)
    hbm = pl.BlockSpec(memory_space=pltpu.HBM)
    args = [x_own, x_oth, *extra] + list(ws)
    specs = [smem, hbm, hbm] + [hbm] * len(extra) + [hbm] * count
    alias = {}
    if acc is not None:
        specs.append(vmem)
        args.append(acc)
        alias = {len(args): 0}
    flops = 2 * 2 * 3 * members * width * block * count
    return pl.pallas_call(
        functools.partial(group_kernel, base, count, acc is not None, len(extra)),
        out_shape=(
            jax.ShapeDtypeStruct((2, 3, members, width), jnp.float32),
            jax.ShapeDtypeStruct((8, 128), jnp.float32),
        ),
        in_specs=specs,
        out_specs=(vmem, vmem),
        scratch_shapes=[
            pltpu.VMEM((count, width, block), jnp.bfloat16),
            pltpu.SemaphoreType.DMA((count,)),
            pltpu.VMEM((count, 2, 3, members, block), jnp.bfloat16),
            pltpu.SemaphoreType.DMA((count, 2)),
        ],
        input_output_aliases=alias,
        compiler_params=pltpu.CompilerParams(vmem_limit_bytes=VMEM_BYTES),
        cost_estimate=pl.CostEstimate(flops=flops, bytes_accessed=16 * 1024 * 1024, transcendentals=0),
    )(kidx, *args)


def last_kernel(first, kidx, x_own, x_oth, sent, pieces, acc, low_own, low_oth, fout_own, fout_oth, readout, *refs):
    before = refs[0] if len(refs) == 6 else None
    out, w, w_sems, buffers, sems = refs[-5:]
    members, width = acc.shape[2], acc.shape[3]
    block = sent.shape[1]
    fetched = fetch_weights([sent], w, w_sems)
    copies = fetch_columns(kidx, 7, 1, block, (x_own, x_oth), buffers, sems)
    fetched[0].wait()
    chunk = 256
    ones = jnp.ones((8, 128), jnp.float32)
    for side, low, fout in ((0, low_own, fout_own), (1, low_oth, fout_oth)):
        copies[side].wait()
        total = jnp.zeros((members, 128), jnp.float32)
        for j in range(0, width, chunk):
            cols = pl.ds(j, chunk)
            part = nt_dot(buffers[0, side].reshape(3 * members, block), w[0, cols, :])
            part = part.reshape(3, members, chunk)
            shift = fout[:, pl.ds(first + j, chunk)].astype(jnp.float32)
            summed = None
            for r in range(3):
                pert = part[r] + acc[side, r, :, cols] + low[r] * shift
                term = jnp.tanh(pert)
                summed = term if summed is None else summed + term
            summed = summed * readout[:, pl.ds(first + j, chunk)]
            for h in range(0, chunk, 128):
                total = total + summed[:, h : h + 128]
        row = lax.dot_general(
            ones,
            total,
            (((1,), (1,)), ((), ())),
            preferred_element_type=jnp.float32,
            precision=lax.Precision.HIGHEST,
        )[0:1]
        at = pl.ds(pl.multiple_of(jnp.bitwise_xor(kidx[8], side) * members, members), members)
        if before is not None:
            row = row + before[0, :, at]
        for k in range(out.shape[0]):
            out[k, :, at] = row


def last_matmul(first, kidx, x_own, x_oth, w, pieces, acc, low_own, low_oth, fout_own, fout_oth, readout, before):
    members = x_own.shape[1]
    width, block = w.shape
    smem = pl.BlockSpec(memory_space=pltpu.SMEM)
    vmem = pl.BlockSpec(memory_space=pltpu.VMEM)
    hbm = pl.BlockSpec(memory_space=pltpu.HBM)
    args = [acc, low_own, low_oth, fout_own, fout_oth, readout]
    if before is not None:
        args.append(before)
    return pl.pallas_call(
        functools.partial(last_kernel, first),
        out_shape=jax.ShapeDtypeStruct((CORE * WA, 1, 2 * members), jnp.float32),
        in_specs=[smem, hbm, hbm, hbm, hbm] + [vmem] * len(args),
        out_specs=vmem,
        scratch_shapes=[
            pltpu.VMEM((1, width, block), jnp.bfloat16),
            pltpu.SemaphoreType.DMA((1,)),
            pltpu.VMEM((1, 2, 3, members, block), jnp.bfloat16),
            pltpu.SemaphoreType.DMA((1, 2)),
        ],
        compiler_params=pltpu.CompilerParams(vmem_limit_bytes=VMEM_BYTES),
        cost_estimate=pl.CostEstimate(
            flops=2 * 6 * members * width * block,
            bytes_accessed=6 * 1024 * 1024,
            transcendentals=6 * members * width,
        ),
    )(kidx, x_own, x_oth, w, pieces, *args)


def after_kernel(*refs):
    pass


def after(values, *done):
    hbm = pl.BlockSpec(memory_space=pl.ANY)
    count = len(values)
    return pl.pallas_call(
        after_kernel,
        out_shape=tuple(jax.ShapeDtypeStruct(v.shape, v.dtype) for v in values),
        in_specs=[hbm] * (count + len(done)),
        out_specs=(hbm,) * count,
        input_output_aliases={i: i for i in range(count)},
        compiler_params=pltpu.CompilerParams(vmem_limit_bytes=SMALL_BYTES),
    )(*values, *done)


def sum_kernel(got, out):
    out[...] = jnp.broadcast_to(jnp.sum(got[...], axis=0, keepdims=True) / ROWS_ALL, out.shape)


def sum_and_copy(got):
    vmem = pl.BlockSpec(memory_space=pltpu.VMEM)
    return pl.pallas_call(
        sum_kernel,
        out_shape=jax.ShapeDtypeStruct((XH * Z,) + got.shape[1:], jnp.float32),
        in_specs=[vmem],
        out_specs=vmem,
        compiler_params=pltpu.CompilerParams(vmem_limit_bytes=SMALL_BYTES),
    )(got)


def take_kernel(place, weight, fin, *refs):
    parts, fin_here, sems = refs[:-2], refs[-2], refs[-1]
    rows, block = parts[0].shape
    copies = []
    for h, out in enumerate(parts):
        at = pl.ds(pl.multiple_of(place[8] * (rows * len(parts)) + h * rows, rows), rows)
        copies.append(pltpu.make_async_copy(weight.at[at, :], out, sems.at[h]))
    cols = pl.ds(pl.multiple_of(place[0] * block, block), block)
    copies.append(pltpu.make_async_copy(fin.at[:, cols], fin_here, sems.at[len(parts)]))
    for copy in copies:
        copy.start()
    for copy in copies:
        copy.wait()


def take_blocks(place, weight, fin, part):
    block = weight.shape[1]
    hbm = pl.BlockSpec(memory_space=pl.ANY)
    shapes = [jax.ShapeDtypeStruct((part, block), weight.dtype)] * CHAINS
    shapes.append(jax.ShapeDtypeStruct((fin.shape[0], block), fin.dtype))
    return pl.pallas_call(
        take_kernel,
        out_shape=tuple(shapes),
        in_specs=[pl.BlockSpec(memory_space=pltpu.SMEM), hbm, hbm],
        out_specs=(hbm,) * len(shapes),
        scratch_shapes=[pltpu.SemaphoreType.DMA((len(shapes),))],
        compiler_params=pltpu.CompilerParams(vmem_limit_bytes=VMEM_BYTES),
    )(place, weight, fin)


def low_kernel(place, x, fin, fout, readout, out, pieces, mine, theirs, read, x_buf, f_buf, sems, out_sems):
    tiles, rows, tile, width = x_buf.shape
    copies = []
    for t in range(tiles):
        span = pl.ds(t * tile, tile)
        pair = (
            pltpu.make_async_copy(x.at[:, span, :], x_buf.at[t], sems.at[t, 0]),
            pltpu.make_async_copy(fin.at[span, :], f_buf.at[t], sems.at[t, 1]),
        )
        for copy in pair:
            copy.start()
        copies.append(pair)
    half = mine.shape[1]
    moves = []
    for at, to in ((place[8], mine), (1 - place[8], theirs)):
        cols = pl.ds(pl.multiple_of(at * half, half), half)
        moves.append((fout.at[:, cols], to))
    run = pieces.shape[2] // XH
    for h in range(XH):
        for k in range(Z):
            cols = pl.ds(h * half + k * run, run)
            moves.append((fout.at[:, cols], pieces.at[k, :, pl.ds(h * run, run)]))
    moved = [pltpu.make_async_copy(a, b, out_sems.at[i]) for i, (a, b) in enumerate(moves)]
    for copy in moved:
        copy.start()
    read[...] = readout[:, pl.ds(pl.multiple_of(place[8] * half, half), half)]
    chunk = 128
    for t in range(tiles):
        for copy in copies[t]:
            copy.wait()
        totals = [None] * rows
        for j in range(0, width, chunk):
            cols = pl.ds(j, chunk)
            f = f_buf[t, :, cols].astype(jnp.float32)
            for r in range(rows):
                term = x_buf[t, r, :, cols].astype(jnp.float32) * f
                totals[r] = term if totals[r] is None else totals[r] + term
        for r in range(rows):
            out[r, pl.ds(t * tile, tile), :] = perturb_scale * jnp.sum(totals[r], axis=1, keepdims=True)
    for copy in moved:
        copy.wait()


def low_term(place, x, fin, fout, readout):
    rows, members, width = x.shape
    out_width = fout.shape[1]
    half = out_width // CORE
    tile = 64
    tiles = members // tile
    hbm = pl.BlockSpec(memory_space=pl.ANY)
    vmem = pl.BlockSpec(memory_space=pltpu.VMEM)
    return pl.pallas_call(
        low_kernel,
        out_shape=(
            jax.ShapeDtypeStruct((rows, members, 1), jnp.float32),
            jax.ShapeDtypeStruct((Z, members, out_width // Z), fout.dtype),
            jax.ShapeDtypeStruct((members, half), fout.dtype),
            jax.ShapeDtypeStruct((members, half), fout.dtype),
            jax.ShapeDtypeStruct((1, half), readout.dtype),
        ),
        in_specs=[pl.BlockSpec(memory_space=pltpu.SMEM), hbm, hbm, hbm, vmem],
        out_specs=(vmem, hbm, hbm, hbm, vmem),
        scratch_shapes=[
            pltpu.VMEM((tiles, rows, tile, width), jnp.bfloat16),
            pltpu.VMEM((tiles, tile, width), jnp.bfloat16),
            pltpu.SemaphoreType.DMA((tiles, 2)),
            pltpu.SemaphoreType.DMA((2 + XH * Z,)),
        ],
        compiler_params=pltpu.CompilerParams(vmem_limit_bytes=VMEM_BYTES),
        cost_estimate=pl.CostEstimate(
            flops=2 * rows * members * width, bytes_accessed=9 * 1024 * 1024, transcendentals=0
        ),
    )(place, x, fin, fout, readout)


def step_kernel(place, fit, fout, fin, keep, give, util, rows_ref):
    values = fit[...]
    members = fin.shape[1]
    count = values.shape[0] * values.shape[2]
    mean = jnp.sum(values) / count
    spread = jnp.sum((values - mean) ** 2) / count
    root = jnp.sqrt(jnp.full((1, 1), spread + epsilon, jnp.float32))
    c, xh, z = place[8], place[9], place[10]
    at = pl.ds(pl.multiple_of(c * members, members), members)
    util[...] = (fit[xh * Z + z, :, at] - mean) / root
    for k in range(Z):
        rows_ref[k : k + 1, :] = fit[xh * Z + k, :, at]
    columns = (jnp.transpose(rows_ref[...]) - mean) / root
    total = None
    for k in range(Z):
        scaled = (fout[k].astype(jnp.float32) * columns[:, k : k + 1]).astype(jnp.bfloat16)
        one = lax.dot_general(
            scaled, fin[k], (((0,), (0,)), ((), ())), preferred_element_type=jnp.float32
        )
        total = one if total is None else total + one
    total = total * (1.0 / np.sqrt(float(count)))
    rows = keep.shape[1]
    total = total.reshape(XH, CORE, rows, total.shape[1])
    for h in range(XH):
        to = jnp.bitwise_xor(xh, h)
        keep[to] = jnp.where(c == 0, total[h, 0], total[h, 1])
        give[to] = jnp.where(c == 0, total[h, 1], total[h, 0])


def weight_part(place, fit, fout, fin):
    members, rows = fout.shape[1], fout.shape[2]
    cols = fin.shape[2]
    vmem = pl.BlockSpec(memory_space=pltpu.VMEM)
    block = jax.ShapeDtypeStruct((XH, rows // (XH * CORE), cols), jnp.float32)
    return pl.pallas_call(
        step_kernel,
        out_shape=(block, block, jax.ShapeDtypeStruct((1, members), jnp.float32)),
        in_specs=[pl.BlockSpec(memory_space=pltpu.SMEM), vmem, vmem, vmem],
        out_specs=(vmem, vmem, vmem),
        scratch_shapes=[pltpu.VMEM((Z, members), jnp.float32)],
        compiler_params=pltpu.CompilerParams(vmem_limit_bytes=VMEM_BYTES),
        cost_estimate=pl.CostEstimate(
            flops=2 * rows * Z * members * cols, bytes_accessed=4 * 1024 * 1024, transcendentals=0
        ),
    )(place, fit, fout, fin)


def share(x, axes):
    return lax.all_to_all(x, axes, 0, 0, tiled=True)


def shards(inputs, weight, factor_in, factor_out, readout):
    members, rows_here, width = inputs.shape
    out_width, block = weight.shape
    half = out_width // 2
    xh, z, c, xl, y = (lax.axis_index(a) for a in AXES)
    wa = xl * Y + y
    sign = 1 - 2 * c
    y_fwd, y_bwd, x_go, core_go = go_y(1), go_y(-1), go_x(), go_core()

    def send(v, pairs):
        return lax.ppermute(v, AXES, pairs)

    def col(xl_at, off):
        return xl_at * Y + lax.rem(y + off + Y, Y)

    xo = 1 - xl
    k_own, k_a, k_b, k_c = col(xl, 0), col(xl, -sign), col(xl, sign), col(xl, 2)
    k_d, k_e, k_f, k_g = col(xo, 0), col(xo, -sign), col(xo, sign), col(xo, 2)

    x_own = inputs.transpose(1, 0, 2)
    def col(xl_at, off):
        return xl_at * Y + lax.rem(y + off + Y, Y)

    xo = 1 - xl
    k_own, k_a, k_b, k_c = col(xl, 0), col(xl, -sign), col(xl, sign), col(xl, 2)
    k_d, k_e, k_f, k_g = col(xo, 0), col(xo, -sign), col(xo, sign), col(xo, 2)

    x_own = inputs.transpose(1, 0, 2)
    w_own = lax.dynamic_slice_in_dim(weight, c * half, half, 0)

    places = jnp.stack([k_own, k_a, k_d, k_b, k_e, k_f, k_c, k_g, c, xh, z]).astype(jnp.int32)

    part = half // CHAINS
    chains = range(CHAINS)
    *own, fin_here = take_blocks(places, weight, factor_in, part)
    w_a = [send(w, y_fwd) for w in own]
    w_d = [send(w, x_go) for w in own]
    x_oth = send(x_own, core_go)

    low_own, pieces_here, fout_mine, fout_theirs, read_mine = low_term(
        places, x_own, factor_in, factor_out, readout[None]
    )
    fin_all = lax.all_gather(fin_here, "z", axis=0)
    pieces = lax.all_to_all(pieces_here, "z", 0, 0, tiled=True)
    low_oth = send(low_own, core_go)
    fout_got = send(fout_theirs, core_go)

    w_b, w_e, w_c, w_f, acc, token = ([None] * CHAINS for _ in range(6))
    for h in chains:
        own[h], w_a[h], w_d[h] = after((own[h], w_a[h], w_d[h]), low_own)
        w_b[h] = send(own[h], y_bwd)
        w_e[h] = send(w_a[h], x_go)
        acc[h], token[h] = group_matmul(
            0, places, x_own, x_oth, [own[h], w_a[h], w_d[h]], None
        )
    for h in chains:
        w_a[h], w_b[h], w_e[h] = after((w_a[h], w_b[h], w_e[h]), token[h])
        w_c[h] = send(w_a[h], y_fwd)
        w_f[h] = send(w_b[h], x_go)
        acc[h], token[h] = group_matmul(
            3, places, x_own, x_oth, [w_b[h], w_e[h]], acc[h], (low_oth, fout_got)
        )
    w_g = [None] * CHAINS
    for h in chains:
        w_c[h], w_f[h], w_e[h] = after((w_c[h], w_f[h], w_e[h]), token[h])
        w_g[h] = send(w_c[h], x_go) if h == 0 else send(w_e[h], y_fwd)
        acc[h], token[h] = group_matmul(
            5, places, x_own, x_oth, [w_f[h], w_c[h]], acc[h]
        )
    partial = None
    for h in chains:
        partial = last_matmul(
            h * part, places, x_own, x_oth, w_g[h], pieces if h == 1 else w_g[h], acc[h],
            low_own, low_oth, fout_mine, fout_got, read_mine, partial,
        )

    fit = share(sum_and_copy(share(partial, ("core", "xl", "y"))), ("xh", "z"))

    keep, give, util = weight_part(places, fit, pieces, fin_all)
    summed = keep + send(give, core_go)
    weight_step = summed[0] + send(summed[1], go_xh())
    return weight_step, util.reshape(members)


def solution(mesh):
    fine = Mesh(mesh.devices.reshape(SIZES), AXES)
    pop, wa = ("xh", "z", "core"), ("xl", "y")
    placed = (P(pop, wa, None), P(None, wa), P(pop, None), P(pop, None), P())
    return jax.shard_map(
        shards, mesh=fine, in_specs=placed, out_specs=(P(pop, wa), P(pop)), check_vma=False
    )
```

```python
import functools

import jax
import jax.numpy as jnp
import numpy as np
from jax import lax
from jax.experimental import pallas as pl
from jax.experimental.pallas import tpu as pltpu
from jax.sharding import Mesh, PartitionSpec as P

perturb_scale = 0.5
epsilon = 1e-05

XH, Z, CORE, XL, Y = 2, 8, 2, 2, 4
AXES = ("xh", "z", "core", "xl", "y")
SIZES = (XH, Z, CORE, XL, Y)
WA = XL * Y
CHAINS = 2
ROWS_ALL = 24
VMEM_BYTES = 41 * 1024 * 1024
LAST_BYTES = 41 * 1024 * 1024
SMALL_BYTES = 1024 * 1024
LARGE_BYTES = 58 * 1024 * 1024


def permutation(move):
    pairs = []
    for i in range(int(np.prod(SIZES))):
        at = [int(v) for v in np.unravel_index(i, SIZES)]
        to = move(*at)
        pairs.append((i, int(np.ravel_multi_index(to, SIZES))))
    return pairs


def go_y(step):
    def move(xh, z, c, xl, y):
        s = step if c == 0 else -step
        return (xh, z, c, xl, (y + s) % Y)

    return permutation(move)


def go_x():
    def move(xh, z, c, xl, y):
        x = xh * 2 + xl
        if c == 0:
            x = x ^ 1
        else:
            x = (x + 1) % 4 if x % 2 else (x - 1) % 4
        return (x // 2, z, c, x % 2, y)

    return permutation(move)


def go_core():
    return permutation(lambda xh, z, c, xl, y: (xh, z, 1 - c, xl, y))


def go_xh():
    return permutation(lambda xh, z, c, xl, y: (1 - xh, z, c, xl, y))


def nt_dot(a, b):
    return lax.dot_general(a, b, (((1,), (1,)), ((), ())), preferred_element_type=jnp.float32)


def fetch(kidx, base, x_own, x_oth, sent, ws, w_sems, buffers, sems):
    count, part, block = len(sent), sent[0][0].shape[0], sent[0][0].shape[1]
    waits = [[], []]

    def start(source, to, sem, side):
        copy = pltpu.make_async_copy(source, to, sem)
        copy.start()
        waits[side].append(copy)

    for side, x in ((0, x_own), (1, x_oth)):
        for s in range(count):
            if side == 0:
                for h in range(CHAINS):
                    start(sent[s][h], ws.at[s, pl.ds(h * part, part), :], w_sems.at[s, h], side)
            cols = pl.ds(pl.multiple_of(kidx[base + s] * block, block), block)
            start(x.at[:, :, cols], buffers.at[s, side], sems.at[s, side], side)
    return waits


def fetch_scratch(count, members, width, block):
    return [
        pltpu.VMEM((count, width, block), jnp.bfloat16),
        pltpu.SemaphoreType.DMA((count, CHAINS)),
        pltpu.VMEM((count, 2, 3, members, block), jnp.bfloat16),
        pltpu.SemaphoreType.DMA((count, 2)),
    ]


def pairs(refs):
    return [refs[i : i + CHAINS] for i in range(0, len(refs), CHAINS)]


def group_kernel(base, count, has_acc, ahead, kidx, x_own, x_oth, *refs):
    sent = pairs(refs[: count * CHAINS])
    acc_in = refs[count * CHAINS] if has_acc else None
    if ahead:
        *refs, x_last, ws, w_sems, buffers, sems, last_sems = refs
        refs = (*refs, ws, w_sems, buffers, sems)
    out, token, ws, w_sems, buffers, sems = refs[-6:]
    members, width = out.shape[2], out.shape[3]
    block = ws.shape[2]
    waits = fetch(kidx, base, x_own, x_oth, sent, ws, w_sems, buffers, sems)
    early = []
    if ahead:
        cols = pl.ds(pl.multiple_of(kidx[base + count] * block, block), block)
        for side, x in ((0, x_own), (1, x_oth)):
            early.append(pltpu.make_async_copy(x.at[:, :, cols], x_last.at[side], last_sems.at[side]))
            early[-1].start()
    token[...] = jnp.zeros_like(token)
    chunk = 512
    for side in range(2):
        for copy in waits[side]:
            copy.wait()
        for j in range(0, width, chunk):
            cols = pl.ds(j, chunk)
            total = None
            for s in range(count):
                part = nt_dot(buffers[s, side].reshape(3 * members, block), ws[s, cols, :])
                total = part if total is None else total + part
            total = total.reshape(3, members, chunk)
            if has_acc:
                total = total + acc_in[side, :, :, cols]
            out[side, :, :, cols] = total
    for copy in early:
        copy.wait()


def group_matmul(base, kidx, x_own, x_oth, sent, acc, ahead=False):
    count = len(sent)
    members = x_own.shape[1]
    part, block = sent[0][0].shape
    width = part * CHAINS
    smem = pl.BlockSpec(memory_space=pltpu.SMEM)
    vmem = pl.BlockSpec(memory_space=pltpu.VMEM)
    hbm = pl.BlockSpec(memory_space=pl.ANY)
    args = [x_own, x_oth] + [w for ws in sent for w in ws]
    specs = [smem] + [hbm] * len(args)
    alias = {}
    if acc is not None:
        specs.append(vmem)
        args.append(acc)
        alias = {len(args): 0}
    flops = 2 * 2 * 3 * members * width * block * count
    return pl.pallas_call(
        functools.partial(group_kernel, base, count, acc is not None, ahead),
        out_shape=(
            jax.ShapeDtypeStruct((2, 3, members, width), jnp.float32),
            jax.ShapeDtypeStruct((8, 128), jnp.float32),
        )
        + ((jax.ShapeDtypeStruct((2, 3, members, block), x_own.dtype),) if ahead else ()),
        in_specs=specs,
        out_specs=(vmem,) * (3 if ahead else 2),
        scratch_shapes=fetch_scratch(count, members, width, block)
        + ([pltpu.SemaphoreType.DMA((2,))] if ahead else []),
        input_output_aliases=alias,
        compiler_params=pltpu.CompilerParams(vmem_limit_bytes=VMEM_BYTES),
        cost_estimate=pl.CostEstimate(flops=flops, bytes_accessed=8 * 1024 * 1024, transcendentals=0),
    )(kidx, *args)


def last_kernel(kidx, *refs):
    sent = refs[:CHAINS]
    x, acc, low_own, low_oth, fout_own, fout_oth, readout, out, ws, w_sems = refs[CHAINS:]
    members, width = acc.shape[2], acc.shape[3]
    block = ws.shape[1]
    part_rows = sent[0].shape[0]
    copies = []
    for h in range(CHAINS):
        to = ws.at[pl.ds(h * part_rows, part_rows), :]
        copies.append(pltpu.make_async_copy(sent[h], to, w_sems.at[h]))
        copies[-1].start()
    for copy in copies:
        copy.wait()
    chunk = 256
    ones = jnp.ones((8, 128), jnp.float32)
    for side, low, fout in ((0, low_own, fout_own), (1, low_oth, fout_oth)):
        total = jnp.zeros((members, 128), jnp.float32)
        for j in range(0, width, chunk):
            cols = pl.ds(j, chunk)
            part = nt_dot(x[side].reshape(3 * members, block), ws[cols, :])
            part = part.reshape(3, members, chunk)
            shift = fout[:, cols].astype(jnp.float32)
            summed = None
            for r in range(3):
                pert = part[r] + acc[side, r, :, cols] + low[r] * shift
                term = jnp.tanh(pert)
                summed = term if summed is None else summed + term
            summed = summed * readout[:, cols]
            for h in range(0, chunk, 128):
                total = total + summed[:, h : h + 128]
        row = lax.dot_general(
            ones,
            total,
            (((1,), (1,)), ((), ())),
            preferred_element_type=jnp.float32,
            precision=lax.Precision.HIGHEST,
        )[0:1]
        at = pl.ds(pl.multiple_of(jnp.bitwise_xor(kidx[8], side) * members, members), members)
        for k in range(out.shape[0]):
            out[k, :, at] = row


def last_matmul(kidx, sent, x, acc, low_own, low_oth, fout_own, fout_oth, readout):
    members = x.shape[2]
    part, block = sent[0].shape
    width = part * CHAINS
    smem = pl.BlockSpec(memory_space=pltpu.SMEM)
    vmem = pl.BlockSpec(memory_space=pltpu.VMEM)
    hbm = pl.BlockSpec(memory_space=pl.ANY)
    return pl.pallas_call(
        last_kernel,
        out_shape=jax.ShapeDtypeStruct((CORE * WA, 1, 2 * members), jnp.float32),
        in_specs=[smem] + [hbm] * CHAINS + [vmem] * 7,
        out_specs=vmem,
        scratch_shapes=[
            pltpu.VMEM((width, block), jnp.bfloat16),
            pltpu.SemaphoreType.DMA((CHAINS,)),
        ],
        compiler_params=pltpu.CompilerParams(vmem_limit_bytes=LAST_BYTES),
        cost_estimate=pl.CostEstimate(
            flops=2 * 6 * members * width * block,
            bytes_accessed=6 * 1024 * 1024,
            transcendentals=6 * members * width,
        ),
    )(kidx, *sent, x, acc, low_own, low_oth, fout_own, fout_oth, readout)


def after_kernel(*refs):
    pass


def after(values, *done):
    hbm = pl.BlockSpec(memory_space=pl.ANY)
    count = len(values)
    return pl.pallas_call(
        after_kernel,
        out_shape=tuple(jax.ShapeDtypeStruct(v.shape, v.dtype) for v in values),
        in_specs=[hbm] * (count + len(done)),
        out_specs=(hbm,) * count,
        input_output_aliases={i: i for i in range(count)},
        compiler_params=pltpu.CompilerParams(vmem_limit_bytes=SMALL_BYTES),
    )(*values, *done)


def sum_kernel(got, out):
    out[...] = jnp.broadcast_to(jnp.sum(got[...], axis=0, keepdims=True) / ROWS_ALL, out.shape)


def sum_and_copy(got):
    vmem = pl.BlockSpec(memory_space=pltpu.VMEM)
    return pl.pallas_call(
        sum_kernel,
        out_shape=jax.ShapeDtypeStruct((XH * Z,) + got.shape[1:], jnp.float32),
        in_specs=[vmem],
        out_specs=vmem,
        compiler_params=pltpu.CompilerParams(vmem_limit_bytes=SMALL_BYTES),
    )(got)


def take_kernel(place, weight, fin, *refs):
    parts, fin_here, sems = refs[:-2], refs[-2], refs[-1]
    rows, block = parts[0].shape
    copies = []
    for h, out in enumerate(parts):
        at = pl.ds(pl.multiple_of(place[8] * (rows * len(parts)) + h * rows, rows), rows)
        copies.append(pltpu.make_async_copy(weight.at[at, :], out, sems.at[h]))
    cols = pl.ds(pl.multiple_of(place[0] * block, block), block)
    copies.append(pltpu.make_async_copy(fin.at[:, cols], fin_here, sems.at[len(parts)]))
    for copy in copies:
        copy.start()
    for copy in copies:
        copy.wait()


def take_blocks(place, weight, fin, part):
    block = weight.shape[1]
    hbm = pl.BlockSpec(memory_space=pl.ANY)
    shapes = [jax.ShapeDtypeStruct((part, block), weight.dtype)] * CHAINS
    shapes.append(jax.ShapeDtypeStruct((fin.shape[0], block), fin.dtype))
    return pl.pallas_call(
        take_kernel,
        out_shape=tuple(shapes),
        in_specs=[pl.BlockSpec(memory_space=pltpu.SMEM), hbm, hbm],
        out_specs=(hbm,) * len(shapes),
        scratch_shapes=[pltpu.SemaphoreType.DMA((len(shapes),))],
        compiler_params=pltpu.CompilerParams(vmem_limit_bytes=LARGE_BYTES),
    )(place, weight, fin)


def low_kernel(place, x, fin, fout, readout, out, pieces, mine, theirs, read, x_buf, f_buf, sems, out_sems):
    tiles, rows, tile, width = x_buf.shape
    copies = []
    for t in range(tiles):
        span = pl.ds(t * tile, tile)
        pair = (
            pltpu.make_async_copy(x.at[:, span, :], x_buf.at[t], sems.at[t, 0]),
            pltpu.make_async_copy(fin.at[span, :], f_buf.at[t], sems.at[t, 1]),
        )
        for copy in pair:
            copy.start()
        copies.append(pair)
    half = mine.shape[1]
    moves = []
    for at, to in ((place[8], mine), (1 - place[8], theirs)):
        cols = pl.ds(pl.multiple_of(at * half, half), half)
        moves.append((fout.at[:, cols], to))
    run = pieces.shape[2] // XH
    for h in range(XH):
        for k in range(Z):
            cols = pl.ds(h * half + k * run, run)
            moves.append((fout.at[:, cols], pieces.at[k, :, pl.ds(h * run, run)]))
    moved = [pltpu.make_async_copy(a, b, out_sems.at[i]) for i, (a, b) in enumerate(moves)]
    for copy in moved:
        copy.start()
    read[...] = readout[:, pl.ds(pl.multiple_of(place[8] * half, half), half)]
    chunk = 128
    for t in range(tiles):
        for copy in copies[t]:
            copy.wait()
        totals = [None] * rows
        for j in range(0, width, chunk):
            cols = pl.ds(j, chunk)
            f = f_buf[t, :, cols].astype(jnp.float32)
            for r in range(rows):
                term = x_buf[t, r, :, cols].astype(jnp.float32) * f
                totals[r] = term if totals[r] is None else totals[r] + term
        for r in range(rows):
            out[r, pl.ds(t * tile, tile), :] = perturb_scale * jnp.sum(totals[r], axis=1, keepdims=True)
    for copy in moved:
        copy.wait()


def low_term(place, x, fin, fout, readout):
    rows, members, width = x.shape
    out_width = fout.shape[1]
    half = out_width // CORE
    tile = 64
    tiles = members // tile
    hbm = pl.BlockSpec(memory_space=pl.ANY)
    vmem = pl.BlockSpec(memory_space=pltpu.VMEM)
    return pl.pallas_call(
        low_kernel,
        out_shape=(
            jax.ShapeDtypeStruct((rows, members, 1), jnp.float32),
            jax.ShapeDtypeStruct((Z, members, out_width // Z), fout.dtype),
            jax.ShapeDtypeStruct((members, half), fout.dtype),
            jax.ShapeDtypeStruct((members, half), fout.dtype),
            jax.ShapeDtypeStruct((1, half), readout.dtype),
        ),
        in_specs=[pl.BlockSpec(memory_space=pltpu.SMEM), hbm, hbm, hbm, vmem],
        out_specs=(vmem, hbm, hbm, hbm, vmem),
        scratch_shapes=[
            pltpu.VMEM((tiles, rows, tile, width), jnp.bfloat16),
            pltpu.VMEM((tiles, tile, width), jnp.bfloat16),
            pltpu.SemaphoreType.DMA((tiles, 2)),
            pltpu.SemaphoreType.DMA((2 + XH * Z,)),
        ],
        compiler_params=pltpu.CompilerParams(vmem_limit_bytes=LARGE_BYTES),
        cost_estimate=pl.CostEstimate(
            flops=2 * rows * members * width, bytes_accessed=9 * 1024 * 1024, transcendentals=0
        ),
    )(place, x, fin, fout, readout)


def step_kernel(place, fit, fout_all, fin_all, keep, give, util, rows_ref, fout, fin, sems):
    copies = []
    for k in range(Z):
        pair = (
            pltpu.make_async_copy(fout_all.at[k], fout.at[k], sems.at[k, 0]),
            pltpu.make_async_copy(fin_all.at[k], fin.at[k], sems.at[k, 1]),
        )
        for copy in pair:
            copy.start()
        copies.append(pair)
    values = fit[...]
    members = fin.shape[1]
    count = values.shape[0] * values.shape[2]
    mean = jnp.sum(values) / count
    spread = jnp.sum((values - mean) ** 2) / count
    root = jnp.sqrt(jnp.full((1, 1), spread + epsilon, jnp.float32))
    c, xh, z = place[8], place[9], place[10]
    at = pl.ds(pl.multiple_of(c * members, members), members)
    util[...] = (fit[xh * Z + z, :, at] - mean) / root
    for k in range(Z):
        rows_ref[k : k + 1, :] = fit[xh * Z + k, :, at]
    columns = (jnp.transpose(rows_ref[...]) - mean) / root
    total = None
    for k in range(Z):
        for copy in copies[k]:
            copy.wait()
        scaled = (fout[k].astype(jnp.float32) * columns[:, k : k + 1]).astype(jnp.bfloat16)
        one = lax.dot_general(
            scaled, fin[k], (((0,), (0,)), ((), ())), preferred_element_type=jnp.float32
        )
        total = one if total is None else total + one
    total = total * (1.0 / np.sqrt(float(count)))
    rows = keep.shape[1]
    total = total.reshape(XH, CORE, rows, total.shape[1])
    for h in range(XH):
        to = jnp.bitwise_xor(xh, h)
        keep[to] = jnp.where(c == 0, total[h, 0], total[h, 1])
        give[to] = jnp.where(c == 0, total[h, 1], total[h, 0])


def weight_part(place, fit, fout, fin):
    members, rows = fout.shape[1], fout.shape[2]
    cols = fin.shape[2]
    vmem = pl.BlockSpec(memory_space=pltpu.VMEM)
    hbm = pl.BlockSpec(memory_space=pl.ANY)
    block = jax.ShapeDtypeStruct((XH, rows // (XH * CORE), cols), jnp.float32)
    return pl.pallas_call(
        step_kernel,
        out_shape=(block, block, jax.ShapeDtypeStruct((1, members), jnp.float32)),
        in_specs=[pl.BlockSpec(memory_space=pltpu.SMEM), vmem, hbm, hbm],
        out_specs=(vmem, vmem, vmem),
        scratch_shapes=[
            pltpu.VMEM((Z, members), jnp.float32),
            pltpu.VMEM(fout.shape, fout.dtype),
            pltpu.VMEM(fin.shape, fin.dtype),
            pltpu.SemaphoreType.DMA((Z, 2)),
        ],
        compiler_params=pltpu.CompilerParams(vmem_limit_bytes=LARGE_BYTES),
        cost_estimate=pl.CostEstimate(
            flops=2 * rows * Z * members * cols, bytes_accessed=4 * 1024 * 1024, transcendentals=0
        ),
    )(place, fit, fout, fin)


def share(x, axes):
    return lax.all_to_all(x, axes, 0, 0, tiled=True)


def shards(inputs, weight, factor_in, factor_out, readout):
    members, rows_here, width = inputs.shape
    out_width, block = weight.shape
    half = out_width // 2
    xh, z, c, xl, y = (lax.axis_index(a) for a in AXES)
    wa = xl * Y + y
    sign = 1 - 2 * c
    y_fwd, y_bwd, x_go, core_go = go_y(1), go_y(-1), go_x(), go_core()

    def send(v, pairs):
        return lax.ppermute(v, AXES, pairs)

    def col(xl_at, off):
        return xl_at * Y + lax.rem(y + off + Y, Y)

    xo = 1 - xl
    k_own, k_a, k_b, k_c = col(xl, 0), col(xl, -sign), col(xl, sign), col(xl, 2)
    k_d, k_e, k_f, k_g = col(xo, 0), col(xo, -sign), col(xo, sign), col(xo, 2)

    x_own = inputs.transpose(1, 0, 2)
    def col(xl_at, off):
        return xl_at * Y + lax.rem(y + off + Y, Y)

    xo = 1 - xl
    k_own, k_a, k_b, k_c = col(xl, 0), col(xl, -sign), col(xl, sign), col(xl, 2)
    k_d, k_e, k_f, k_g = col(xo, 0), col(xo, -sign), col(xo, sign), col(xo, 2)

    x_own = inputs.transpose(1, 0, 2)
    w_own = lax.dynamic_slice_in_dim(weight, c * half, half, 0)

    places = jnp.stack([k_own, k_a, k_d, k_b, k_e, k_f, k_c, k_g, c, xh, z]).astype(jnp.int32)

    part = half // CHAINS
    chains = range(CHAINS)
    *own, fin_here = take_blocks(places, weight, factor_in, part)
    w_a = [send(w, y_fwd) for w in own]
    w_d = [send(w, x_go) for w in own]
    x_oth = send(x_own, core_go)

    low_own, pieces_here, fout_mine, fout_theirs, read_mine = low_term(
        places, x_own, factor_in, factor_out, readout[None]
    )
    fin_all = lax.all_gather(fin_here, "z", axis=0)
    pieces = lax.all_to_all(pieces_here, "z", 0, 0, tiled=True)
    low_oth = send(low_own, core_go)
    fout_got = send(fout_theirs, core_go)

    w_b, w_e, w_c, w_f, w_g = ([None] * CHAINS for _ in range(5))
    for h in chains:
        own[h], w_a[h], w_d[h] = after((own[h], w_a[h], w_d[h]), low_own)
        w_b[h] = send(own[h], y_bwd)
        w_e[h] = send(w_a[h], x_go)
    acc, token = group_matmul(0, places, x_own, x_oth, [own, w_a, w_d], None)
    for h in chains:
        w_a[h], w_b[h], w_e[h] = after((w_a[h], w_b[h], w_e[h]), token)
        w_c[h] = send(w_a[h], y_fwd)
        w_f[h] = send(w_b[h], x_go)
    acc, token = group_matmul(3, places, x_own, x_oth, [w_b, w_e], acc)
    for h in chains:
        w_c[h], w_f[h], w_e[h] = after((w_c[h], w_f[h], w_e[h]), token)
        w_g[h] = send(w_c[h], x_go) if h == 0 else send(w_e[h], y_fwd)
    acc, token, x_last = group_matmul(5, places, x_own, x_oth, [w_f, w_c], acc, ahead=True)
    partial = last_matmul(
        places, w_g, x_last, acc, low_own, low_oth, fout_mine, fout_got, read_mine
    )
    (partial,) = after((partial,), pieces)

    fit = share(sum_and_copy(share(partial, ("core", "xl", "y"))), ("xh", "z"))

    keep, give, util = weight_part(places, fit, pieces, fin_all)
    summed = keep + send(give, core_go)
    weight_step = summed[0] + send(summed[1], go_xh())
    return weight_step, util.reshape(members)


def solution(mesh):
    fine = Mesh(mesh.devices.reshape(SIZES), AXES)
    pop, wa = ("xh", "z", "core"), ("xl", "y")
    placed = (P(pop, wa, None), P(None, wa), P(pop, None), P(pop, None), P())
    return jax.shard_map(
        shards, mesh=fine, in_specs=placed, out_specs=(P(pop, wa), P(pop)), check_vma=False
    )
```

```python
import functools

import jax
import jax.numpy as jnp
import numpy as np
from jax import lax
from jax.experimental import pallas as pl
from jax.experimental.pallas import tpu as pltpu
from jax.sharding import Mesh, PartitionSpec as P

perturb_scale = 0.5
epsilon = 1e-05

XH, Z, CORE, XL, Y = 2, 8, 2, 2, 4
AXES = ("xh", "z", "core", "xl", "y")
SIZES = (XH, Z, CORE, XL, Y)
WA = XL * Y
CHAINS = 2
ROWS_ALL = 24
VMEM_BYTES = 41 * 1024 * 1024
LAST_BYTES = 41 * 1024 * 1024
SMALL_BYTES = 1024 * 1024
LARGE_BYTES = 58 * 1024 * 1024


def permutation(move):
    pairs = []
    for i in range(int(np.prod(SIZES))):
        at = [int(v) for v in np.unravel_index(i, SIZES)]
        to = move(*at)
        pairs.append((i, int(np.ravel_multi_index(to, SIZES))))
    return pairs


def go_y(step):
    def move(xh, z, c, xl, y):
        s = step if c == 0 else -step
        return (xh, z, c, xl, (y + s) % Y)

    return permutation(move)


def go_x():
    def move(xh, z, c, xl, y):
        x = xh * 2 + xl
        if c == 0:
            x = x ^ 1
        else:
            x = (x + 1) % 4 if x % 2 else (x - 1) % 4
        return (x // 2, z, c, x % 2, y)

    return permutation(move)


def go_core():
    return permutation(lambda xh, z, c, xl, y: (xh, z, 1 - c, xl, y))


def go_xh():
    return permutation(lambda xh, z, c, xl, y: (1 - xh, z, c, xl, y))


def nt_dot(a, b):
    return lax.dot_general(a, b, (((1,), (1,)), ((), ())), preferred_element_type=jnp.float32)


def fetch(kidx, base, x_own, x_oth, sent, ws, w_sems, buffers, sems):
    count, part, block = len(sent), sent[0][0].shape[0], sent[0][0].shape[1]
    waits = [[], []]

    def start(source, to, sem, side):
        copy = pltpu.make_async_copy(source, to, sem)
        copy.start()
        waits[side].append(copy)

    for side, x in ((0, x_own), (1, x_oth)):
        for s in range(count):
            if side == 0:
                for h in range(CHAINS):
                    start(sent[s][h], ws.at[s, pl.ds(h * part, part), :], w_sems.at[s, h], side)
            cols = pl.ds(pl.multiple_of(kidx[base + s] * block, block), block)
            start(x.at[:, :, cols], buffers.at[s, side], sems.at[s, side], side)
    return waits


def fetch_scratch(count, members, width, block):
    return [
        pltpu.VMEM((count, width, block), jnp.bfloat16),
        pltpu.SemaphoreType.DMA((count, CHAINS)),
        pltpu.VMEM((count, 2, 3, members, block), jnp.bfloat16),
        pltpu.SemaphoreType.DMA((count, 2)),
    ]


def pairs(refs):
    return [refs[i : i + CHAINS] for i in range(0, len(refs), CHAINS)]


def group_kernel(base, count, has_acc, ahead, kidx, x_own, x_oth, *refs):
    sent = pairs(refs[: count * CHAINS])
    acc_in = refs[count * CHAINS] if has_acc else None
    if ahead:
        *refs, x_last, ws, w_sems, buffers, sems, last_sems = refs
        refs = (*refs, ws, w_sems, buffers, sems)
    out, token, ws, w_sems, buffers, sems = refs[-6:]
    members, width = out.shape[2], out.shape[3]
    block = ws.shape[2]
    waits = fetch(kidx, base, x_own, x_oth, sent, ws, w_sems, buffers, sems)
    early = []
    if ahead:
        cols = pl.ds(pl.multiple_of(kidx[base + count] * block, block), block)
        for side, x in ((0, x_own), (1, x_oth)):
            early.append(pltpu.make_async_copy(x.at[:, :, cols], x_last.at[side], last_sems.at[side]))
            early[-1].start()
    token[...] = jnp.zeros_like(token)
    chunk = 512
    for side in range(2):
        for copy in waits[side]:
            copy.wait()
        for j in range(0, width, chunk):
            cols = pl.ds(j, chunk)
            total = None
            for s in range(count):
                part = nt_dot(buffers[s, side].reshape(3 * members, block), ws[s, cols, :])
                total = part if total is None else total + part
            total = total.reshape(3, members, chunk)
            if has_acc:
                total = total + acc_in[side, :, :, cols]
            out[side, :, :, cols] = total
    for copy in early:
        copy.wait()


def group_matmul(base, kidx, x_own, x_oth, sent, acc, ahead=False):
    count = len(sent)
    members = x_own.shape[1]
    part, block = sent[0][0].shape
    width = part * CHAINS
    smem = pl.BlockSpec(memory_space=pltpu.SMEM)
    vmem = pl.BlockSpec(memory_space=pltpu.VMEM)
    hbm = pl.BlockSpec(memory_space=pl.ANY)
    args = [x_own, x_oth] + [w for ws in sent for w in ws]
    specs = [smem] + [hbm] * len(args)
    alias = {}
    if acc is not None:
        specs.append(vmem)
        args.append(acc)
        alias = {len(args): 0}
    flops = 2 * 2 * 3 * members * width * block * count
    return pl.pallas_call(
        functools.partial(group_kernel, base, count, acc is not None, ahead),
        out_shape=(
            jax.ShapeDtypeStruct((2, 3, members, width), jnp.float32),
            jax.ShapeDtypeStruct((8, 128), jnp.float32),
        )
        + ((jax.ShapeDtypeStruct((2, 3, members, block), x_own.dtype),) if ahead else ()),
        in_specs=specs,
        out_specs=(vmem,) * (3 if ahead else 2),
        scratch_shapes=fetch_scratch(count, members, width, block)
        + ([pltpu.SemaphoreType.DMA((2,))] if ahead else []),
        input_output_aliases=alias,
        compiler_params=pltpu.CompilerParams(vmem_limit_bytes=VMEM_BYTES),
        cost_estimate=pl.CostEstimate(flops=flops, bytes_accessed=8 * 1024 * 1024, transcendentals=0),
    )(kidx, *args)


def last_kernel(kidx, *refs):
    sent = refs[:CHAINS]
    x, acc, low_own, low_oth, fout_own, fout_oth, readout, out, ws, w_sems = refs[CHAINS:]
    members, width = acc.shape[2], acc.shape[3]
    block = ws.shape[1]
    part_rows = sent[0].shape[0]
    copies = []
    for h in range(CHAINS):
        to = ws.at[pl.ds(h * part_rows, part_rows), :]
        copies.append(pltpu.make_async_copy(sent[h], to, w_sems.at[h]))
        copies[-1].start()
    for copy in copies:
        copy.wait()
    chunk = 256
    ones = jnp.ones((8, 128), jnp.float32)
    for side, low, fout in ((0, low_own, fout_own), (1, low_oth, fout_oth)):
        total = jnp.zeros((members, 128), jnp.float32)
        for j in range(0, width, chunk):
            cols = pl.ds(j, chunk)
            part = nt_dot(x[side].reshape(3 * members, block), ws[cols, :])
            part = part.reshape(3, members, chunk)
            shift = fout[:, cols].astype(jnp.float32)
            summed = None
            for r in range(3):
                pert = part[r] + acc[side, r, :, cols] + low[r] * shift
                term = jnp.tanh(pert)
                summed = term if summed is None else summed + term
            summed = summed * readout[:, cols]
            for h in range(0, chunk, 128):
                total = total + summed[:, h : h + 128]
        row = lax.dot_general(
            ones,
            total,
            (((1,), (1,)), ((), ())),
            preferred_element_type=jnp.float32,
            precision=lax.Precision.HIGHEST,
        )[0:1]
        at = pl.ds(pl.multiple_of(jnp.bitwise_xor(kidx[8], side) * members, members), members)
        for k in range(out.shape[0]):
            out[k, :, at] = row


def last_matmul(kidx, sent, x, acc, low_own, low_oth, fout_own, fout_oth, readout):
    members = x.shape[2]
    part, block = sent[0].shape
    width = part * CHAINS
    smem = pl.BlockSpec(memory_space=pltpu.SMEM)
    vmem = pl.BlockSpec(memory_space=pltpu.VMEM)
    hbm = pl.BlockSpec(memory_space=pl.ANY)
    return pl.pallas_call(
        last_kernel,
        out_shape=jax.ShapeDtypeStruct((CORE * WA, 1, 2 * members), jnp.float32),
        in_specs=[smem] + [hbm] * CHAINS + [vmem] * 7,
        out_specs=vmem,
        scratch_shapes=[
            pltpu.VMEM((width, block), jnp.bfloat16),
            pltpu.SemaphoreType.DMA((CHAINS,)),
        ],
        compiler_params=pltpu.CompilerParams(vmem_limit_bytes=LAST_BYTES),
        cost_estimate=pl.CostEstimate(
            flops=2 * 6 * members * width * block,
            bytes_accessed=6 * 1024 * 1024,
            transcendentals=6 * members * width,
        ),
    )(kidx, *sent, x, acc, low_own, low_oth, fout_own, fout_oth, readout)


def after_kernel(*refs):
    pass


def after(values, *done):
    hbm = pl.BlockSpec(memory_space=pl.ANY)
    count = len(values)
    return pl.pallas_call(
        after_kernel,
        out_shape=tuple(jax.ShapeDtypeStruct(v.shape, v.dtype) for v in values),
        in_specs=[hbm] * (count + len(done)),
        out_specs=(hbm,) * count,
        input_output_aliases={i: i for i in range(count)},
        compiler_params=pltpu.CompilerParams(vmem_limit_bytes=SMALL_BYTES),
    )(*values, *done)


def sum_kernel(got, out):
    out[...] = jnp.broadcast_to(jnp.sum(got[...], axis=0, keepdims=True) / ROWS_ALL, out.shape)


def sum_and_copy(got):
    vmem = pl.BlockSpec(memory_space=pltpu.VMEM)
    return pl.pallas_call(
        sum_kernel,
        out_shape=jax.ShapeDtypeStruct((XH * Z,) + got.shape[1:], jnp.float32),
        in_specs=[vmem],
        out_specs=vmem,
        compiler_params=pltpu.CompilerParams(vmem_limit_bytes=SMALL_BYTES),
    )(got)


def take_kernel(place, weight, fin, *refs):
    parts, fin_here, sems = refs[:-2], refs[-2], refs[-1]
    rows, block = parts[0].shape
    copies = []
    for h, out in enumerate(parts):
        at = pl.ds(pl.multiple_of(place[8] * (rows * len(parts)) + h * rows, rows), rows)
        copies.append(pltpu.make_async_copy(weight.at[at, :], out, sems.at[h]))
    cols = pl.ds(pl.multiple_of(place[0] * block, block), block)
    copies.append(pltpu.make_async_copy(fin.at[:, cols], fin_here, sems.at[len(parts)]))
    for copy in copies:
        copy.start()
    for copy in copies:
        copy.wait()


def take_blocks(place, weight, fin, part):
    block = weight.shape[1]
    hbm = pl.BlockSpec(memory_space=pl.ANY)
    shapes = [jax.ShapeDtypeStruct((part, block), weight.dtype)] * CHAINS
    shapes.append(jax.ShapeDtypeStruct((fin.shape[0], block), fin.dtype))
    return pl.pallas_call(
        take_kernel,
        out_shape=tuple(shapes),
        in_specs=[pl.BlockSpec(memory_space=pltpu.SMEM), hbm, hbm],
        out_specs=(pl.BlockSpec(memory_space=pltpu.VMEM),) * len(shapes),
        scratch_shapes=[pltpu.SemaphoreType.DMA((len(shapes),))],
        compiler_params=pltpu.CompilerParams(vmem_limit_bytes=LARGE_BYTES),
    )(place, weight, fin)


def low_kernel(place, x, fin, fout_all, readout, out, pieces, mine, theirs, read, x_buf, f_buf, fout, sems, out_sems):
    whole = pltpu.make_async_copy(fout_all, fout, out_sems.at[0])
    whole.start()
    tiles, rows, tile, width = x_buf.shape
    copies = []
    for t in range(tiles):
        span = pl.ds(t * tile, tile)
        pair = (
            pltpu.make_async_copy(x.at[:, span, :], x_buf.at[t], sems.at[t, 0]),
            pltpu.make_async_copy(fin.at[span, :], f_buf.at[t], sems.at[t, 1]),
        )
        for copy in pair:
            copy.start()
        copies.append(pair)
    half = mine.shape[1]
    moves = []
    for at, to in ((place[8], mine), (1 - place[8], theirs)):
        cols = pl.ds(pl.multiple_of(at * half, half), half)
        moves.append((fout.at[:, cols], to))
    run = pieces.shape[2] // XH
    for h in range(XH):
        for k in range(Z):
            cols = pl.ds(h * half + k * run, run)
            moves.append((fout.at[:, cols], pieces.at[k, :, pl.ds(h * run, run)]))
    moved = [pltpu.make_async_copy(a, b, out_sems.at[i + 1]) for i, (a, b) in enumerate(moves)]
    whole.wait()
    for copy in moved:
        copy.start()
    read[...] = readout[:, pl.ds(pl.multiple_of(place[8] * half, half), half)]
    chunk = 128
    for t in range(tiles):
        for copy in copies[t]:
            copy.wait()
        totals = [None] * rows
        for j in range(0, width, chunk):
            cols = pl.ds(j, chunk)
            f = f_buf[t, :, cols].astype(jnp.float32)
            for r in range(rows):
                term = x_buf[t, r, :, cols].astype(jnp.float32) * f
                totals[r] = term if totals[r] is None else totals[r] + term
        for r in range(rows):
            out[r, pl.ds(t * tile, tile), :] = perturb_scale * jnp.sum(totals[r], axis=1, keepdims=True)
    for copy in moved:
        copy.wait()


def low_term(place, x, fin, fout, readout):
    rows, members, width = x.shape
    out_width = fout.shape[1]
    half = out_width // CORE
    tile = 64
    tiles = members // tile
    hbm = pl.BlockSpec(memory_space=pl.ANY)
    vmem = pl.BlockSpec(memory_space=pltpu.VMEM)
    return pl.pallas_call(
        low_kernel,
        out_shape=(
            jax.ShapeDtypeStruct((rows, members, 1), jnp.float32),
            jax.ShapeDtypeStruct((Z, members, out_width // Z), fout.dtype),
            jax.ShapeDtypeStruct((members, half), fout.dtype),
            jax.ShapeDtypeStruct((members, half), fout.dtype),
            jax.ShapeDtypeStruct((1, half), readout.dtype),
        ),
        in_specs=[pl.BlockSpec(memory_space=pltpu.SMEM), hbm, hbm, hbm, vmem],
        out_specs=(vmem, hbm, hbm, hbm, vmem),
        scratch_shapes=[
            pltpu.VMEM((tiles, rows, tile, width), jnp.bfloat16),
            pltpu.VMEM((tiles, tile, width), jnp.bfloat16),
            pltpu.VMEM(fout.shape, fout.dtype),
            pltpu.SemaphoreType.DMA((tiles, 2)),
            pltpu.SemaphoreType.DMA((3 + XH * Z,)),
        ],
        compiler_params=pltpu.CompilerParams(vmem_limit_bytes=LARGE_BYTES),
        cost_estimate=pl.CostEstimate(
            flops=2 * rows * members * width, bytes_accessed=9 * 1024 * 1024, transcendentals=0
        ),
    )(place, x, fin, fout, readout)


def step_kernel(place, fit, fout_all, fin_all, keep, give, util, rows_ref, fout, fin, sems):
    copies = []
    for k in range(Z):
        pair = (
            pltpu.make_async_copy(fout_all.at[k], fout.at[k], sems.at[k, 0]),
            pltpu.make_async_copy(fin_all.at[k], fin.at[k], sems.at[k, 1]),
        )
        for copy in pair:
            copy.start()
        copies.append(pair)
    values = fit[...]
    members = fin.shape[1]
    count = values.shape[0] * values.shape[2]
    mean = jnp.sum(values) / count
    spread = jnp.sum((values - mean) ** 2) / count
    root = jnp.sqrt(jnp.full((1, 1), spread + epsilon, jnp.float32))
    c, xh, z = place[8], place[9], place[10]
    at = pl.ds(pl.multiple_of(c * members, members), members)
    util[...] = (fit[xh * Z + z, :, at] - mean) / root
    for k in range(Z):
        rows_ref[k : k + 1, :] = fit[xh * Z + k, :, at]
    columns = (jnp.transpose(rows_ref[...]) - mean) / root
    total = None
    for k in range(Z):
        for copy in copies[k]:
            copy.wait()
        scaled = (fout[k].astype(jnp.float32) * columns[:, k : k + 1]).astype(jnp.bfloat16)
        one = lax.dot_general(
            scaled, fin[k], (((0,), (0,)), ((), ())), preferred_element_type=jnp.float32
        )
        total = one if total is None else total + one
    total = total * (1.0 / np.sqrt(float(count)))
    rows = keep.shape[1]
    total = total.reshape(XH, CORE, rows, total.shape[1])
    for h in range(XH):
        to = jnp.bitwise_xor(xh, h)
        keep[to] = jnp.where(c == 0, total[h, 0], total[h, 1])
        give[to] = jnp.where(c == 0, total[h, 1], total[h, 0])


def weight_part(place, fit, fout, fin):
    members, rows = fout.shape[1], fout.shape[2]
    cols = fin.shape[2]
    vmem = pl.BlockSpec(memory_space=pltpu.VMEM)
    hbm = pl.BlockSpec(memory_space=pl.ANY)
    block = jax.ShapeDtypeStruct((XH, rows // (XH * CORE), cols), jnp.float32)
    return pl.pallas_call(
        step_kernel,
        out_shape=(block, block, jax.ShapeDtypeStruct((1, members), jnp.float32)),
        in_specs=[pl.BlockSpec(memory_space=pltpu.SMEM), vmem, hbm, hbm],
        out_specs=(vmem, vmem, vmem),
        scratch_shapes=[
            pltpu.VMEM((Z, members), jnp.float32),
            pltpu.VMEM(fout.shape, fout.dtype),
            pltpu.VMEM(fin.shape, fin.dtype),
            pltpu.SemaphoreType.DMA((Z, 2)),
        ],
        compiler_params=pltpu.CompilerParams(vmem_limit_bytes=LARGE_BYTES),
        cost_estimate=pl.CostEstimate(
            flops=2 * rows * Z * members * cols, bytes_accessed=4 * 1024 * 1024, transcendentals=0
        ),
    )(place, fit, fout, fin)


def share(x, axes):
    return lax.all_to_all(x, axes, 0, 0, tiled=True)


def shards(inputs, weight, factor_in, factor_out, readout):
    members, rows_here, width = inputs.shape
    out_width, block = weight.shape
    half = out_width // 2
    xh, z, c, xl, y = (lax.axis_index(a) for a in AXES)
    wa = xl * Y + y
    sign = 1 - 2 * c
    y_fwd, y_bwd, x_go, core_go = go_y(1), go_y(-1), go_x(), go_core()

    def send(v, pairs):
        return lax.ppermute(v, AXES, pairs)

    def col(xl_at, off):
        return xl_at * Y + lax.rem(y + off + Y, Y)

    xo = 1 - xl
    k_own, k_a, k_b, k_c = col(xl, 0), col(xl, -sign), col(xl, sign), col(xl, 2)
    k_d, k_e, k_f, k_g = col(xo, 0), col(xo, -sign), col(xo, sign), col(xo, 2)

    x_own = inputs.transpose(1, 0, 2)
    def col(xl_at, off):
        return xl_at * Y + lax.rem(y + off + Y, Y)

    xo = 1 - xl
    k_own, k_a, k_b, k_c = col(xl, 0), col(xl, -sign), col(xl, sign), col(xl, 2)
    k_d, k_e, k_f, k_g = col(xo, 0), col(xo, -sign), col(xo, sign), col(xo, 2)

    x_own = inputs.transpose(1, 0, 2)
    w_own = lax.dynamic_slice_in_dim(weight, c * half, half, 0)

    places = jnp.stack([k_own, k_a, k_d, k_b, k_e, k_f, k_c, k_g, c, xh, z]).astype(jnp.int32)

    part = half // CHAINS
    chains = range(CHAINS)
    *own, fin_here = take_blocks(places, weight, factor_in, part)
    w_a = [send(w, y_fwd) for w in own]
    w_d = [send(w, x_go) for w in own]
    x_oth = send(x_own, core_go)

    low_own, pieces_here, fout_mine, fout_theirs, read_mine = low_term(
        places, x_own, factor_in, factor_out, readout[None]
    )
    fin_all = lax.all_gather(fin_here, "z", axis=0)
    pieces = lax.all_to_all(pieces_here, "z", 0, 0, tiled=True)
    low_oth = send(low_own, core_go)
    fout_got = send(fout_theirs, core_go)

    w_b, w_e, w_c, w_f, w_g = ([None] * CHAINS for _ in range(5))
    for h in chains:
        own[h], w_a[h], w_d[h] = after((own[h], w_a[h], w_d[h]), read_mine)
        w_b[h] = send(own[h], y_bwd)
        w_e[h] = send(w_a[h], x_go)
    acc, token = group_matmul(0, places, x_own, x_oth, [own, w_a, w_d], None)
    for h in chains:
        w_a[h], w_b[h], w_e[h] = after((w_a[h], w_b[h], w_e[h]), token)
        w_c[h] = send(w_a[h], y_fwd)
        w_f[h] = send(w_b[h], x_go)
    acc, token = group_matmul(3, places, x_own, x_oth, [w_b, w_e], acc)
    for h in chains:
        w_c[h], w_f[h], w_e[h] = after((w_c[h], w_f[h], w_e[h]), token)
        w_g[h] = send(w_c[h], x_go) if h == 0 else send(w_e[h], y_fwd)
    acc, token, x_last = group_matmul(5, places, x_own, x_oth, [w_f, w_c], acc, ahead=True)
    partial = last_matmul(
        places, w_g, x_last, acc, low_own, low_oth, fout_mine, fout_got, read_mine
    )
    (partial,) = after((partial,), pieces)

    fit = share(sum_and_copy(share(partial, ("core", "xl", "y"))), ("xh", "z"))

    keep, give, util = weight_part(places, fit, pieces, fin_all)
    summed = keep + send(give, core_go)
    weight_step = summed[0] + send(summed[1], go_xh())
    return weight_step, util.reshape(members)


def solution(mesh):
    fine = Mesh(mesh.devices.reshape(SIZES), AXES)
    pop, wa = ("xh", "z", "core"), ("xl", "y")
    placed = (P(pop, wa, None), P(None, wa), P(pop, None), P(pop, None), P())
    return jax.shard_map(
        shards, mesh=fine, in_specs=placed, out_specs=(P(pop, wa), P(pop)), check_vma=False
    )
```

```python
import functools

import jax
import jax.numpy as jnp
import numpy as np
from jax import lax
from jax.experimental import pallas as pl
from jax.experimental.pallas import tpu as pltpu
from jax.sharding import Mesh, PartitionSpec as P

perturb_scale = 0.5
epsilon = 1e-05

XH, Z, CORE, XL, Y = 2, 8, 2, 2, 4
AXES = ("xh", "z", "core", "xl", "y")
SIZES = (XH, Z, CORE, XL, Y)
WA = XL * Y
CHAINS = 2
ROWS_ALL = 24
VMEM_BYTES = 40 * 1024 * 1024
LAST_BYTES = 40 * 1024 * 1024
SMALL_BYTES = 1024 * 1024
LARGE_BYTES = 58 * 1024 * 1024


def permutation(move):
    pairs = []
    for i in range(int(np.prod(SIZES))):
        at = [int(v) for v in np.unravel_index(i, SIZES)]
        to = move(*at)
        pairs.append((i, int(np.ravel_multi_index(to, SIZES))))
    return pairs


def go_y(step):
    def move(xh, z, c, xl, y):
        s = step if c == 0 else -step
        return (xh, z, c, xl, (y + s) % Y)

    return permutation(move)


def go_x():
    def move(xh, z, c, xl, y):
        x = xh * 2 + xl
        if c == 0:
            x = x ^ 1
        else:
            x = (x + 1) % 4 if x % 2 else (x - 1) % 4
        return (x // 2, z, c, x % 2, y)

    return permutation(move)


def go_core():
    return permutation(lambda xh, z, c, xl, y: (xh, z, 1 - c, xl, y))


def go_xh():
    return permutation(lambda xh, z, c, xl, y: (1 - xh, z, c, xl, y))


def nt_dot(a, b):
    return lax.dot_general(a, b, (((1,), (1,)), ((), ())), preferred_element_type=jnp.float32)


def fetch(kidx, base, x_own, x_oth, sent, ws, w_sems, buffers, sems):
    count, part, block = len(sent), sent[0][0].shape[0], sent[0][0].shape[1]
    copies = [[], []]
    for side, x in ((0, x_own), (1, x_oth)):
        for s in range(count):
            cols = pl.ds(pl.multiple_of(kidx[base + s] * block, block), block)
            copies[side].append(
                pltpu.make_async_copy(x.at[:, :, cols], buffers.at[s, side], sems.at[s, side])
            )
            if side == 0:
                for h in range(CHAINS):
                    to = ws.at[s, pl.ds(h * part, part), :]
                    copies[side].append(pltpu.make_async_copy(sent[s][h], to, w_sems.at[s, h]))
    return copies


def fetch_scratch(count, members, width, block):
    return [
        pltpu.VMEM((count, width, block), jnp.bfloat16),
        pltpu.SemaphoreType.DMA((count, CHAINS)),
        pltpu.VMEM((count, 2, 3, members, block), jnp.bfloat16),
        pltpu.SemaphoreType.DMA((count, 2)),
    ]


def pairs(refs):
    return [refs[i : i + CHAINS] for i in range(0, len(refs), CHAINS)]


def group_kernel(base, count, has_acc, ahead, extra, kidx, x_own, x_oth, *refs):
    refs = refs[extra:]
    sent = pairs(refs[: count * CHAINS])
    acc_in = refs[count * CHAINS] if has_acc else None
    if ahead:
        *refs, x_last, ws, w_sems, buffers, sems, last_sems = refs
        refs = (*refs, ws, w_sems, buffers, sems)
    out, token, ws, w_sems, buffers, sems = refs[-6:]
    members, width = out.shape[2], out.shape[3]
    block = ws.shape[2]
    copies = fetch(kidx, base, x_own, x_oth, sent, ws, w_sems, buffers, sems)
    for copy in copies[0]:
        copy.start()
    early = []
    if ahead:
        cols = pl.ds(pl.multiple_of(kidx[base + count] * block, block), block)
        for side, x in ((0, x_own), (1, x_oth)):
            early.append(pltpu.make_async_copy(x.at[:, :, cols], x_last.at[side], last_sems.at[side]))
    token[...] = jnp.zeros_like(token)
    chunk = 512
    for side in range(2):
        for copy in copies[side]:
            copy.wait()
        if side == 0:
            for copy in copies[1] + early:
                copy.start()
        for j in range(0, width, chunk):
            cols = pl.ds(j, chunk)
            total = None
            for s in range(count):
                part = nt_dot(buffers[s, side].reshape(3 * members, block), ws[s, cols, :])
                total = part if total is None else total + part
            total = total.reshape(3, members, chunk)
            if has_acc:
                total = total + acc_in[side, :, :, cols]
            out[side, :, :, cols] = total
    for copy in early:
        copy.wait()


def group_matmul(base, kidx, x_own, x_oth, sent, acc, ahead=False, extra=()):
    count = len(sent)
    members = x_own.shape[1]
    part, block = sent[0][0].shape
    width = part * CHAINS
    smem = pl.BlockSpec(memory_space=pltpu.SMEM)
    vmem = pl.BlockSpec(memory_space=pltpu.VMEM)
    hbm = pl.BlockSpec(memory_space=pl.ANY)
    args = [x_own, x_oth, *extra] + [w for ws in sent for w in ws]
    specs = [smem] + [hbm] * len(args)
    alias = {}
    if acc is not None:
        specs.append(vmem)
        args.append(acc)
        alias = {len(args): 0}
    flops = 2 * 2 * 3 * members * width * block * count
    return pl.pallas_call(
        functools.partial(group_kernel, base, count, acc is not None, ahead, len(extra)),
        out_shape=(
            jax.ShapeDtypeStruct((2, 3, members, width), jnp.float32),
            jax.ShapeDtypeStruct((8, 128), jnp.float32),
        )
        + ((jax.ShapeDtypeStruct((2, 3, members, block), x_own.dtype),) if ahead else ()),
        in_specs=specs,
        out_specs=(vmem,) * (3 if ahead else 2),
        scratch_shapes=fetch_scratch(count, members, width, block)
        + ([pltpu.SemaphoreType.DMA((2,))] if ahead else []),
        input_output_aliases=alias,
        compiler_params=pltpu.CompilerParams(vmem_limit_bytes=VMEM_BYTES),
        cost_estimate=pl.CostEstimate(flops=flops, bytes_accessed=8 * 1024 * 1024, transcendentals=0),
    )(kidx, *args)


def last_kernel(kidx, *refs):
    sent = refs[:CHAINS]
    x, acc, low_own, low_oth, fout_own, fout_oth, readout, out, ws, w_sems = refs[CHAINS:]
    members, width = acc.shape[2], acc.shape[3]
    block = ws.shape[1]
    part_rows = sent[0].shape[0]
    copies = []
    for h in range(CHAINS):
        to = ws.at[pl.ds(h * part_rows, part_rows), :]
        copies.append(pltpu.make_async_copy(sent[h], to, w_sems.at[h]))
        copies[-1].start()
    for copy in copies:
        copy.wait()
    chunk = 256
    ones = jnp.ones((8, 128), jnp.float32)
    for side, low, fout in ((0, low_own, fout_own), (1, low_oth, fout_oth)):
        total = jnp.zeros((members, 128), jnp.float32)
        for j in range(0, width, chunk):
            cols = pl.ds(j, chunk)
            part = nt_dot(x[side].reshape(3 * members, block), ws[cols, :])
            part = part.reshape(3, members, chunk)
            shift = fout[:, cols].astype(jnp.float32)
            summed = None
            for r in range(3):
                pert = part[r] + acc[side, r, :, cols] + low[r] * shift
                term = jnp.tanh(pert)
                summed = term if summed is None else summed + term
            summed = summed * readout[:, cols]
            for h in range(0, chunk, 128):
                total = total + summed[:, h : h + 128]
        row = lax.dot_general(
            ones,
            total,
            (((1,), (1,)), ((), ())),
            preferred_element_type=jnp.float32,
            precision=lax.Precision.HIGHEST,
        )[0:1]
        at = pl.ds(pl.multiple_of(jnp.bitwise_xor(kidx[8], side) * members, members), members)
        for k in range(out.shape[0]):
            out[k, :, at] = row


def last_matmul(kidx, sent, x, acc, low_own, low_oth, fout_own, fout_oth, readout):
    members = x.shape[2]
    part, block = sent[0].shape
    width = part * CHAINS
    smem = pl.BlockSpec(memory_space=pltpu.SMEM)
    vmem = pl.BlockSpec(memory_space=pltpu.VMEM)
    hbm = pl.BlockSpec(memory_space=pl.ANY)
    return pl.pallas_call(
        last_kernel,
        out_shape=jax.ShapeDtypeStruct((CORE * WA, 1, 2 * members), jnp.float32),
        in_specs=[smem] + [hbm] * CHAINS + [vmem] * 7,
        out_specs=vmem,
        scratch_shapes=[
            pltpu.VMEM((width, block), jnp.bfloat16),
            pltpu.SemaphoreType.DMA((CHAINS,)),
        ],
        compiler_params=pltpu.CompilerParams(vmem_limit_bytes=LAST_BYTES),
        cost_estimate=pl.CostEstimate(
            flops=2 * 6 * members * width * block,
            bytes_accessed=6 * 1024 * 1024,
            transcendentals=6 * members * width,
        ),
    )(kidx, *sent, x, acc, low_own, low_oth, fout_own, fout_oth, readout)


def after_kernel(*refs):
    pass


def after(values, *done):
    hbm = pl.BlockSpec(memory_space=pl.ANY)
    count = len(values)
    return pl.pallas_call(
        after_kernel,
        out_shape=tuple(jax.ShapeDtypeStruct(v.shape, v.dtype) for v in values),
        in_specs=[hbm] * (count + len(done)),
        out_specs=(hbm,) * count,
        input_output_aliases={i: i for i in range(count)},
        compiler_params=pltpu.CompilerParams(vmem_limit_bytes=SMALL_BYTES),
    )(*values, *done)


def sum_kernel(got, out):
    out[...] = jnp.broadcast_to(jnp.sum(got[...], axis=0, keepdims=True) / ROWS_ALL, out.shape)


def sum_and_copy(got):
    vmem = pl.BlockSpec(memory_space=pltpu.VMEM)
    return pl.pallas_call(
        sum_kernel,
        out_shape=jax.ShapeDtypeStruct((XH * Z,) + got.shape[1:], jnp.float32),
        in_specs=[vmem],
        out_specs=vmem,
        compiler_params=pltpu.CompilerParams(vmem_limit_bytes=SMALL_BYTES),
    )(got)


def cut_kernel(place, fout_all, readout, pieces, mine, theirs, read, fout, sems):
    half = mine.shape[1]
    first = pltpu.make_async_copy(fout_all, fout, sems.at[0])
    first.start()
    read[...] = readout[:, pl.ds(pl.multiple_of(place[8] * half, half), half)]
    moves = []
    run = pieces.shape[2] // XH
    for h in range(XH):
        for k in range(Z):
            cols = pl.ds(h * half + k * run, run)
            moves.append((fout.at[:, cols], pieces.at[k, :, pl.ds(h * run, run)]))
    for at, to in ((place[8], mine), (1 - place[8], theirs)):
        cols = pl.ds(pl.multiple_of(at * half, half), half)
        moves.append((fout.at[:, cols], to))
    copies = [pltpu.make_async_copy(x, y, sems.at[i + 1]) for i, (x, y) in enumerate(moves)]
    first.wait()
    for copy in copies:
        copy.start()
    for copy in copies:
        copy.wait()


def cut_factors(place, fout, readout):
    members, out_width = fout.shape
    half = out_width // CORE
    hbm = pl.BlockSpec(memory_space=pl.ANY)
    vmem = pl.BlockSpec(memory_space=pltpu.VMEM)
    return pl.pallas_call(
        cut_kernel,
        out_shape=(
            jax.ShapeDtypeStruct((Z, members, out_width // Z), fout.dtype),
            jax.ShapeDtypeStruct((members, half), fout.dtype),
            jax.ShapeDtypeStruct((members, half), fout.dtype),
            jax.ShapeDtypeStruct((1, half), readout.dtype),
        ),
        in_specs=[pl.BlockSpec(memory_space=pltpu.SMEM), hbm, vmem],
        out_specs=(hbm, hbm, hbm, vmem),
        scratch_shapes=[
            pltpu.VMEM(fout.shape, fout.dtype),
            pltpu.SemaphoreType.DMA((3 + XH * Z,)),
        ],
        compiler_params=pltpu.CompilerParams(vmem_limit_bytes=LARGE_BYTES),
        cost_estimate=pl.CostEstimate(flops=0, bytes_accessed=4 * 1024 * 1024, transcendentals=0),
    )(place, fout, readout)


def block_kernel(place, fin, *refs):
    out, sem = refs[-2:]
    block = out.shape[1]
    cols = pl.ds(pl.multiple_of(place[0] * block, block), block)
    copy = pltpu.make_async_copy(fin.at[:, cols], out, sem.at[0])
    copy.start()
    copy.wait()


def cut_block(place, fin, block, *done):
    hbm = pl.BlockSpec(memory_space=pl.ANY)
    return pl.pallas_call(
        block_kernel,
        out_shape=jax.ShapeDtypeStruct((fin.shape[0], block), fin.dtype),
        in_specs=[pl.BlockSpec(memory_space=pltpu.SMEM), hbm] + [hbm] * len(done),
        out_specs=pl.BlockSpec(memory_space=pltpu.VMEM),
        scratch_shapes=[pltpu.SemaphoreType.DMA((1,))],
        compiler_params=pltpu.CompilerParams(vmem_limit_bytes=LARGE_BYTES),
    )(place, fin, *done)


def low_kernel(x, fin, out, x_buf, f_buf, sems):
    tiles, rows, tile, width = x_buf.shape
    copies = []
    for t in range(tiles):
        span = pl.ds(t * tile, tile)
        pair = (
            pltpu.make_async_copy(x.at[:, span, :], x_buf.at[t], sems.at[t, 0]),
            pltpu.make_async_copy(fin.at[span, :], f_buf.at[t], sems.at[t, 1]),
        )
        for copy in pair:
            copy.start()
        copies.append(pair)
    chunk = 128
    for t in range(tiles):
        for copy in copies[t]:
            copy.wait()
        totals = [None] * rows
        for j in range(0, width, chunk):
            cols = pl.ds(j, chunk)
            f = f_buf[t, :, cols].astype(jnp.float32)
            for r in range(rows):
                term = x_buf[t, r, :, cols].astype(jnp.float32) * f
                totals[r] = term if totals[r] is None else totals[r] + term
        for r in range(rows):
            out[r, pl.ds(t * tile, tile), :] = perturb_scale * jnp.sum(totals[r], axis=1, keepdims=True)


def low_term(x, fin):
    rows, members, width = x.shape
    tile = 64
    tiles = members // tile
    hbm = pl.BlockSpec(memory_space=pl.ANY)
    return pl.pallas_call(
        low_kernel,
        out_shape=jax.ShapeDtypeStruct((rows, members, 1), jnp.float32),
        in_specs=[hbm, hbm],
        out_specs=pl.BlockSpec(memory_space=pltpu.VMEM),
        scratch_shapes=[
            pltpu.VMEM((tiles, rows, tile, width), jnp.bfloat16),
            pltpu.VMEM((tiles, tile, width), jnp.bfloat16),
            pltpu.SemaphoreType.DMA((tiles, 2)),
        ],
        compiler_params=pltpu.CompilerParams(vmem_limit_bytes=VMEM_BYTES),
        cost_estimate=pl.CostEstimate(
            flops=2 * rows * members * width, bytes_accessed=9 * 1024 * 1024, transcendentals=0
        ),
    )(x, fin)


def step_kernel(place, fit, fout_all, fin_all, keep, give, util, rows_ref, fout, fin, sems):
    copies = []
    for k in range(Z):
        pair = (
            pltpu.make_async_copy(fout_all.at[k], fout.at[k], sems.at[k, 0]),
            pltpu.make_async_copy(fin_all.at[k], fin.at[k], sems.at[k, 1]),
        )
        for copy in pair:
            copy.start()
        copies.append(pair)
    values = fit[...]
    members = fin.shape[1]
    count = values.shape[0] * values.shape[2]
    mean = jnp.sum(values) / count
    spread = jnp.sum((values - mean) ** 2) / count
    root = jnp.sqrt(jnp.full((1, 1), spread + epsilon, jnp.float32))
    c, xh, z = place[8], place[9], place[10]
    at = pl.ds(pl.multiple_of(c * members, members), members)
    util[...] = (fit[xh * Z + z, :, at] - mean) / root
    for k in range(Z):
        rows_ref[k : k + 1, :] = fit[xh * Z + k, :, at]
    columns = (jnp.transpose(rows_ref[...]) - mean) / root
    total = None
    for k in range(Z):
        for copy in copies[k]:
            copy.wait()
        scaled = (fout[k].astype(jnp.float32) * columns[:, k : k + 1]).astype(jnp.bfloat16)
        one = lax.dot_general(
            scaled, fin[k], (((0,), (0,)), ((), ())), preferred_element_type=jnp.float32
        )
        total = one if total is None else total + one
    total = total * (1.0 / np.sqrt(float(count)))
    rows = keep.shape[1]
    total = total.reshape(XH, CORE, rows, total.shape[1])
    for h in range(XH):
        to = jnp.bitwise_xor(xh, h)
        keep[to] = jnp.where(c == 0, total[h, 0], total[h, 1])
        give[to] = jnp.where(c == 0, total[h, 1], total[h, 0])


def weight_part(place, fit, fout, fin):
    members, rows = fout.shape[1], fout.shape[2]
    cols = fin.shape[2]
    vmem = pl.BlockSpec(memory_space=pltpu.VMEM)
    hbm = pl.BlockSpec(memory_space=pl.ANY)
    block = jax.ShapeDtypeStruct((XH, rows // (XH * CORE), cols), jnp.float32)
    return pl.pallas_call(
        step_kernel,
        out_shape=(block, block, jax.ShapeDtypeStruct((1, members), jnp.float32)),
        in_specs=[pl.BlockSpec(memory_space=pltpu.SMEM), vmem, hbm, hbm],
        out_specs=(vmem, vmem, vmem),
        scratch_shapes=[
            pltpu.VMEM((Z, members), jnp.float32),
            pltpu.VMEM(fout.shape, fout.dtype),
            pltpu.VMEM(fin.shape, fin.dtype),
            pltpu.SemaphoreType.DMA((Z, 2)),
        ],
        compiler_params=pltpu.CompilerParams(vmem_limit_bytes=LARGE_BYTES),
        cost_estimate=pl.CostEstimate(
            flops=2 * rows * Z * members * cols, bytes_accessed=4 * 1024 * 1024, transcendentals=0
        ),
    )(place, fit, fout, fin)


def share(x, axes):
    return lax.all_to_all(x, axes, 0, 0, tiled=True)


def shards(inputs, weight, factor_in, factor_out, readout):
    members, rows_here, width = inputs.shape
    out_width, block = weight.shape
    half = out_width // 2
    xh, z, c, xl, y = (lax.axis_index(a) for a in AXES)
    wa = xl * Y + y
    sign = 1 - 2 * c
    y_fwd, y_bwd, x_go, core_go = go_y(1), go_y(-1), go_x(), go_core()

    def send(v, pairs):
        return lax.ppermute(v, AXES, pairs)

    def col(xl_at, off):
        return xl_at * Y + lax.rem(y + off + Y, Y)

    xo = 1 - xl
    k_own, k_a, k_b, k_c = col(xl, 0), col(xl, -sign), col(xl, sign), col(xl, 2)
    k_d, k_e, k_f, k_g = col(xo, 0), col(xo, -sign), col(xo, sign), col(xo, 2)

    x_own = inputs.transpose(1, 0, 2)
    def col(xl_at, off):
        return xl_at * Y + lax.rem(y + off + Y, Y)

    xo = 1 - xl
    k_own, k_a, k_b, k_c = col(xl, 0), col(xl, -sign), col(xl, sign), col(xl, 2)
    k_d, k_e, k_f, k_g = col(xo, 0), col(xo, -sign), col(xo, sign), col(xo, 2)

    x_own = inputs.transpose(1, 0, 2)
    w_own = lax.dynamic_slice_in_dim(weight, c * half, half, 0)

    places = jnp.stack([k_own, k_a, k_d, k_b, k_e, k_f, k_c, k_g, c, xh, z]).astype(jnp.int32)

    part = half // CHAINS
    chains = range(CHAINS)
    own = [lax.dynamic_slice_in_dim(weight, c * half + h * part, part, 0) for h in chains]
    w_a = [send(w, y_fwd) for w in own]
    w_d = [send(w, x_go) for w in own]
    x_oth = send(x_own, core_go)

    fin_all = lax.all_gather(cut_block(places, factor_in, block), "z", axis=0)
    pieces_here, fout_mine, fout_theirs, read_mine = cut_factors(places, factor_out, readout[None])
    pieces = lax.all_to_all(pieces_here, "z", 0, 0, tiled=True)
    low_own = low_term(x_own, factor_in)
    low_oth = send(low_own, core_go)
    fout_got = send(fout_theirs, core_go)

    w_b, w_e, w_c, w_f, w_g = ([None] * CHAINS for _ in range(5))
    for h in chains:
        own[h], w_a[h], w_d[h] = after((own[h], w_a[h], w_d[h]))
        w_b[h] = send(own[h], y_bwd)
        w_e[h] = send(w_a[h], x_go)
    acc, token = group_matmul(0, places, x_own, x_oth, [own, w_a, w_d], None)
    for h in chains:
        w_a[h], w_b[h], w_e[h] = after((w_a[h], w_b[h], w_e[h]), token)
        w_c[h] = send(w_a[h], y_fwd)
        w_f[h] = send(w_b[h], x_go)
    acc, token = group_matmul(3, places, x_own, x_oth, [w_b, w_e], acc, extra=(low_own,))
    for h in chains:
        w_c[h], w_f[h], w_e[h] = after((w_c[h], w_f[h], w_e[h]), token)
        w_g[h] = send(w_c[h], x_go) if h == 0 else send(w_e[h], y_fwd)
    acc, token, x_last = group_matmul(5, places, x_own, x_oth, [w_f, w_c], acc, ahead=True)
    partial = last_matmul(
        places, w_g, x_last, acc, low_own, low_oth, fout_mine, fout_got, read_mine
    )
    (partial,) = after((partial,), pieces)

    fit = share(sum_and_copy(share(partial, ("core", "xl", "y"))), ("xh", "z"))

    keep, give, util = weight_part(places, fit, pieces, fin_all)
    summed = keep + send(give, core_go)
    weight_step = summed[0] + send(summed[1], go_xh())
    return weight_step, util.reshape(members)


def solution(mesh):
    fine = Mesh(mesh.devices.reshape(SIZES), AXES)
    pop, wa = ("xh", "z", "core"), ("xl", "y")
    placed = (P(pop, wa, None), P(None, wa), P(pop, None), P(pop, None), P())
    return jax.shard_map(
        shards, mesh=fine, in_specs=placed, out_specs=(P(pop, wa), P(pop)), check_vma=False
    )
```

```python
import functools

import jax
import jax.numpy as jnp
import numpy as np
from jax import lax
from jax.experimental import pallas as pl
from jax.experimental.pallas import tpu as pltpu
from jax.sharding import Mesh, PartitionSpec as P

perturb_scale = 0.5
epsilon = 1e-05

XH, Z, CORE, XL, Y = 2, 8, 2, 2, 4
AXES = ("xh", "z", "core", "xl", "y")
SIZES = (XH, Z, CORE, XL, Y)
WA = XL * Y
ROWS_ALL = 24
VMEM_BYTES = 40 * 1024 * 1024
LAST_BYTES = 40 * 1024 * 1024
SMALL_BYTES = 1024 * 1024
LARGE_BYTES = 58 * 1024 * 1024


def permutation(move):
    pairs = []
    for i in range(int(np.prod(SIZES))):
        at = [int(v) for v in np.unravel_index(i, SIZES)]
        to = move(*at)
        pairs.append((i, int(np.ravel_multi_index(to, SIZES))))
    return pairs


def go_y(step):
    def move(xh, z, c, xl, y):
        s = step if c == 0 else -step
        return (xh, z, c, xl, (y + s) % Y)

    return permutation(move)


def go_x():
    def move(xh, z, c, xl, y):
        x = xh * 2 + xl
        if c == 0:
            x = x ^ 1
        else:
            x = (x + 1) % 4 if x % 2 else (x - 1) % 4
        return (x // 2, z, c, x % 2, y)

    return permutation(move)


def go_core():
    return permutation(lambda xh, z, c, xl, y: (xh, z, 1 - c, xl, y))


def go_xh():
    return permutation(lambda xh, z, c, xl, y: (1 - xh, z, c, xl, y))


def nt_dot(a, b):
    return lax.dot_general(a, b, (((1,), (1,)), ((), ())), preferred_element_type=jnp.float32)


def fetch(kidx, base, x_own, x_oth, sent, ws, w_sems, buffers, sems):
    block = ws.shape[2]
    copies = [[], []]
    for side, x in ((0, x_own), (1, x_oth)):
        for s, parts in enumerate(sent):
            cols = pl.ds(pl.multiple_of(kidx[base + s] * block, block), block)
            copies[side].append(
                pltpu.make_async_copy(x.at[:, :, cols], buffers.at[s, side], sems.at[s, side])
            )
            if side == 0:
                rows = parts[0].shape[0]
                for h, part in enumerate(parts):
                    to = ws.at[s, pl.ds(h * rows, rows), :]
                    copies[side].append(pltpu.make_async_copy(part, to, w_sems.at[s, h]))
    return copies


def group_kernel(base, counts, has_acc, ahead, extra, hand, kidx, x_own, x_oth, *refs):
    refs = list(refs[extra:])
    sent = []
    for n in counts:
        sent.append(refs[:n])
        refs = refs[n:]
    acc_in = refs.pop(0) if has_acc else None
    out = refs.pop(0)
    handed = [refs.pop(0) for _ in hand]
    x_last = refs.pop(0) if ahead else None
    ws, w_sems, buffers, sems, more_sems = refs
    members, width = out.shape[2], out.shape[3]
    block = ws.shape[2]
    copies = fetch(kidx, base, x_own, x_oth, sent, ws, w_sems, buffers, sems)
    for copy in copies[0]:
        copy.start()
    early = []
    for i, (s, row) in enumerate(hand):
        source = ws.at[s, pl.ds(row, handed[i].shape[0]), :]
        early.append(pltpu.make_async_copy(source, handed[i], more_sems.at[i]))
    if ahead:
        cols = pl.ds(pl.multiple_of(kidx[base + len(counts)] * block, block), block)
        for side, x in ((0, x_own), (1, x_oth)):
            early.append(pltpu.make_async_copy(x.at[:, :, cols], x_last.at[side], more_sems.at[2 + side]))
    chunk = 512
    for side in range(2):
        for copy in copies[side]:
            copy.wait()
        if side == 0:
            for copy in copies[1] + early:
                copy.start()
        for j in range(0, width, chunk):
            cols = pl.ds(j, chunk)
            total = None
            for s in range(len(counts)):
                part = nt_dot(buffers[s, side].reshape(3 * members, block), ws[s, cols, :])
                total = part if total is None else total + part
            total = total.reshape(3, members, chunk)
            if has_acc:
                total = total + acc_in[side, :, :, cols]
            out[side, :, :, cols] = total
    for copy in early:
        copy.wait()


def group_matmul(base, kidx, x_own, x_oth, sent, acc, ahead=False, extra=(), hand=(), hand_rows=0):
    counts = [len(parts) for parts in sent]
    members = x_own.shape[1]
    block = sent[0][0].shape[1]
    width = sent[0][0].shape[0] * counts[0]
    smem = pl.BlockSpec(memory_space=pltpu.SMEM)
    vmem = pl.BlockSpec(memory_space=pltpu.VMEM)
    hbm = pl.BlockSpec(memory_space=pl.ANY)
    args = [x_own, x_oth, *extra] + [w for ws in sent for w in ws]
    specs = [smem] + [hbm] * len(args)
    alias = {}
    if acc is not None:
        specs.append(vmem)
        args.append(acc)
        alias = {len(args): 0}
    shapes = [jax.ShapeDtypeStruct((2, 3, members, width), jnp.float32)]
    outs = [vmem]
    for _ in hand:
        shapes.append(jax.ShapeDtypeStruct((hand_rows, block), jnp.bfloat16))
        outs.append(hbm)
    if ahead:
        shapes.append(jax.ShapeDtypeStruct((2, 3, members, block), x_own.dtype))
        outs.append(vmem)
    flops = 2 * 2 * 3 * members * width * block * len(counts)
    return pl.pallas_call(
        functools.partial(group_kernel, base, counts, acc is not None, ahead, len(extra), hand),
        out_shape=tuple(shapes),
        in_specs=specs,
        out_specs=tuple(outs),
        scratch_shapes=[
            pltpu.VMEM((len(counts), width, block), jnp.bfloat16),
            pltpu.SemaphoreType.DMA((len(counts), 2)),
            pltpu.VMEM((len(counts), 2, 3, members, block), jnp.bfloat16),
            pltpu.SemaphoreType.DMA((len(counts), 2)),
            pltpu.SemaphoreType.DMA((4,)),
        ],
        input_output_aliases=alias,
        compiler_params=pltpu.CompilerParams(vmem_limit_bytes=VMEM_BYTES),
        cost_estimate=pl.CostEstimate(flops=flops, bytes_accessed=8 * 1024 * 1024, transcendentals=0),
    )(kidx, *args)


def last_kernel(kidx, w_lo, w_hi, fout_mine, fout_theirs, x, acc, low_own, low_oth, readout, out, ws, w_sems, fouts, f_sems):
    members, width = acc.shape[2], acc.shape[3]
    block = ws.shape[1]
    rows = w_lo.shape[0]
    first = pl.multiple_of(kidx[8] * width, width)
    copies = []
    for h, part in enumerate((w_lo, w_hi)):
        copies.append(pltpu.make_async_copy(part, ws.at[pl.ds(h * rows, rows), :], w_sems.at[h]))
    moves = []
    for side, fout in ((0, fout_mine), (1, fout_theirs)):
        moves.append(pltpu.make_async_copy(fout.at[:, pl.ds(first, width)], fouts.at[side], f_sems.at[side]))
    for copy in copies + moves:
        copy.start()
    for copy in copies:
        copy.wait()
    chunk = 256
    ones = jnp.ones((8, 128), jnp.float32)
    for side, low in ((0, low_own), (1, low_oth)):
        moves[side].wait()
        total = jnp.zeros((members, 128), jnp.float32)
        for j in range(0, width, chunk):
            cols = pl.ds(j, chunk)
            part = nt_dot(x[side].reshape(3 * members, block), ws[cols, :])
            part = part.reshape(3, members, chunk)
            shift = fouts[side, :, cols].astype(jnp.float32)
            summed = None
            for r in range(3):
                pert = part[r] + acc[side, r, :, cols] + low[r] * shift
                term = jnp.tanh(pert)
                summed = term if summed is None else summed + term
            summed = summed * readout[:, pl.ds(pl.multiple_of(first + j, chunk), chunk)]
            for h in range(0, chunk, 128):
                total = total + summed[:, h : h + 128]
        row = lax.dot_general(
            ones,
            total,
            (((1,), (1,)), ((), ())),
            preferred_element_type=jnp.float32,
            precision=lax.Precision.HIGHEST,
        )[0:1]
        at = pl.ds(pl.multiple_of(jnp.bitwise_xor(kidx[8], side) * members, members), members)
        for k in range(out.shape[0]):
            out[k, :, at] = row


def last_matmul(kidx, w_lo, w_hi, fout_mine, fout_theirs, x, acc, low_own, low_oth, readout):
    members = x.shape[2]
    block = w_lo.shape[1]
    width = acc.shape[3]
    smem = pl.BlockSpec(memory_space=pltpu.SMEM)
    vmem = pl.BlockSpec(memory_space=pltpu.VMEM)
    hbm = pl.BlockSpec(memory_space=pl.ANY)
    return pl.pallas_call(
        last_kernel,
        out_shape=jax.ShapeDtypeStruct((CORE * WA, 1, 2 * members), jnp.float32),
        in_specs=[smem] + [hbm] * 4 + [vmem] * 5,
        out_specs=vmem,
        scratch_shapes=[
            pltpu.VMEM((width, block), jnp.bfloat16),
            pltpu.SemaphoreType.DMA((2,)),
            pltpu.VMEM((2, members, width), jnp.bfloat16),
            pltpu.SemaphoreType.DMA((2,)),
        ],
        compiler_params=pltpu.CompilerParams(vmem_limit_bytes=LAST_BYTES),
        cost_estimate=pl.CostEstimate(
            flops=2 * 6 * members * width * block,
            bytes_accessed=6 * 1024 * 1024,
            transcendentals=6 * members * width,
        ),
    )(kidx, w_lo, w_hi, fout_mine, fout_theirs, x, acc, low_own, low_oth, readout)


def after_kernel(*refs):
    pass


def after(values, *done):
    hbm = pl.BlockSpec(memory_space=pl.ANY)
    count = len(values)
    return pl.pallas_call(
        after_kernel,
        out_shape=tuple(jax.ShapeDtypeStruct(v.shape, v.dtype) for v in values),
        in_specs=[hbm] * (count + len(done)),
        out_specs=(hbm,) * count,
        input_output_aliases={i: i for i in range(count)},
        compiler_params=pltpu.CompilerParams(vmem_limit_bytes=SMALL_BYTES),
    )(*values, *done)


def sum_kernel(got, out):
    out[...] = jnp.broadcast_to(jnp.sum(got[...], axis=0, keepdims=True) / ROWS_ALL, out.shape)


def sum_and_copy(got):
    vmem = pl.BlockSpec(memory_space=pltpu.VMEM)
    return pl.pallas_call(
        sum_kernel,
        out_shape=jax.ShapeDtypeStruct((XH * Z,) + got.shape[1:], jnp.float32),
        in_specs=[vmem],
        out_specs=vmem,
        compiler_params=pltpu.CompilerParams(vmem_limit_bytes=SMALL_BYTES),
    )(got)


def cut_kernel(fout, pieces, token):
    token[...] = jnp.zeros_like(token)
    half = fout.shape[1] // XH
    run = pieces.shape[1] // XH
    for h in range(XH):
        for k in range(Z):
            cols = pl.ds(h * half + k * run, run)
            pieces[k, pl.ds(h * run, run), :] = jnp.transpose(fout[:, cols])


def cut_factors(fout):
    members, out_width = fout.shape
    vmem = pl.BlockSpec(memory_space=pltpu.VMEM)
    return pl.pallas_call(
        cut_kernel,
        out_shape=(
            jax.ShapeDtypeStruct((Z, out_width // Z, members), fout.dtype),
            jax.ShapeDtypeStruct((8, 128), jnp.float32),
        ),
        in_specs=[vmem],
        out_specs=(vmem, vmem),
        compiler_params=pltpu.CompilerParams(vmem_limit_bytes=LARGE_BYTES),
        cost_estimate=pl.CostEstimate(flops=0, bytes_accessed=4 * 1024 * 1024, transcendentals=0),
    )(fout)


def block_kernel(place, fin, *refs):
    out, sem = refs[-2:]
    block = out.shape[1]
    cols = pl.ds(pl.multiple_of(place[0] * block, block), block)
    copy = pltpu.make_async_copy(fin.at[:, cols], out, sem.at[0])
    copy.start()
    copy.wait()


def cut_block(place, fin, block, *done):
    hbm = pl.BlockSpec(memory_space=pl.ANY)
    return pl.pallas_call(
        block_kernel,
        out_shape=jax.ShapeDtypeStruct((fin.shape[0], block), fin.dtype),
        in_specs=[pl.BlockSpec(memory_space=pltpu.SMEM), hbm] + [hbm] * len(done),
        out_specs=pl.BlockSpec(memory_space=pltpu.VMEM),
        scratch_shapes=[pltpu.SemaphoreType.DMA((1,))],
        compiler_params=pltpu.CompilerParams(vmem_limit_bytes=LARGE_BYTES),
    )(place, fin, *done)


def low_kernel(x, fin, out, token, x_buf, f_buf, sems):
    token[...] = jnp.zeros_like(token)
    tiles, rows, tile, width = x_buf.shape
    copies = []
    for t in range(tiles):
        span = pl.ds(t * tile, tile)
        pair = (
            pltpu.make_async_copy(x.at[:, span, :], x_buf.at[t], sems.at[t, 0]),
            pltpu.make_async_copy(fin.at[span, :], f_buf.at[t], sems.at[t, 1]),
        )
        for copy in pair:
            copy.start()
        copies.append(pair)
    chunk = 128
    for t in range(tiles):
        for copy in copies[t]:
            copy.wait()
        totals = [None] * rows
        for j in range(0, width, chunk):
            cols = pl.ds(j, chunk)
            f = f_buf[t, :, cols].astype(jnp.float32)
            for r in range(rows):
                term = x_buf[t, r, :, cols].astype(jnp.float32) * f
                totals[r] = term if totals[r] is None else totals[r] + term
        for r in range(rows):
            out[r, pl.ds(t * tile, tile), :] = perturb_scale * jnp.sum(totals[r], axis=1, keepdims=True)


def low_term(x, fin):
    rows, members, width = x.shape
    tile = 64
    tiles = members // tile
    hbm = pl.BlockSpec(memory_space=pl.ANY)
    return pl.pallas_call(
        low_kernel,
        out_shape=(
            jax.ShapeDtypeStruct((rows, members, 1), jnp.float32),
            jax.ShapeDtypeStruct((8, 128), jnp.float32),
        ),
        in_specs=[hbm, hbm],
        out_specs=(pl.BlockSpec(memory_space=pltpu.VMEM),) * 2,
        scratch_shapes=[
            pltpu.VMEM((tiles, rows, tile, width), jnp.bfloat16),
            pltpu.VMEM((tiles, tile, width), jnp.bfloat16),
            pltpu.SemaphoreType.DMA((tiles, 2)),
        ],
        compiler_params=pltpu.CompilerParams(vmem_limit_bytes=LARGE_BYTES),
        cost_estimate=pl.CostEstimate(
            flops=2 * rows * members * width, bytes_accessed=9 * 1024 * 1024, transcendentals=0
        ),
    )(x, fin)


def step_kernel(place, fit, fout_all, fin_all, keep, give, util, fout, fin, sems):
    copies = []
    for k in range(Z):
        pair = (
            pltpu.make_async_copy(fout_all.at[k], fout.at[k], sems.at[k, 0]),
            pltpu.make_async_copy(fin_all.at[k], fin.at[k], sems.at[k, 1]),
        )
        for copy in pair:
            copy.start()
        copies.append(pair)
    values = fit[...]
    members = fin.shape[1]
    count = values.shape[0] * values.shape[2]
    mean = jnp.sum(values) / count
    spread = jnp.sum((values - mean) ** 2) / count
    root = jnp.sqrt(jnp.full((1, 1), spread + epsilon, jnp.float32))
    c, xh, z = place[8], place[9], place[10]
    at = pl.ds(pl.multiple_of(c * members, members), members)
    util[...] = (fit[xh * Z + z, :, at] - mean) / root
    total = None
    for k in range(Z):
        for copy in copies[k]:
            copy.wait()
        row = (fit[xh * Z + k, :, at] - mean) / root
        scaled = (fout[k].astype(jnp.float32) * row).astype(jnp.bfloat16)
        one = jnp.dot(scaled, fin[k], preferred_element_type=jnp.float32)
        total = one if total is None else total + one
    total = total * (1.0 / np.sqrt(float(count)))
    rows = keep.shape[1]
    total = total.reshape(XH, CORE, rows, total.shape[1])
    for h in range(XH):
        to = jnp.bitwise_xor(xh, h)
        keep[to] = jnp.where(c == 0, total[h, 0], total[h, 1])
        give[to] = jnp.where(c == 0, total[h, 1], total[h, 0])


def weight_part(place, fit, fout, fin):
    rows, members = fout.shape[1], fout.shape[2]
    cols = fin.shape[2]
    vmem = pl.BlockSpec(memory_space=pltpu.VMEM)
    hbm = pl.BlockSpec(memory_space=pl.ANY)
    block = jax.ShapeDtypeStruct((XH, rows // (XH * CORE), cols), jnp.float32)
    return pl.pallas_call(
        step_kernel,
        out_shape=(block, block, jax.ShapeDtypeStruct((1, members), jnp.float32)),
        in_specs=[pl.BlockSpec(memory_space=pltpu.SMEM), vmem, hbm, hbm],
        out_specs=(vmem, vmem, vmem),
        scratch_shapes=[
            pltpu.VMEM(fout.shape, fout.dtype),
            pltpu.VMEM(fin.shape, fin.dtype),
            pltpu.SemaphoreType.DMA((Z, 2)),
        ],
        compiler_params=pltpu.CompilerParams(vmem_limit_bytes=LARGE_BYTES),
        cost_estimate=pl.CostEstimate(
            flops=2 * rows * Z * members * cols, bytes_accessed=4 * 1024 * 1024, transcendentals=0
        ),
    )(place, fit, fout, fin)


def share(x, axes):
    return lax.all_to_all(x, axes, 0, 0, tiled=True)


def shards(inputs, weight, factor_in, factor_out, readout):
    members, rows_here, width = inputs.shape
    out_width, block = weight.shape
    half = out_width // 2
    xh, z, c, xl, y = (lax.axis_index(a) for a in AXES)
    wa = xl * Y + y
    sign = 1 - 2 * c
    y_fwd, y_bwd, x_go, core_go = go_y(1), go_y(-1), go_x(), go_core()

    def send(v, pairs):
        return lax.ppermute(v, AXES, pairs)

    def col(xl_at, off):
        return xl_at * Y + lax.rem(y + off + Y, Y)

    xo = 1 - xl
    k_own, k_a, k_b, k_c = col(xl, 0), col(xl, -sign), col(xl, sign), col(xl, 2)
    k_d, k_e, k_f, k_g = col(xo, 0), col(xo, -sign), col(xo, sign), col(xo, 2)

    x_own = inputs.transpose(1, 0, 2)
    def col(xl_at, off):
        return xl_at * Y + lax.rem(y + off + Y, Y)

    xo = 1 - xl
    k_own, k_a, k_b, k_c = col(xl, 0), col(xl, -sign), col(xl, sign), col(xl, 2)
    k_d, k_e, k_f, k_g = col(xo, 0), col(xo, -sign), col(xo, sign), col(xo, 2)

    x_own = inputs.transpose(1, 0, 2)
    w_own = lax.dynamic_slice_in_dim(weight, c * half, half, 0)

    places = jnp.stack([k_own, k_a, k_d, k_b, k_e, k_f, k_c, k_g, c, xh, z]).astype(jnp.int32)

    own = lax.dynamic_slice_in_dim(weight, c * half, half, 0)
    w_a = send(own, y_fwd)
    w_d = send(own, x_go)
    x_oth = send(x_own, core_go)
    fout_oth = send(factor_out, core_go)

    fin_all = lax.all_gather(cut_block(places, factor_in, block), "z", axis=0)
    pieces_here, cut_done = cut_factors(factor_out)
    pieces = lax.all_to_all(pieces_here, "z", 0, 0, tiled=True)
    low_own, low_done = low_term(x_own, factor_in)
    low_oth = send(low_own, core_go)

    part = half // 2
    own, w_a, w_d = after((own, w_a, w_d), cut_done, low_done)
    w_b = send(own, y_bwd)
    w_e = send(w_a, x_go)
    acc, a_on = group_matmul(
        0, places, x_own, x_oth, [[own], [w_a], [w_d]], None, hand=((1, 0),), hand_rows=half
    )
    w_c = send(a_on, y_fwd)
    w_b, w_e = after((w_b, w_e), a_on)
    w_f = send(w_b, x_go)
    acc, e_hi = group_matmul(
        3, places, x_own, x_oth, [[w_b], [w_e]], acc, hand=((1, part),), hand_rows=part
    )
    g_lo = send(w_c[:part], x_go)
    g_hi = send(e_hi, y_fwd)
    acc, x_last = group_matmul(5, places, x_own, x_oth, [[w_f], [w_c]], acc, ahead=True)
    partial = last_matmul(
        places, g_lo, g_hi, factor_out, fout_oth, x_last, acc, low_own, low_oth, readout[None]
    )
    (partial,) = after((partial,), pieces)

    fit = share(sum_and_copy(share(partial, ("core", "xl", "y"))), ("xh", "z"))

    keep, give, util = weight_part(places, fit, pieces, fin_all)
    summed = keep + send(give, core_go)
    weight_step = summed[0] + send(summed[1], go_xh())
    return weight_step, util.reshape(members)


def solution(mesh):
    fine = Mesh(mesh.devices.reshape(SIZES), AXES)
    pop, wa = ("xh", "z", "core"), ("xl", "y")
    placed = (P(pop, wa, None), P(None, wa), P(pop, None), P(pop, None), P())
    return jax.shard_map(
        shards, mesh=fine, in_specs=placed, out_specs=(P(pop, wa), P(pop)), check_vma=False
    )
```

```python
import functools

import jax
import jax.numpy as jnp
import numpy as np
from jax import lax
from jax.experimental import pallas as pl
from jax.experimental.pallas import tpu as pltpu
from jax.sharding import Mesh, PartitionSpec as P

perturb_scale = 0.5
epsilon = 1e-05

XH, Z, CORE, XL, Y = 2, 8, 2, 2, 4
AXES = ("xh", "z", "core", "xl", "y")
SIZES = (XH, Z, CORE, XL, Y)
WA = XL * Y
ROWS_ALL = 24
VMEM_BYTES = 40 * 1024 * 1024
LAST_BYTES = 40 * 1024 * 1024
SMALL_BYTES = 1024 * 1024
LARGE_BYTES = 58 * 1024 * 1024


def permutation(move):
    pairs = []
    for i in range(int(np.prod(SIZES))):
        at = [int(v) for v in np.unravel_index(i, SIZES)]
        to = move(*at)
        pairs.append((i, int(np.ravel_multi_index(to, SIZES))))
    return pairs


def go_y(step):
    def move(xh, z, c, xl, y):
        s = step if c == 0 else -step
        return (xh, z, c, xl, (y + s) % Y)

    return permutation(move)


def go_x():
    def move(xh, z, c, xl, y):
        x = xh * 2 + xl
        if c == 0:
            x = x ^ 1
        else:
            x = (x + 1) % 4 if x % 2 else (x - 1) % 4
        return (x // 2, z, c, x % 2, y)

    return permutation(move)


def go_core():
    return permutation(lambda xh, z, c, xl, y: (xh, z, 1 - c, xl, y))


def go_xh():
    return permutation(lambda xh, z, c, xl, y: (1 - xh, z, c, xl, y))


def nt_dot(a, b):
    return lax.dot_general(a, b, (((1,), (1,)), ((), ())), preferred_element_type=jnp.float32)


def fetch(kidx, base, x_own, x_oth, sent, ws, w_sems, buffers, sems):
    block = ws.shape[2]
    copies = [[], []]
    for side, x in ((0, x_own), (1, x_oth)):
        for s, parts in enumerate(sent):
            cols = pl.ds(pl.multiple_of(kidx[base + s] * block, block), block)
            copies[side].append(
                pltpu.make_async_copy(x.at[:, :, cols], buffers.at[s, side], sems.at[s, side])
            )
            if side == 0:
                rows = parts[0].shape[0]
                for h, part in enumerate(parts):
                    to = ws.at[s, pl.ds(h * rows, rows), :]
                    copies[side].append(pltpu.make_async_copy(part, to, w_sems.at[s, h]))
    return copies


def group_kernel(base, counts, has_acc, ahead, extra, hand, kidx, x_own, x_oth, *refs):
    refs = list(refs[extra:])
    sent = []
    for n in counts:
        sent.append(refs[:n])
        refs = refs[n:]
    acc_in = refs.pop(0) if has_acc else None
    out = refs.pop(0)
    handed = [refs.pop(0) for _ in hand]
    x_last = refs.pop(0) if ahead else None
    ws, w_sems, buffers, sems, more_sems = refs
    members, width = out.shape[2], out.shape[3]
    block = ws.shape[2]
    copies = fetch(kidx, base, x_own, x_oth, sent, ws, w_sems, buffers, sems)
    for copy in copies[0]:
        copy.start()
    early = []
    for i, (s, row) in enumerate(hand):
        source = ws.at[s, pl.ds(row, handed[i].shape[0]), :]
        early.append(pltpu.make_async_copy(source, handed[i], more_sems.at[i]))
    if ahead:
        cols = pl.ds(pl.multiple_of(kidx[base + len(counts)] * block, block), block)
        for side, x in ((0, x_own), (1, x_oth)):
            early.append(pltpu.make_async_copy(x.at[:, :, cols], x_last.at[side], more_sems.at[2 + side]))
    chunk = 512
    for side in range(2):
        for copy in copies[side]:
            copy.wait()
        if side == 0:
            for copy in copies[1] + early:
                copy.start()
        for j in range(0, width, chunk):
            cols = pl.ds(j, chunk)
            total = None
            for s in range(len(counts)):
                part = nt_dot(buffers[s, side].reshape(3 * members, block), ws[s, cols, :])
                total = part if total is None else total + part
            total = total.reshape(3, members, chunk)
            if has_acc:
                total = total + acc_in[side, :, :, cols]
            out[side, :, :, cols] = total
    for copy in early:
        copy.wait()


def group_matmul(base, kidx, x_own, x_oth, sent, acc, ahead=False, extra=(), hand=(), hand_rows=0):
    counts = [len(parts) for parts in sent]
    members = x_own.shape[1]
    block = sent[0][0].shape[1]
    width = sent[0][0].shape[0] * counts[0]
    smem = pl.BlockSpec(memory_space=pltpu.SMEM)
    vmem = pl.BlockSpec(memory_space=pltpu.VMEM)
    hbm = pl.BlockSpec(memory_space=pl.ANY)
    args = [x_own, x_oth, *extra] + [w for ws in sent for w in ws]
    specs = [smem] + [hbm] * len(args)
    alias = {}
    if acc is not None:
        specs.append(vmem)
        args.append(acc)
        alias = {len(args): 0}
    shapes = [jax.ShapeDtypeStruct((2, 3, members, width), jnp.float32)]
    outs = [vmem]
    for _ in hand:
        shapes.append(jax.ShapeDtypeStruct((hand_rows, block), jnp.bfloat16))
        outs.append(hbm)
    if ahead:
        shapes.append(jax.ShapeDtypeStruct((2, 3, members, block), x_own.dtype))
        outs.append(vmem)
    flops = 2 * 2 * 3 * members * width * block * len(counts)
    return pl.pallas_call(
        functools.partial(group_kernel, base, counts, acc is not None, ahead, len(extra), hand),
        out_shape=tuple(shapes),
        in_specs=specs,
        out_specs=tuple(outs),
        scratch_shapes=[
            pltpu.VMEM((len(counts), width, block), jnp.bfloat16),
            pltpu.SemaphoreType.DMA((len(counts), 2)),
            pltpu.VMEM((len(counts), 2, 3, members, block), jnp.bfloat16),
            pltpu.SemaphoreType.DMA((len(counts), 2)),
            pltpu.SemaphoreType.DMA((4,)),
        ],
        input_output_aliases=alias,
        compiler_params=pltpu.CompilerParams(vmem_limit_bytes=VMEM_BYTES),
        cost_estimate=pl.CostEstimate(flops=flops, bytes_accessed=8 * 1024 * 1024, transcendentals=0),
    )(kidx, *args)


def last_kernel(kidx, w_lo, w_hi, fout_mine, fout_theirs, x, acc, low_own, low_oth, readout, out, ws, w_sems, fouts, f_sems):
    members, width = acc.shape[2], acc.shape[3]
    block = ws.shape[1]
    rows = w_lo.shape[0]
    first = pl.multiple_of(kidx[8] * width, width)
    copies = []
    for h, part in enumerate((w_lo, w_hi)):
        copies.append(pltpu.make_async_copy(part, ws.at[pl.ds(h * rows, rows), :], w_sems.at[h]))
    moves = []
    for side, fout in ((0, fout_mine), (1, fout_theirs)):
        moves.append(pltpu.make_async_copy(fout.at[:, pl.ds(first, width)], fouts.at[side], f_sems.at[side]))
    for copy in copies + moves:
        copy.start()
    for copy in copies:
        copy.wait()
    chunk = 256
    ones = jnp.ones((8, 128), jnp.float32)
    for side, low in ((0, low_own), (1, low_oth)):
        moves[side].wait()
        total = jnp.zeros((members, 128), jnp.float32)
        for j in range(0, width, chunk):
            cols = pl.ds(j, chunk)
            part = nt_dot(x[side].reshape(3 * members, block), ws[cols, :])
            part = part.reshape(3, members, chunk)
            shift = fouts[side, :, cols].astype(jnp.float32)
            summed = None
            for r in range(3):
                pert = part[r] + acc[side, r, :, cols] + low[r] * shift
                term = jnp.tanh(pert)
                summed = term if summed is None else summed + term
            summed = summed * readout[:, pl.ds(pl.multiple_of(first + j, chunk), chunk)]
            for h in range(0, chunk, 128):
                total = total + summed[:, h : h + 128]
        row = lax.dot_general(
            ones,
            total,
            (((1,), (1,)), ((), ())),
            preferred_element_type=jnp.float32,
            precision=lax.Precision.HIGHEST,
        )[0:1]
        at = pl.ds(pl.multiple_of(jnp.bitwise_xor(kidx[8], side) * members, members), members)
        for k in range(out.shape[0]):
            out[k, :, at] = row


def last_matmul(kidx, w_lo, w_hi, fout_mine, fout_theirs, x, acc, low_own, low_oth, readout):
    members = x.shape[2]
    block = w_lo.shape[1]
    width = acc.shape[3]
    smem = pl.BlockSpec(memory_space=pltpu.SMEM)
    vmem = pl.BlockSpec(memory_space=pltpu.VMEM)
    hbm = pl.BlockSpec(memory_space=pl.ANY)
    return pl.pallas_call(
        last_kernel,
        out_shape=jax.ShapeDtypeStruct((CORE * WA, 1, 2 * members), jnp.float32),
        in_specs=[smem] + [hbm] * 4 + [vmem] * 5,
        out_specs=vmem,
        scratch_shapes=[
            pltpu.VMEM((width, block), jnp.bfloat16),
            pltpu.SemaphoreType.DMA((2,)),
            pltpu.VMEM((2, members, width), jnp.bfloat16),
            pltpu.SemaphoreType.DMA((2,)),
        ],
        compiler_params=pltpu.CompilerParams(vmem_limit_bytes=LAST_BYTES),
        cost_estimate=pl.CostEstimate(
            flops=2 * 6 * members * width * block,
            bytes_accessed=6 * 1024 * 1024,
            transcendentals=6 * members * width,
        ),
    )(kidx, w_lo, w_hi, fout_mine, fout_theirs, x, acc, low_own, low_oth, readout)


def after_kernel(*refs):
    pass


def after(values, *done):
    hbm = pl.BlockSpec(memory_space=pl.ANY)
    count = len(values)
    return pl.pallas_call(
        after_kernel,
        out_shape=tuple(jax.ShapeDtypeStruct(v.shape, v.dtype) for v in values),
        in_specs=[hbm] * (count + len(done)),
        out_specs=(hbm,) * count,
        input_output_aliases={i: i for i in range(count)},
        compiler_params=pltpu.CompilerParams(vmem_limit_bytes=SMALL_BYTES),
    )(*values, *done)


def sum_kernel(got, out):
    out[...] = jnp.broadcast_to(jnp.sum(got[...], axis=0, keepdims=True) / ROWS_ALL, out.shape)


def sum_and_copy(got):
    vmem = pl.BlockSpec(memory_space=pltpu.VMEM)
    return pl.pallas_call(
        sum_kernel,
        out_shape=jax.ShapeDtypeStruct((XH * Z,) + got.shape[1:], jnp.float32),
        in_specs=[vmem],
        out_specs=vmem,
        compiler_params=pltpu.CompilerParams(vmem_limit_bytes=SMALL_BYTES),
    )(got)


def cut_kernel(fout, pieces, token):
    token[...] = jnp.zeros_like(token)
    half = fout.shape[1] // XH
    run = pieces.shape[1] // XH
    for h in range(XH):
        for k in range(Z):
            cols = pl.ds(h * half + k * run, run)
            pieces[k, pl.ds(h * run, run), :] = jnp.transpose(fout[:, cols])


def cut_factors(fout):
    members, out_width = fout.shape
    vmem = pl.BlockSpec(memory_space=pltpu.VMEM)
    return pl.pallas_call(
        cut_kernel,
        out_shape=(
            jax.ShapeDtypeStruct((Z, out_width // Z, members), fout.dtype),
            jax.ShapeDtypeStruct((8, 128), jnp.float32),
        ),
        in_specs=[vmem],
        out_specs=(vmem, vmem),
        compiler_params=pltpu.CompilerParams(vmem_limit_bytes=LARGE_BYTES),
        cost_estimate=pl.CostEstimate(flops=0, bytes_accessed=4 * 1024 * 1024, transcendentals=0),
    )(fout)


def block_kernel(place, fin, *refs):
    out, sem = refs[-2:]
    block = out.shape[1]
    cols = pl.ds(pl.multiple_of(place[0] * block, block), block)
    copy = pltpu.make_async_copy(fin.at[:, cols], out, sem.at[0])
    copy.start()
    copy.wait()


def cut_block(place, fin, block, *done):
    hbm = pl.BlockSpec(memory_space=pl.ANY)
    return pl.pallas_call(
        block_kernel,
        out_shape=jax.ShapeDtypeStruct((fin.shape[0], block), fin.dtype),
        in_specs=[pl.BlockSpec(memory_space=pltpu.SMEM), hbm] + [hbm] * len(done),
        out_specs=pl.BlockSpec(memory_space=pltpu.VMEM),
        scratch_shapes=[pltpu.SemaphoreType.DMA((1,))],
        compiler_params=pltpu.CompilerParams(vmem_limit_bytes=LARGE_BYTES),
    )(place, fin, *done)


def low_kernel(x, fin, out, token, x_buf, f_buf, sems):
    token[...] = jnp.zeros_like(token)
    tiles, rows, tile, width = x_buf.shape
    copies = []
    for t in range(tiles):
        span = pl.ds(t * tile, tile)
        pair = (
            pltpu.make_async_copy(x.at[:, span, :], x_buf.at[t], sems.at[t, 0]),
            pltpu.make_async_copy(fin.at[span, :], f_buf.at[t], sems.at[t, 1]),
        )
        for copy in pair:
            copy.start()
        copies.append(pair)
    chunk = 128
    for t in range(tiles):
        for copy in copies[t]:
            copy.wait()
        totals = [None] * rows
        for j in range(0, width, chunk):
            cols = pl.ds(j, chunk)
            f = f_buf[t, :, cols].astype(jnp.float32)
            for r in range(rows):
                term = x_buf[t, r, :, cols].astype(jnp.float32) * f
                totals[r] = term if totals[r] is None else totals[r] + term
        for r in range(rows):
            out[r, pl.ds(t * tile, tile), :] = perturb_scale * jnp.sum(totals[r], axis=1, keepdims=True)


def low_term(x, fin):
    rows, members, width = x.shape
    tile = 64
    tiles = members // tile
    hbm = pl.BlockSpec(memory_space=pl.ANY)
    return pl.pallas_call(
        low_kernel,
        out_shape=(
            jax.ShapeDtypeStruct((rows, members, 1), jnp.float32),
            jax.ShapeDtypeStruct((8, 128), jnp.float32),
        ),
        in_specs=[hbm, hbm],
        out_specs=(pl.BlockSpec(memory_space=pltpu.VMEM),) * 2,
        scratch_shapes=[
            pltpu.VMEM((tiles, rows, tile, width), jnp.bfloat16),
            pltpu.VMEM((tiles, tile, width), jnp.bfloat16),
            pltpu.SemaphoreType.DMA((tiles, 2)),
        ],
        compiler_params=pltpu.CompilerParams(vmem_limit_bytes=VMEM_BYTES),
        cost_estimate=pl.CostEstimate(
            flops=2 * rows * members * width, bytes_accessed=9 * 1024 * 1024, transcendentals=0
        ),
    )(x, fin)


def step_kernel(place, fit, fout_all, fin_all, keep, give, util, fout, fin, sems):
    copies = []
    for k in range(Z):
        pair = (
            pltpu.make_async_copy(fout_all.at[k], fout.at[k], sems.at[k, 0]),
            pltpu.make_async_copy(fin_all.at[k], fin.at[k], sems.at[k, 1]),
        )
        for copy in pair:
            copy.start()
        copies.append(pair)
    values = fit[...]
    members = fin.shape[1]
    count = values.shape[0] * values.shape[2]
    mean = jnp.sum(values) / count
    spread = jnp.sum((values - mean) ** 2) / count
    root = jnp.sqrt(jnp.full((1, 1), spread + epsilon, jnp.float32))
    c, xh, z = place[8], place[9], place[10]
    at = pl.ds(pl.multiple_of(c * members, members), members)
    util[...] = (fit[xh * Z + z, :, at] - mean) / root
    total = None
    for k in range(Z):
        for copy in copies[k]:
            copy.wait()
        row = (fit[xh * Z + k, :, at] - mean) / root
        scaled = (fout[k].astype(jnp.float32) * row).astype(jnp.bfloat16)
        one = jnp.dot(scaled, fin[k], preferred_element_type=jnp.float32)
        total = one if total is None else total + one
    total = total * (1.0 / np.sqrt(float(count)))
    rows = keep.shape[1]
    total = total.reshape(XH, CORE, rows, total.shape[1])
    for h in range(XH):
        to = jnp.bitwise_xor(xh, h)
        keep[to] = jnp.where(c == 0, total[h, 0], total[h, 1])
        give[to] = jnp.where(c == 0, total[h, 1], total[h, 0])


def weight_part(place, fit, fout, fin):
    rows, members = fout.shape[1], fout.shape[2]
    cols = fin.shape[2]
    vmem = pl.BlockSpec(memory_space=pltpu.VMEM)
    hbm = pl.BlockSpec(memory_space=pl.ANY)
    block = jax.ShapeDtypeStruct((XH, rows // (XH * CORE), cols), jnp.float32)
    return pl.pallas_call(
        step_kernel,
        out_shape=(block, block, jax.ShapeDtypeStruct((1, members), jnp.float32)),
        in_specs=[pl.BlockSpec(memory_space=pltpu.SMEM), vmem, hbm, hbm],
        out_specs=(vmem, vmem, vmem),
        scratch_shapes=[
            pltpu.VMEM(fout.shape, fout.dtype),
            pltpu.VMEM(fin.shape, fin.dtype),
            pltpu.SemaphoreType.DMA((Z, 2)),
        ],
        compiler_params=pltpu.CompilerParams(vmem_limit_bytes=LARGE_BYTES),
        cost_estimate=pl.CostEstimate(
            flops=2 * rows * Z * members * cols, bytes_accessed=4 * 1024 * 1024, transcendentals=0
        ),
    )(place, fit, fout, fin)


def share(x, axes):
    return lax.all_to_all(x, axes, 0, 0, tiled=True)


def shards(inputs, weight, factor_in, factor_out, readout):
    members, rows_here, width = inputs.shape
    out_width, block = weight.shape
    half = out_width // 2
    xh, z, c, xl, y = (lax.axis_index(a) for a in AXES)
    wa = xl * Y + y
    sign = 1 - 2 * c
    y_fwd, y_bwd, x_go, core_go = go_y(1), go_y(-1), go_x(), go_core()

    def send(v, pairs):
        return lax.ppermute(v, AXES, pairs)

    def col(xl_at, off):
        return xl_at * Y + lax.rem(y + off + Y, Y)

    xo = 1 - xl
    k_own, k_a, k_b, k_c = col(xl, 0), col(xl, -sign), col(xl, sign), col(xl, 2)
    k_d, k_e, k_f, k_g = col(xo, 0), col(xo, -sign), col(xo, sign), col(xo, 2)

    x_own = inputs.transpose(1, 0, 2)
    def col(xl_at, off):
        return xl_at * Y + lax.rem(y + off + Y, Y)

    xo = 1 - xl
    k_own, k_a, k_b, k_c = col(xl, 0), col(xl, -sign), col(xl, sign), col(xl, 2)
    k_d, k_e, k_f, k_g = col(xo, 0), col(xo, -sign), col(xo, sign), col(xo, 2)

    x_own = inputs.transpose(1, 0, 2)
    w_own = lax.dynamic_slice_in_dim(weight, c * half, half, 0)

    places = jnp.stack([k_own, k_a, k_d, k_b, k_e, k_f, k_c, k_g, c, xh, z]).astype(jnp.int32)

    part = half // 2
    own = lax.dynamic_slice_in_dim(weight, c * half, half, 0)
    own_parts = [lax.dynamic_slice_in_dim(weight, c * half + h * part, part, 0) for h in range(2)]
    w_a = [send(w, y_fwd) for w in own_parts]
    w_d = [send(w, x_go) for w in own_parts]
    x_oth = send(x_own, core_go)
    fout_oth = send(factor_out, core_go)

    fin_all = lax.all_gather(cut_block(places, factor_in, block, own_parts[0]), "z", axis=0)
    pieces_here, cut_done = cut_factors(factor_out)
    pieces = lax.all_to_all(pieces_here, "z", 0, 0, tiled=True)
    low_own, low_done = low_term(x_own, factor_in)
    low_oth = send(low_own, core_go)

    w_a[0], w_d[0] = after((w_a[0], w_d[0]))
    e_lo = send(w_a[0], x_go)
    w_a[1], w_d[1], own = after((w_a[1], w_d[1], own), cut_done)
    w_b = send(own, y_bwd)
    e_hi = send(w_a[1], x_go)
    acc, a_on = group_matmul(
        0, places, x_own, x_oth, [[own], w_a, w_d], None, hand=((1, 0),), hand_rows=half
    )
    w_c = send(a_on, y_fwd)
    w_b, e_lo, e_hi = after((w_b, e_lo, e_hi), a_on)
    w_f = send(w_b, x_go)
    acc, e_on = group_matmul(
        3, places, x_own, x_oth, [[w_b], [e_lo, e_hi]], acc, extra=(low_done,), hand=((1, part),), hand_rows=part
    )
    g_lo = send(w_c[:part], x_go)
    g_hi = send(e_on, y_fwd)
    acc, x_last = group_matmul(5, places, x_own, x_oth, [[w_f], [w_c]], acc, ahead=True)
    partial = last_matmul(
        places, g_lo, g_hi, factor_out, fout_oth, x_last, acc, low_own, low_oth, readout[None]
    )
    (partial,) = after((partial,), pieces)

    fit = share(sum_and_copy(share(partial, ("core", "xl", "y"))), ("xh", "z"))

    keep, give, util = weight_part(places, fit, pieces, fin_all)
    summed = keep + send(give, core_go)
    weight_step = summed[0] + send(summed[1], go_xh())
    return weight_step, util.reshape(members)


def solution(mesh):
    fine = Mesh(mesh.devices.reshape(SIZES), AXES)
    pop, wa = ("xh", "z", "core"), ("xl", "y")
    placed = (P(pop, wa, None), P(None, wa), P(pop, None), P(pop, None), P())
    return jax.shard_map(
        shards, mesh=fine, in_specs=placed, out_specs=(P(pop, wa), P(pop)), check_vma=False
    )
```

```python
import functools

import jax
import jax.numpy as jnp
import numpy as np
from jax import lax
from jax.experimental import pallas as pl
from jax.experimental.pallas import tpu as pltpu
from jax.sharding import Mesh, PartitionSpec as P

perturb_scale = 0.5
epsilon = 1e-05

XH, Z, CORE, XL, Y = 2, 8, 2, 2, 4
AXES = ("xh", "z", "core", "xl", "y")
SIZES = (XH, Z, CORE, XL, Y)
WA = XL * Y
CHAINS = 2
ROWS_ALL = 24
VMEM_BYTES = 42 * 1024 * 1024
LAST_BYTES = 42 * 1024 * 1024
SMALL_BYTES = 1024 * 1024
LARGE_BYTES = 58 * 1024 * 1024


def permutation(move):
    pairs = []
    for i in range(int(np.prod(SIZES))):
        at = [int(v) for v in np.unravel_index(i, SIZES)]
        to = move(*at)
        pairs.append((i, int(np.ravel_multi_index(to, SIZES))))
    return pairs


def go_y(step):
    def move(xh, z, c, xl, y):
        s = step if c == 0 else -step
        return (xh, z, c, xl, (y + s) % Y)

    return permutation(move)


def go_x():
    def move(xh, z, c, xl, y):
        x = xh * 2 + xl
        if c == 0:
            x = x ^ 1
        else:
            x = (x + 1) % 4 if x % 2 else (x - 1) % 4
        return (x // 2, z, c, x % 2, y)

    return permutation(move)


def go_core():
    return permutation(lambda xh, z, c, xl, y: (xh, z, 1 - c, xl, y))


def go_xh():
    return permutation(lambda xh, z, c, xl, y: (1 - xh, z, c, xl, y))


def nt_dot(a, b):
    return lax.dot_general(a, b, (((1,), (1,)), ((), ())), preferred_element_type=jnp.float32)


def fetch(kidx, base, x_own, x_oth, sent, ws, w_sems, buffers, sems):
    count, part, block = len(sent), sent[0][0].shape[0], sent[0][0].shape[1]
    copies = [[], []]
    for side, x in ((0, x_own), (1, x_oth)):
        for s in range(count):
            cols = pl.ds(pl.multiple_of(kidx[base + s] * block, block), block)
            copies[side].append(
                pltpu.make_async_copy(x.at[:, :, cols], buffers.at[s, side], sems.at[s, side])
            )
            if side == 0:
                for h in range(CHAINS):
                    to = ws.at[s, pl.ds(h * part, part), :]
                    copies[side].append(pltpu.make_async_copy(sent[s][h], to, w_sems.at[s, h]))
    return copies


def fetch_scratch(count, members, width, block):
    return [
        pltpu.VMEM((count, width, block), jnp.bfloat16),
        pltpu.SemaphoreType.DMA((count, CHAINS)),
        pltpu.VMEM((count, 2, 3, members, block), jnp.bfloat16),
        pltpu.SemaphoreType.DMA((count, 2)),
    ]


def pairs(refs):
    return [refs[i : i + CHAINS] for i in range(0, len(refs), CHAINS)]


def group_kernel(base, count, has_acc, ahead, extra, kidx, x_own, x_oth, *refs):
    refs = refs[extra:]
    sent = pairs(refs[: count * CHAINS])
    acc_in = refs[count * CHAINS] if has_acc else None
    if ahead:
        *refs, x_last, ws, w_sems, buffers, sems, last_sems = refs
        refs = (*refs, ws, w_sems, buffers, sems)
    out, token, ws, w_sems, buffers, sems = refs[-6:]
    members, width = out.shape[2], out.shape[3]
    block = ws.shape[2]
    copies = fetch(kidx, base, x_own, x_oth, sent, ws, w_sems, buffers, sems)
    for copy in copies[0]:
        copy.start()
    early = []
    if ahead:
        cols = pl.ds(pl.multiple_of(kidx[base + count] * block, block), block)
        for side, x in ((0, x_own), (1, x_oth)):
            early.append(pltpu.make_async_copy(x.at[:, :, cols], x_last.at[side], last_sems.at[side]))
    token[...] = jnp.zeros_like(token)
    chunk = 512
    for side in range(2):
        for copy in copies[side]:
            copy.wait()
        if side == 0:
            for copy in copies[1] + early:
                copy.start()
        for j in range(0, width, chunk):
            cols = pl.ds(j, chunk)
            total = None
            for s in range(count):
                part = nt_dot(buffers[s, side].reshape(3 * members, block), ws[s, cols, :])
                total = part if total is None else total + part
            total = total.reshape(3, members, chunk)
            if has_acc:
                total = total + acc_in[side, :, :, cols]
            out[side, :, :, cols] = total
    for copy in early:
        copy.wait()


def group_matmul(base, kidx, x_own, x_oth, sent, acc, ahead=False, extra=()):
    count = len(sent)
    members = x_own.shape[1]
    part, block = sent[0][0].shape
    width = part * CHAINS
    smem = pl.BlockSpec(memory_space=pltpu.SMEM)
    vmem = pl.BlockSpec(memory_space=pltpu.VMEM)
    hbm = pl.BlockSpec(memory_space=pl.ANY)
    args = [x_own, x_oth, *extra] + [w for ws in sent for w in ws]
    specs = [smem] + [hbm] * len(args)
    alias = {}
    if acc is not None:
        specs.append(vmem)
        args.append(acc)
        alias = {len(args): 0}
    flops = 2 * 2 * 3 * members * width * block * count
    return pl.pallas_call(
        functools.partial(group_kernel, base, count, acc is not None, ahead, len(extra)),
        out_shape=(
            jax.ShapeDtypeStruct((2, 3, members, width), jnp.float32),
            jax.ShapeDtypeStruct((8, 128), jnp.float32),
        )
        + ((jax.ShapeDtypeStruct((2, 3, members, block), x_own.dtype),) if ahead else ()),
        in_specs=specs,
        out_specs=(vmem,) * (3 if ahead else 2),
        scratch_shapes=fetch_scratch(count, members, width, block)
        + ([pltpu.SemaphoreType.DMA((2,))] if ahead else []),
        input_output_aliases=alias,
        compiler_params=pltpu.CompilerParams(vmem_limit_bytes=VMEM_BYTES),
        cost_estimate=pl.CostEstimate(flops=flops, bytes_accessed=8 * 1024 * 1024, transcendentals=0),
    )(kidx, *args)


def last_kernel(kidx, w_lo, w_hi, fout_mine, fout_theirs, x, acc, low_own, low_oth, readout, out, ws, w_sems, fouts, f_sems):
    members, width = acc.shape[2], acc.shape[3]
    block = ws.shape[1]
    rows = w_lo.shape[0]
    first = pl.multiple_of(kidx[8] * width, width)
    copies = []
    for h, part in enumerate((w_lo, w_hi)):
        copies.append(pltpu.make_async_copy(part, ws.at[pl.ds(h * rows, rows), :], w_sems.at[h]))
    moves = []
    for side, fout in ((0, fout_mine), (1, fout_theirs)):
        moves.append(pltpu.make_async_copy(fout.at[:, pl.ds(first, width)], fouts.at[side], f_sems.at[side]))
    for copy in copies + moves:
        copy.start()
    for copy in copies:
        copy.wait()
    chunk = 256
    ones = jnp.ones((8, 128), jnp.float32)
    for side, low in ((0, low_own), (1, low_oth)):
        moves[side].wait()
        total = jnp.zeros((members, 128), jnp.float32)
        for j in range(0, width, chunk):
            cols = pl.ds(j, chunk)
            part = nt_dot(x[side].reshape(3 * members, block), ws[cols, :])
            part = part.reshape(3, members, chunk)
            shift = fouts[side, :, cols].astype(jnp.float32)
            summed = None
            for r in range(3):
                pert = part[r] + acc[side, r, :, cols] + low[r] * shift
                term = jnp.tanh(pert)
                summed = term if summed is None else summed + term
            summed = summed * readout[:, pl.ds(pl.multiple_of(first + j, chunk), chunk)]
            for h in range(0, chunk, 128):
                total = total + summed[:, h : h + 128]
        row = lax.dot_general(
            ones,
            total,
            (((1,), (1,)), ((), ())),
            preferred_element_type=jnp.float32,
            precision=lax.Precision.HIGHEST,
        )[0:1]
        at = pl.ds(pl.multiple_of(jnp.bitwise_xor(kidx[8], side) * members, members), members)
        for k in range(out.shape[0]):
            out[k, :, at] = row


def last_matmul(kidx, w_lo, w_hi, fout_mine, fout_theirs, x, acc, low_own, low_oth, readout):
    members = x.shape[2]
    block = w_lo.shape[1]
    width = acc.shape[3]
    smem = pl.BlockSpec(memory_space=pltpu.SMEM)
    vmem = pl.BlockSpec(memory_space=pltpu.VMEM)
    hbm = pl.BlockSpec(memory_space=pl.ANY)
    return pl.pallas_call(
        last_kernel,
        out_shape=jax.ShapeDtypeStruct((CORE * WA, 1, 2 * members), jnp.float32),
        in_specs=[smem] + [hbm] * 4 + [vmem] * 5,
        out_specs=vmem,
        scratch_shapes=[
            pltpu.VMEM((width, block), jnp.bfloat16),
            pltpu.SemaphoreType.DMA((2,)),
            pltpu.VMEM((2, members, width), jnp.bfloat16),
            pltpu.SemaphoreType.DMA((2,)),
        ],
        compiler_params=pltpu.CompilerParams(vmem_limit_bytes=LAST_BYTES),
        cost_estimate=pl.CostEstimate(
            flops=2 * 6 * members * width * block,
            bytes_accessed=6 * 1024 * 1024,
            transcendentals=6 * members * width,
        ),
    )(kidx, w_lo, w_hi, fout_mine, fout_theirs, x, acc, low_own, low_oth, readout)


def after_kernel(*refs):
    pass


def after(values, *done):
    hbm = pl.BlockSpec(memory_space=pl.ANY)
    count = len(values)
    return pl.pallas_call(
        after_kernel,
        out_shape=tuple(jax.ShapeDtypeStruct(v.shape, v.dtype) for v in values),
        in_specs=[hbm] * (count + len(done)),
        out_specs=(hbm,) * count,
        input_output_aliases={i: i for i in range(count)},
        compiler_params=pltpu.CompilerParams(vmem_limit_bytes=SMALL_BYTES),
    )(*values, *done)


def sum_kernel(got, out):
    out[...] = jnp.broadcast_to(jnp.sum(got[...], axis=0, keepdims=True) / ROWS_ALL, out.shape)


def sum_and_copy(got):
    vmem = pl.BlockSpec(memory_space=pltpu.VMEM)
    return pl.pallas_call(
        sum_kernel,
        out_shape=jax.ShapeDtypeStruct((XH * Z,) + got.shape[1:], jnp.float32),
        in_specs=[vmem],
        out_specs=vmem,
        compiler_params=pltpu.CompilerParams(vmem_limit_bytes=SMALL_BYTES),
    )(got)


def cut_kernel(fout, pieces, token):
    token[...] = jnp.zeros_like(token)
    half = fout.shape[1] // XH
    run = pieces.shape[1] // XH
    for h in range(XH):
        for k in range(Z):
            cols = pl.ds(h * half + k * run, run)
            pieces[k, pl.ds(h * run, run), :] = jnp.transpose(fout[:, cols])


def cut_factors(fout):
    members, out_width = fout.shape
    vmem = pl.BlockSpec(memory_space=pltpu.VMEM)
    return pl.pallas_call(
        cut_kernel,
        out_shape=(
            jax.ShapeDtypeStruct((Z, out_width // Z, members), fout.dtype),
            jax.ShapeDtypeStruct((8, 128), jnp.float32),
        ),
        in_specs=[vmem],
        out_specs=(vmem, vmem),
        compiler_params=pltpu.CompilerParams(vmem_limit_bytes=LARGE_BYTES),
        cost_estimate=pl.CostEstimate(flops=0, bytes_accessed=4 * 1024 * 1024, transcendentals=0),
    )(fout)


def low_kernel(x, fin, out, x_buf, f_buf, sems):
    tiles, rows, tile, width = x_buf.shape
    copies = []
    for t in range(tiles):
        span = pl.ds(t * tile, tile)
        pair = (
            pltpu.make_async_copy(x.at[:, span, :], x_buf.at[t], sems.at[t, 0]),
            pltpu.make_async_copy(fin.at[span, :], f_buf.at[t], sems.at[t, 1]),
        )
        for copy in pair:
            copy.start()
        copies.append(pair)
    chunk = 128
    for t in range(tiles):
        for copy in copies[t]:
            copy.wait()
        totals = [None] * rows
        for j in range(0, width, chunk):
            cols = pl.ds(j, chunk)
            f = f_buf[t, :, cols].astype(jnp.float32)
            for r in range(rows):
                term = x_buf[t, r, :, cols].astype(jnp.float32) * f
                totals[r] = term if totals[r] is None else totals[r] + term
        for r in range(rows):
            out[r, pl.ds(t * tile, tile), :] = perturb_scale * jnp.sum(totals[r], axis=1, keepdims=True)


def low_term(x, fin):
    rows, members, width = x.shape
    tile = 64
    tiles = members // tile
    hbm = pl.BlockSpec(memory_space=pl.ANY)
    return pl.pallas_call(
        low_kernel,
        out_shape=jax.ShapeDtypeStruct((rows, members, 1), jnp.float32),
        in_specs=[hbm, hbm],
        out_specs=pl.BlockSpec(memory_space=pltpu.VMEM),
        scratch_shapes=[
            pltpu.VMEM((tiles, rows, tile, width), jnp.bfloat16),
            pltpu.VMEM((tiles, tile, width), jnp.bfloat16),
            pltpu.SemaphoreType.DMA((tiles, 2)),
        ],
        compiler_params=pltpu.CompilerParams(vmem_limit_bytes=VMEM_BYTES),
        cost_estimate=pl.CostEstimate(
            flops=2 * rows * members * width, bytes_accessed=9 * 1024 * 1024, transcendentals=0
        ),
    )(x, fin)


def step_kernel(place, fit, fout_all, fin_all, keep, give, util, fout, fin, sems):
    copies = []
    for k in range(Z):
        pair = (
            pltpu.make_async_copy(fout_all.at[k], fout.at[k], sems.at[k, 0]),
            pltpu.make_async_copy(fin_all.at[k], fin.at[k], sems.at[k, 1]),
        )
        for copy in pair:
            copy.start()
        copies.append(pair)
    values = fit[...]
    members = fin.shape[1]
    count = values.shape[0] * values.shape[2]
    mean = jnp.sum(values) / count
    spread = jnp.sum((values - mean) ** 2) / count
    root = jnp.sqrt(jnp.full((1, 1), spread + epsilon, jnp.float32))
    c, xh, z = place[8], place[9], place[10]
    at = pl.ds(pl.multiple_of(c * members, members), members)
    util[...] = (fit[xh * Z + z, :, at] - mean) / root
    total = None
    for k in range(Z):
        for copy in copies[k]:
            copy.wait()
        row = (fit[xh * Z + k, :, at] - mean) / root
        scaled = (fout[k].astype(jnp.float32) * row).astype(jnp.bfloat16)
        one = jnp.dot(scaled, fin[k], preferred_element_type=jnp.float32)
        total = one if total is None else total + one
    total = total * (1.0 / np.sqrt(float(count)))
    rows = keep.shape[1]
    total = total.reshape(XH, CORE, rows, total.shape[1])
    for h in range(XH):
        to = jnp.bitwise_xor(xh, h)
        keep[to] = jnp.where(c == 0, total[h, 0], total[h, 1])
        give[to] = jnp.where(c == 0, total[h, 1], total[h, 0])


def weight_part(place, fit, fout, fin):
    rows, members = fout.shape[1], fout.shape[2]
    cols = fin.shape[2]
    vmem = pl.BlockSpec(memory_space=pltpu.VMEM)
    hbm = pl.BlockSpec(memory_space=pl.ANY)
    block = jax.ShapeDtypeStruct((XH, rows // (XH * CORE), cols), jnp.float32)
    return pl.pallas_call(
        step_kernel,
        out_shape=(block, block, jax.ShapeDtypeStruct((1, members), jnp.float32)),
        in_specs=[pl.BlockSpec(memory_space=pltpu.SMEM), vmem, hbm, hbm],
        out_specs=(vmem, vmem, vmem),
        scratch_shapes=[
            pltpu.VMEM(fout.shape, fout.dtype),
            pltpu.VMEM(fin.shape, fin.dtype),
            pltpu.SemaphoreType.DMA((Z, 2)),
        ],
        compiler_params=pltpu.CompilerParams(vmem_limit_bytes=LARGE_BYTES),
        cost_estimate=pl.CostEstimate(
            flops=2 * rows * Z * members * cols, bytes_accessed=4 * 1024 * 1024, transcendentals=0
        ),
    )(place, fit, fout, fin)


def share(x, axes):
    return lax.all_to_all(x, axes, 0, 0, tiled=True)


def shards(inputs, weight, factor_in, factor_out, readout):
    members, rows_here, width = inputs.shape
    out_width, block = weight.shape
    half = out_width // 2
    xh, z, c, xl, y = (lax.axis_index(a) for a in AXES)
    wa = xl * Y + y
    sign = 1 - 2 * c
    y_fwd, y_bwd, x_go, core_go = go_y(1), go_y(-1), go_x(), go_core()

    def send(v, pairs):
        return lax.ppermute(v, AXES, pairs)

    def col(xl_at, off):
        return xl_at * Y + lax.rem(y + off + Y, Y)

    xo = 1 - xl
    k_own, k_a, k_b, k_c = col(xl, 0), col(xl, -sign), col(xl, sign), col(xl, 2)
    k_d, k_e, k_f, k_g = col(xo, 0), col(xo, -sign), col(xo, sign), col(xo, 2)

    x_own = inputs.transpose(1, 0, 2)
    def col(xl_at, off):
        return xl_at * Y + lax.rem(y + off + Y, Y)

    xo = 1 - xl
    k_own, k_a, k_b, k_c = col(xl, 0), col(xl, -sign), col(xl, sign), col(xl, 2)
    k_d, k_e, k_f, k_g = col(xo, 0), col(xo, -sign), col(xo, sign), col(xo, 2)

    x_own = inputs.transpose(1, 0, 2)
    w_own = lax.dynamic_slice_in_dim(weight, c * half, half, 0)

    places = jnp.stack([k_own, k_a, k_d, k_b, k_e, k_f, k_c, k_g, c, xh, z]).astype(jnp.int32)

    part = half // CHAINS
    chains = range(CHAINS)
    own = [lax.dynamic_slice_in_dim(weight, c * half + h * part, part, 0) for h in chains]
    w_a = [send(w, y_fwd) for w in own]
    w_d = [send(w, x_go) for w in own]
    x_oth = send(x_own, core_go)

    fin_here = lax.dynamic_slice_in_dim(factor_in, wa * block, block, 1)
    fin_all = lax.all_gather(fin_here, "z", axis=0)
    pieces_here, cut_done = cut_factors(factor_out)
    pieces = lax.all_to_all(pieces_here, "z", 0, 0, tiled=True)
    fout_oth = send(factor_out, core_go)
    low_own = low_term(x_own, factor_in)
    low_oth = send(low_own, core_go)

    w_b, w_e, w_c, w_f, w_g = ([None] * CHAINS for _ in range(5))
    for h in chains:
        own[h], w_a[h], w_d[h] = after((own[h], w_a[h], w_d[h]))
        w_b[h] = send(own[h], y_bwd)
        w_e[h] = send(w_a[h], x_go)
    acc, token = group_matmul(0, places, x_own, x_oth, [own, w_a, w_d], None)
    for h in chains:
        w_a[h], w_b[h], w_e[h] = after((w_a[h], w_b[h], w_e[h]), token)
        w_c[h] = send(w_a[h], y_fwd)
        w_f[h] = send(w_b[h], x_go)
    acc, token = group_matmul(3, places, x_own, x_oth, [w_b, w_e], acc, extra=(low_own,))
    for h in chains:
        w_c[h], w_f[h], w_e[h] = after((w_c[h], w_f[h], w_e[h]), token)
        w_g[h] = send(w_c[h], x_go) if h == 0 else send(w_e[h], y_fwd)
    acc, token, x_last = group_matmul(5, places, x_own, x_oth, [w_f, w_c], acc, ahead=True)
    partial = last_matmul(
        places, *w_g, factor_out, fout_oth, x_last, acc, low_own, low_oth, readout[None]
    )
    (partial,) = after((partial,), pieces)

    fit = share(sum_and_copy(share(partial, ("core", "xl", "y"))), ("xh", "z"))

    keep, give, util = weight_part(places, fit, pieces, fin_all)
    summed = keep + send(give, core_go)
    weight_step = summed[0] + send(summed[1], go_xh())
    return weight_step, util.reshape(members)


def solution(mesh):
    fine = Mesh(mesh.devices.reshape(SIZES), AXES)
    pop, wa = ("xh", "z", "core"), ("xl", "y")
    placed = (P(pop, wa, None), P(None, wa), P(pop, None), P(pop, None), P())
    return jax.shard_map(
        shards, mesh=fine, in_specs=placed, out_specs=(P(pop, wa), P(pop)), check_vma=False
    )
```

```python
import functools

import jax
import jax.numpy as jnp
import numpy as np
from jax import lax
from jax.experimental import pallas as pl
from jax.experimental.pallas import tpu as pltpu
from jax.sharding import Mesh, PartitionSpec as P

perturb_scale = 0.5
epsilon = 1e-05

XH, Z, CORE, XL, Y = 2, 8, 2, 2, 4
AXES = ("xh", "z", "core", "xl", "y")
SIZES = (XH, Z, CORE, XL, Y)
WA = XL * Y
CHAINS = 2
ROWS_ALL = 24
VMEM_BYTES = 36 * 1024 * 1024
LAST_BYTES = 36 * 1024 * 1024
SMALL_BYTES = 1024 * 1024
LARGE_BYTES = 58 * 1024 * 1024


def permutation(move):
    pairs = []
    for i in range(int(np.prod(SIZES))):
        at = [int(v) for v in np.unravel_index(i, SIZES)]
        to = move(*at)
        pairs.append((i, int(np.ravel_multi_index(to, SIZES))))
    return pairs


def go_y(step):
    def move(xh, z, c, xl, y):
        s = step if c == 0 else -step
        return (xh, z, c, xl, (y + s) % Y)

    return permutation(move)


def go_x():
    def move(xh, z, c, xl, y):
        x = xh * 2 + xl
        if c == 0:
            x = x ^ 1
        else:
            x = (x + 1) % 4 if x % 2 else (x - 1) % 4
        return (x // 2, z, c, x % 2, y)

    return permutation(move)


def go_core():
    return permutation(lambda xh, z, c, xl, y: (xh, z, 1 - c, xl, y))


def go_xh():
    return permutation(lambda xh, z, c, xl, y: (1 - xh, z, c, xl, y))


def nt_dot(a, b):
    return lax.dot_general(a, b, (((1,), (1,)), ((), ())), preferred_element_type=jnp.float32)


def fetch(kidx, base, x_own, x_oth, sent, ws, w_sems, buffers, sems):
    count, part, block = len(sent), sent[0][0].shape[0], sent[0][0].shape[1]
    copies = [[], []]
    for side, x in ((0, x_own), (1, x_oth)):
        for s in range(count):
            cols = pl.ds(pl.multiple_of(kidx[base + s] * block, block), block)
            copies[side].append(
                pltpu.make_async_copy(x.at[:, :, cols], buffers.at[s, side], sems.at[s, side])
            )
            if side == 0:
                for h in range(CHAINS):
                    to = ws.at[s, pl.ds(h * part, part), :]
                    copies[side].append(pltpu.make_async_copy(sent[s][h], to, w_sems.at[s, h]))
    return copies


def fetch_scratch(count, members, width, block):
    return [
        pltpu.VMEM((count, width, block), jnp.bfloat16),
        pltpu.SemaphoreType.DMA((count, CHAINS)),
        pltpu.VMEM((count, 2, 3, members, block), jnp.bfloat16),
        pltpu.SemaphoreType.DMA((count, 2)),
    ]


def pairs(refs):
    return [refs[i : i + CHAINS] for i in range(0, len(refs), CHAINS)]


def group_kernel(base, count, has_acc, ahead, extra, kidx, x_own, x_oth, *refs):
    refs = refs[extra:]
    sent = pairs(refs[: count * CHAINS])
    acc_in = refs[count * CHAINS] if has_acc else None
    if ahead:
        *refs, x_last, ws, w_sems, buffers, sems, last_sems = refs
        refs = (*refs, ws, w_sems, buffers, sems)
    out, token, ws, w_sems, buffers, sems = refs[-6:]
    members, width = out.shape[2], out.shape[3]
    block = ws.shape[2]
    copies = fetch(kidx, base, x_own, x_oth, sent, ws, w_sems, buffers, sems)
    for copy in copies[0]:
        copy.start()
    early = []
    if ahead:
        cols = pl.ds(pl.multiple_of(kidx[base + count] * block, block), block)
        for side, x in ((0, x_own), (1, x_oth)):
            early.append(pltpu.make_async_copy(x.at[:, :, cols], x_last.at[side], last_sems.at[side]))
    token[...] = jnp.zeros_like(token)
    chunk = 512
    for side in range(2):
        for copy in copies[side]:
            copy.wait()
        if side == 0:
            for copy in copies[1] + early:
                copy.start()
        for j in range(0, width, chunk):
            cols = pl.ds(j, chunk)
            total = None
            for s in range(count):
                part = nt_dot(buffers[s, side].reshape(3 * members, block), ws[s, cols, :])
                total = part if total is None else total + part
            total = total.reshape(3, members, chunk)
            if has_acc:
                total = total + acc_in[side, :, :, cols]
            out[side, :, :, cols] = total
    for copy in early:
        copy.wait()


def group_matmul(base, kidx, x_own, x_oth, sent, acc, ahead=False, extra=()):
    count = len(sent)
    members = x_own.shape[1]
    part, block = sent[0][0].shape
    width = part * CHAINS
    smem = pl.BlockSpec(memory_space=pltpu.SMEM)
    vmem = pl.BlockSpec(memory_space=pltpu.VMEM)
    hbm = pl.BlockSpec(memory_space=pl.ANY)
    args = [x_own, x_oth, *extra] + [w for ws in sent for w in ws]
    specs = [smem] + [hbm] * len(args)
    alias = {}
    if acc is not None:
        specs.append(vmem)
        args.append(acc)
        alias = {len(args): 0}
    flops = 2 * 2 * 3 * members * width * block * count
    return pl.pallas_call(
        functools.partial(group_kernel, base, count, acc is not None, ahead, len(extra)),
        out_shape=(
            jax.ShapeDtypeStruct((2, 3, members, width), jnp.float32),
            jax.ShapeDtypeStruct((8, 128), jnp.float32),
        )
        + ((jax.ShapeDtypeStruct((2, 3, members, block), x_own.dtype),) if ahead else ()),
        in_specs=specs,
        out_specs=(vmem,) * (3 if ahead else 2),
        scratch_shapes=fetch_scratch(count, members, width, block)
        + ([pltpu.SemaphoreType.DMA((2,))] if ahead else []),
        input_output_aliases=alias,
        compiler_params=pltpu.CompilerParams(vmem_limit_bytes=VMEM_BYTES),
        cost_estimate=pl.CostEstimate(flops=flops, bytes_accessed=8 * 1024 * 1024, transcendentals=0),
    )(kidx, *args)


def last_kernel(kidx, w_lo, w_hi, fout_mine, fout_theirs, x, acc, low_own, low_oth, readout, out, ws, w_sems, fouts, f_sems):
    members, width = acc.shape[2], acc.shape[3]
    block = ws.shape[1]
    rows = w_lo.shape[0]
    first = pl.multiple_of(kidx[8] * width, width)
    copies = []
    for h, part in enumerate((w_lo, w_hi)):
        copies.append(pltpu.make_async_copy(part, ws.at[pl.ds(h * rows, rows), :], w_sems.at[h]))
    moves = []
    for side, fout in ((0, fout_mine), (1, fout_theirs)):
        moves.append(pltpu.make_async_copy(fout.at[:, pl.ds(first, width)], fouts.at[side], f_sems.at[side]))
    for copy in copies + moves:
        copy.start()
    for copy in copies:
        copy.wait()
    chunk = 256
    ones = jnp.ones((8, 128), jnp.float32)
    for side, low in ((0, low_own), (1, low_oth)):
        moves[side].wait()
        total = jnp.zeros((members, 128), jnp.float32)
        for j in range(0, width, chunk):
            cols = pl.ds(j, chunk)
            part = nt_dot(x[side].reshape(3 * members, block), ws[cols, :])
            part = part.reshape(3, members, chunk)
            shift = fouts[side, :, cols].astype(jnp.float32)
            summed = None
            for r in range(3):
                pert = part[r] + acc[side, r, :, cols] + low[r] * shift
                term = jnp.tanh(pert)
                summed = term if summed is None else summed + term
            summed = summed * readout[:, pl.ds(pl.multiple_of(first + j, chunk), chunk)]
            for h in range(0, chunk, 128):
                total = total + summed[:, h : h + 128]
        row = lax.dot_general(
            ones,
            total,
            (((1,), (1,)), ((), ())),
            preferred_element_type=jnp.float32,
            precision=lax.Precision.HIGHEST,
        )[0:1]
        at = pl.ds(pl.multiple_of(jnp.bitwise_xor(kidx[8], side) * members, members), members)
        for k in range(out.shape[0]):
            out[k, :, at] = row


def last_matmul(kidx, w_lo, w_hi, fout_mine, fout_theirs, x, acc, low_own, low_oth, readout):
    members = x.shape[2]
    block = w_lo.shape[1]
    width = acc.shape[3]
    smem = pl.BlockSpec(memory_space=pltpu.SMEM)
    vmem = pl.BlockSpec(memory_space=pltpu.VMEM)
    hbm = pl.BlockSpec(memory_space=pl.ANY)
    return pl.pallas_call(
        last_kernel,
        out_shape=jax.ShapeDtypeStruct((CORE * WA, 1, 2 * members), jnp.float32),
        in_specs=[smem] + [hbm] * 4 + [vmem] * 5,
        out_specs=vmem,
        scratch_shapes=[
            pltpu.VMEM((width, block), jnp.bfloat16),
            pltpu.SemaphoreType.DMA((2,)),
            pltpu.VMEM((2, members, width), jnp.bfloat16),
            pltpu.SemaphoreType.DMA((2,)),
        ],
        compiler_params=pltpu.CompilerParams(vmem_limit_bytes=LAST_BYTES),
        cost_estimate=pl.CostEstimate(
            flops=2 * 6 * members * width * block,
            bytes_accessed=6 * 1024 * 1024,
            transcendentals=6 * members * width,
        ),
    )(kidx, w_lo, w_hi, fout_mine, fout_theirs, x, acc, low_own, low_oth, readout)


def after_kernel(*refs):
    pass


def after(values, *done):
    hbm = pl.BlockSpec(memory_space=pl.ANY)
    count = len(values)
    return pl.pallas_call(
        after_kernel,
        out_shape=tuple(jax.ShapeDtypeStruct(v.shape, v.dtype) for v in values),
        in_specs=[hbm] * (count + len(done)),
        out_specs=(hbm,) * count,
        input_output_aliases={i: i for i in range(count)},
        compiler_params=pltpu.CompilerParams(vmem_limit_bytes=SMALL_BYTES),
    )(*values, *done)


def sum_kernel(got, out):
    out[...] = jnp.broadcast_to(jnp.sum(got[...], axis=0, keepdims=True) / ROWS_ALL, out.shape)


def sum_and_copy(got):
    vmem = pl.BlockSpec(memory_space=pltpu.VMEM)
    return pl.pallas_call(
        sum_kernel,
        out_shape=jax.ShapeDtypeStruct((XH * Z,) + got.shape[1:], jnp.float32),
        in_specs=[vmem],
        out_specs=vmem,
        compiler_params=pltpu.CompilerParams(vmem_limit_bytes=SMALL_BYTES),
    )(got)


def cut_kernel(fout, pieces, token):
    token[...] = jnp.zeros_like(token)
    half = fout.shape[1] // XH
    run = pieces.shape[1] // XH
    for h in range(XH):
        for k in range(Z):
            cols = pl.ds(h * half + k * run, run)
            pieces[k, pl.ds(h * run, run), :] = jnp.transpose(fout[:, cols])


def cut_factors(fout):
    members, out_width = fout.shape
    vmem = pl.BlockSpec(memory_space=pltpu.VMEM)
    return pl.pallas_call(
        cut_kernel,
        out_shape=(
            jax.ShapeDtypeStruct((Z, out_width // Z, members), fout.dtype),
            jax.ShapeDtypeStruct((8, 128), jnp.float32),
        ),
        in_specs=[vmem],
        out_specs=(vmem, vmem),
        compiler_params=pltpu.CompilerParams(vmem_limit_bytes=LARGE_BYTES),
        cost_estimate=pl.CostEstimate(flops=0, bytes_accessed=4 * 1024 * 1024, transcendentals=0),
    )(fout)


def low_kernel(x, fin, out, x_buf, f_buf, sems):
    tiles, rows, tile, width = x_buf.shape
    copies = []
    for t in range(tiles):
        span = pl.ds(t * tile, tile)
        pair = (
            pltpu.make_async_copy(x.at[:, span, :], x_buf.at[t], sems.at[t, 0]),
            pltpu.make_async_copy(fin.at[span, :], f_buf.at[t], sems.at[t, 1]),
        )
        for copy in pair:
            copy.start()
        copies.append(pair)
    chunk = 128
    for t in range(tiles):
        for copy in copies[t]:
            copy.wait()
        totals = [None] * rows
        for j in range(0, width, chunk):
            cols = pl.ds(j, chunk)
            f = f_buf[t, :, cols].astype(jnp.float32)
            for r in range(rows):
                term = x_buf[t, r, :, cols].astype(jnp.float32) * f
                totals[r] = term if totals[r] is None else totals[r] + term
        for r in range(rows):
            out[r, pl.ds(t * tile, tile), :] = perturb_scale * jnp.sum(totals[r], axis=1, keepdims=True)


def low_term(x, fin):
    rows, members, width = x.shape
    tile = 64
    tiles = members // tile
    hbm = pl.BlockSpec(memory_space=pl.ANY)
    return pl.pallas_call(
        low_kernel,
        out_shape=jax.ShapeDtypeStruct((rows, members, 1), jnp.float32),
        in_specs=[hbm, hbm],
        out_specs=pl.BlockSpec(memory_space=pltpu.VMEM),
        scratch_shapes=[
            pltpu.VMEM((tiles, rows, tile, width), jnp.bfloat16),
            pltpu.VMEM((tiles, tile, width), jnp.bfloat16),
            pltpu.SemaphoreType.DMA((tiles, 2)),
        ],
        compiler_params=pltpu.CompilerParams(vmem_limit_bytes=VMEM_BYTES),
        cost_estimate=pl.CostEstimate(
            flops=2 * rows * members * width, bytes_accessed=9 * 1024 * 1024, transcendentals=0
        ),
    )(x, fin)


def step_kernel(place, fit, fout_all, fin_all, keep, give, util, fout, fin, sems):
    copies = []
    for k in range(Z):
        pair = (
            pltpu.make_async_copy(fout_all.at[k], fout.at[k], sems.at[k, 0]),
            pltpu.make_async_copy(fin_all.at[k], fin.at[k], sems.at[k, 1]),
        )
        for copy in pair:
            copy.start()
        copies.append(pair)
    values = fit[...]
    members = fin.shape[1]
    count = values.shape[0] * values.shape[2]
    mean = jnp.sum(values) / count
    spread = jnp.sum((values - mean) ** 2) / count
    root = jnp.sqrt(jnp.full((1, 1), spread + epsilon, jnp.float32))
    c, xh, z = place[8], place[9], place[10]
    at = pl.ds(pl.multiple_of(c * members, members), members)
    util[...] = (fit[xh * Z + z, :, at] - mean) / root
    total = None
    for k in range(Z):
        for copy in copies[k]:
            copy.wait()
        row = (fit[xh * Z + k, :, at] - mean) / root
        scaled = (fout[k].astype(jnp.float32) * row).astype(jnp.bfloat16)
        one = jnp.dot(scaled, fin[k], preferred_element_type=jnp.float32)
        total = one if total is None else total + one
    total = total * (1.0 / np.sqrt(float(count)))
    rows = keep.shape[1]
    total = total.reshape(XH, CORE, rows, total.shape[1])
    for h in range(XH):
        to = jnp.bitwise_xor(xh, h)
        keep[to] = jnp.where(c == 0, total[h, 0], total[h, 1])
        give[to] = jnp.where(c == 0, total[h, 1], total[h, 0])


def weight_part(place, fit, fout, fin):
    rows, members = fout.shape[1], fout.shape[2]
    cols = fin.shape[2]
    vmem = pl.BlockSpec(memory_space=pltpu.VMEM)
    hbm = pl.BlockSpec(memory_space=pl.ANY)
    block = jax.ShapeDtypeStruct((XH, rows // (XH * CORE), cols), jnp.float32)
    return pl.pallas_call(
        step_kernel,
        out_shape=(block, block, jax.ShapeDtypeStruct((1, members), jnp.float32)),
        in_specs=[pl.BlockSpec(memory_space=pltpu.SMEM), vmem, hbm, hbm],
        out_specs=(vmem, vmem, vmem),
        scratch_shapes=[
            pltpu.VMEM(fout.shape, fout.dtype),
            pltpu.VMEM(fin.shape, fin.dtype),
            pltpu.SemaphoreType.DMA((Z, 2)),
        ],
        compiler_params=pltpu.CompilerParams(vmem_limit_bytes=48 * 1024 * 1024),
        cost_estimate=pl.CostEstimate(
            flops=2 * rows * Z * members * cols, bytes_accessed=4 * 1024 * 1024, transcendentals=0
        ),
    )(place, fit, fout, fin)


def share(x, axes):
    return lax.all_to_all(x, axes, 0, 0, tiled=True)


def shards(inputs, weight, factor_in, factor_out, readout):
    members, rows_here, width = inputs.shape
    out_width, block = weight.shape
    half = out_width // 2
    xh, z, c, xl, y = (lax.axis_index(a) for a in AXES)
    wa = xl * Y + y
    sign = 1 - 2 * c
    y_fwd, y_bwd, x_go, core_go = go_y(1), go_y(-1), go_x(), go_core()

    def send(v, pairs):
        return lax.ppermute(v, AXES, pairs)

    def col(xl_at, off):
        return xl_at * Y + lax.rem(y + off + Y, Y)

    xo = 1 - xl
    k_own, k_a, k_b, k_c = col(xl, 0), col(xl, -sign), col(xl, sign), col(xl, 2)
    k_d, k_e, k_f, k_g = col(xo, 0), col(xo, -sign), col(xo, sign), col(xo, 2)

    x_own = inputs.transpose(1, 0, 2)
    def col(xl_at, off):
        return xl_at * Y + lax.rem(y + off + Y, Y)

    xo = 1 - xl
    k_own, k_a, k_b, k_c = col(xl, 0), col(xl, -sign), col(xl, sign), col(xl, 2)
    k_d, k_e, k_f, k_g = col(xo, 0), col(xo, -sign), col(xo, sign), col(xo, 2)

    x_own = inputs.transpose(1, 0, 2)
    w_own = lax.dynamic_slice_in_dim(weight, c * half, half, 0)

    places = jnp.stack([k_own, k_a, k_d, k_b, k_e, k_f, k_c, k_g, c, xh, z]).astype(jnp.int32)

    part = half // CHAINS
    chains = range(CHAINS)
    own = [lax.dynamic_slice_in_dim(weight, c * half + h * part, part, 0) for h in chains]
    w_a = [send(w, y_fwd) for w in own]
    w_d = [send(w, x_go) for w in own]
    x_oth = send(x_own, core_go)

    fin_here = lax.dynamic_slice_in_dim(factor_in, wa * block, block, 1)
    fin_all = lax.all_gather(fin_here, "z", axis=0)
    pieces_here, cut_done = cut_factors(factor_out)
    pieces = lax.all_to_all(pieces_here, "z", 0, 0, tiled=True)
    fout_oth = send(factor_out, core_go)
    low_own = low_term(x_own, factor_in)
    low_oth = send(low_own, core_go)

    w_b, w_e, w_c, w_f, w_g = ([None] * CHAINS for _ in range(5))
    for h in chains:
        own[h], w_a[h], w_d[h] = after((own[h], w_a[h], w_d[h]))
        w_b[h] = send(own[h], y_bwd)
        w_e[h] = send(w_a[h], x_go)
    acc, token = group_matmul(0, places, x_own, x_oth, [own, w_a, w_d], None)
    for h in chains:
        w_a[h], w_b[h], w_e[h] = after((w_a[h], w_b[h], w_e[h]), token)
        w_c[h] = send(w_a[h], y_fwd)
        w_f[h] = send(w_b[h], x_go)
    acc, token = group_matmul(3, places, x_own, x_oth, [w_b, w_e], acc, extra=(low_own,))
    for h in chains:
        w_c[h], w_f[h], w_e[h] = after((w_c[h], w_f[h], w_e[h]), token)
        w_g[h] = send(w_c[h], x_go) if h == 0 else send(w_e[h], y_fwd)
    acc, token, x_last = group_matmul(5, places, x_own, x_oth, [w_f, w_c], acc, ahead=True)
    partial = last_matmul(
        places, *w_g, factor_out, fout_oth, x_last, acc, low_own, low_oth, readout[None]
    )
    (partial,) = after((partial,), pieces)

    fit = share(sum_and_copy(share(partial, ("core", "xl", "y"))), ("xh", "z"))

    keep, give, util = weight_part(places, fit, pieces, fin_all)
    summed = keep + send(give, core_go)
    weight_step = summed[0] + send(summed[1], go_xh())
    return weight_step, util.reshape(members)


def solution(mesh):
    fine = Mesh(mesh.devices.reshape(SIZES), AXES)
    pop, wa = ("xh", "z", "core"), ("xl", "y")
    placed = (P(pop, wa, None), P(None, wa), P(pop, None), P(pop, None), P())
    return jax.shard_map(
        shards, mesh=fine, in_specs=placed, out_specs=(P(pop, wa), P(pop)), check_vma=False
    )
```

```python
import functools

import jax
import jax.numpy as jnp
import numpy as np
from jax import lax
from jax.experimental import pallas as pl
from jax.experimental.pallas import tpu as pltpu
from jax.sharding import Mesh, PartitionSpec as P

perturb_scale = 0.5
epsilon = 1e-05

XH, Z, CORE, XL, Y = 2, 8, 2, 2, 4
AXES = ("xh", "z", "core", "xl", "y")
SIZES = (XH, Z, CORE, XL, Y)
WA = XL * Y
CHAINS = 2
ROWS_ALL = 24
VMEM_BYTES = 36 * 1024 * 1024
LAST_BYTES = 36 * 1024 * 1024
SMALL_BYTES = 1024 * 1024
STEP_BYTES = 54 * 1024 * 1024
LARGE_BYTES = 58 * 1024 * 1024


def permutation(move):
    pairs = []
    for i in range(int(np.prod(SIZES))):
        at = [int(v) for v in np.unravel_index(i, SIZES)]
        to = move(*at)
        pairs.append((i, int(np.ravel_multi_index(to, SIZES))))
    return pairs


def go_y(step):
    def move(xh, z, c, xl, y):
        s = step if c == 0 else -step
        return (xh, z, c, xl, (y + s) % Y)

    return permutation(move)


def go_x():
    def move(xh, z, c, xl, y):
        x = xh * 2 + xl
        if c == 0:
            x = x ^ 1
        else:
            x = (x + 1) % 4 if x % 2 else (x - 1) % 4
        return (x // 2, z, c, x % 2, y)

    return permutation(move)


def go_core():
    return permutation(lambda xh, z, c, xl, y: (xh, z, 1 - c, xl, y))


def go_xh():
    return permutation(lambda xh, z, c, xl, y: (1 - xh, z, c, xl, y))


def nt_dot(a, b):
    return lax.dot_general(a, b, (((1,), (1,)), ((), ())), preferred_element_type=jnp.float32)


def fetch(kidx, base, x_own, x_oth, sent, ws, w_sems, buffers, sems):
    count, part, block = len(sent), sent[0][0].shape[0], sent[0][0].shape[1]
    copies = [[], []]
    for side, x in ((0, x_own), (1, x_oth)):
        for s in range(count):
            cols = pl.ds(pl.multiple_of(kidx[base + s] * block, block), block)
            copies[side].append(
                pltpu.make_async_copy(x.at[:, :, cols], buffers.at[s, side], sems.at[s, side])
            )
            if side == 0:
                for h in range(CHAINS):
                    to = ws.at[s, pl.ds(h * part, part), :]
                    copies[side].append(pltpu.make_async_copy(sent[s][h], to, w_sems.at[s, h]))
    return copies


def fetch_scratch(count, members, width, block):
    return [
        pltpu.VMEM((count, width, block), jnp.bfloat16),
        pltpu.SemaphoreType.DMA((count, CHAINS)),
        pltpu.VMEM((count, 2, 3, members, block), jnp.bfloat16),
        pltpu.SemaphoreType.DMA((count, 2)),
    ]


def pairs(refs):
    return [refs[i : i + CHAINS] for i in range(0, len(refs), CHAINS)]


def group_kernel(base, count, has_acc, ahead, extra, kidx, x_own, x_oth, *refs):
    refs = refs[extra:]
    sent = pairs(refs[: count * CHAINS])
    acc_in = refs[count * CHAINS] if has_acc else None
    if ahead:
        *refs, x_last, ws, w_sems, buffers, sems, last_sems = refs
        refs = (*refs, ws, w_sems, buffers, sems)
    out, token, ws, w_sems, buffers, sems = refs[-6:]
    members, width = out.shape[2], out.shape[3]
    block = ws.shape[2]
    copies = fetch(kidx, base, x_own, x_oth, sent, ws, w_sems, buffers, sems)
    for copy in copies[0]:
        copy.start()
    early = []
    if ahead:
        cols = pl.ds(pl.multiple_of(kidx[base + count] * block, block), block)
        for side, x in ((0, x_own), (1, x_oth)):
            early.append(pltpu.make_async_copy(x.at[:, :, cols], x_last.at[side], last_sems.at[side]))
    token[...] = jnp.zeros_like(token)
    chunk = 512
    for side in range(2):
        for copy in copies[side]:
            copy.wait()
        if side == 0:
            for copy in copies[1] + early:
                copy.start()
        for j in range(0, width, chunk):
            cols = pl.ds(j, chunk)
            total = None
            for s in range(count):
                part = nt_dot(buffers[s, side].reshape(3 * members, block), ws[s, cols, :])
                total = part if total is None else total + part
            total = total.reshape(3, members, chunk)
            if has_acc:
                total = total + acc_in[side, :, :, cols]
            out[side, :, :, cols] = total
    for copy in early:
        copy.wait()


def group_matmul(base, kidx, x_own, x_oth, sent, acc, ahead=False, extra=()):
    count = len(sent)
    members = x_own.shape[1]
    part, block = sent[0][0].shape
    width = part * CHAINS
    smem = pl.BlockSpec(memory_space=pltpu.SMEM)
    vmem = pl.BlockSpec(memory_space=pltpu.VMEM)
    hbm = pl.BlockSpec(memory_space=pl.ANY)
    args = [x_own, x_oth, *extra] + [w for ws in sent for w in ws]
    specs = [smem] + [hbm] * len(args)
    alias = {}
    if acc is not None:
        specs.append(vmem)
        args.append(acc)
        alias = {len(args): 0}
    flops = 2 * 2 * 3 * members * width * block * count
    return pl.pallas_call(
        functools.partial(group_kernel, base, count, acc is not None, ahead, len(extra)),
        out_shape=(
            jax.ShapeDtypeStruct((2, 3, members, width), jnp.float32),
            jax.ShapeDtypeStruct((8, 128), jnp.float32),
        )
        + ((jax.ShapeDtypeStruct((2, 3, members, block), x_own.dtype),) if ahead else ()),
        in_specs=specs,
        out_specs=(vmem,) * (3 if ahead else 2),
        scratch_shapes=fetch_scratch(count, members, width, block)
        + ([pltpu.SemaphoreType.DMA((2,))] if ahead else []),
        input_output_aliases=alias,
        compiler_params=pltpu.CompilerParams(vmem_limit_bytes=VMEM_BYTES),
        cost_estimate=pl.CostEstimate(flops=flops, bytes_accessed=8 * 1024 * 1024, transcendentals=0),
    )(kidx, *args)


def last_kernel(kidx, w_lo, w_hi, fout_mine, fout_theirs, x, acc, low_own, low_oth, readout, out, ws, w_sems, fouts, f_sems):
    members, width = acc.shape[2], acc.shape[3]
    block = ws.shape[1]
    rows = w_lo.shape[0]
    first = pl.multiple_of(kidx[8] * width, width)
    copies = []
    for h, part in enumerate((w_lo, w_hi)):
        copies.append(pltpu.make_async_copy(part, ws.at[pl.ds(h * rows, rows), :], w_sems.at[h]))
    moves = []
    for side, fout in ((0, fout_mine), (1, fout_theirs)):
        moves.append(pltpu.make_async_copy(fout.at[:, pl.ds(first, width)], fouts.at[side], f_sems.at[side]))
    for copy in copies + moves:
        copy.start()
    for copy in copies:
        copy.wait()
    chunk = 256
    ones = jnp.ones((8, 128), jnp.float32)
    for side, low in ((0, low_own), (1, low_oth)):
        moves[side].wait()
        total = jnp.zeros((members, 128), jnp.float32)
        for j in range(0, width, chunk):
            cols = pl.ds(j, chunk)
            part = nt_dot(x[side].reshape(3 * members, block), ws[cols, :])
            part = part.reshape(3, members, chunk)
            shift = fouts[side, :, cols].astype(jnp.float32)
            summed = None
            for r in range(3):
                pert = part[r] + acc[side, r, :, cols] + low[r] * shift
                term = jnp.tanh(pert)
                summed = term if summed is None else summed + term
            summed = summed * readout[:, pl.ds(pl.multiple_of(first + j, chunk), chunk)]
            for h in range(0, chunk, 128):
                total = total + summed[:, h : h + 128]
        row = lax.dot_general(
            ones,
            total,
            (((1,), (1,)), ((), ())),
            preferred_element_type=jnp.float32,
            precision=lax.Precision.HIGHEST,
        )[0:1]
        at = pl.ds(pl.multiple_of(jnp.bitwise_xor(kidx[8], side) * members, members), members)
        for k in range(out.shape[0]):
            out[k, :, at] = row


def last_matmul(kidx, w_lo, w_hi, fout_mine, fout_theirs, x, acc, low_own, low_oth, readout):
    members = x.shape[2]
    block = w_lo.shape[1]
    width = acc.shape[3]
    smem = pl.BlockSpec(memory_space=pltpu.SMEM)
    vmem = pl.BlockSpec(memory_space=pltpu.VMEM)
    hbm = pl.BlockSpec(memory_space=pl.ANY)
    return pl.pallas_call(
        last_kernel,
        out_shape=jax.ShapeDtypeStruct((CORE * WA, 1, 2 * members), jnp.float32),
        in_specs=[smem] + [hbm] * 4 + [vmem] * 5,
        out_specs=vmem,
        scratch_shapes=[
            pltpu.VMEM((width, block), jnp.bfloat16),
            pltpu.SemaphoreType.DMA((2,)),
            pltpu.VMEM((2, members, width), jnp.bfloat16),
            pltpu.SemaphoreType.DMA((2,)),
        ],
        compiler_params=pltpu.CompilerParams(vmem_limit_bytes=LAST_BYTES),
        cost_estimate=pl.CostEstimate(
            flops=2 * 6 * members * width * block,
            bytes_accessed=6 * 1024 * 1024,
            transcendentals=6 * members * width,
        ),
    )(kidx, w_lo, w_hi, fout_mine, fout_theirs, x, acc, low_own, low_oth, readout)


def after_kernel(*refs):
    pass


def after(values, *done):
    hbm = pl.BlockSpec(memory_space=pl.ANY)
    count = len(values)
    return pl.pallas_call(
        after_kernel,
        out_shape=tuple(jax.ShapeDtypeStruct(v.shape, v.dtype) for v in values),
        in_specs=[hbm] * (count + len(done)),
        out_specs=(hbm,) * count,
        input_output_aliases={i: i for i in range(count)},
        compiler_params=pltpu.CompilerParams(vmem_limit_bytes=SMALL_BYTES),
    )(*values, *done)


def sum_kernel(got, out):
    out[...] = jnp.broadcast_to(jnp.sum(got[...], axis=0, keepdims=True) / ROWS_ALL, out.shape)


def sum_and_copy(got):
    vmem = pl.BlockSpec(memory_space=pltpu.VMEM)
    return pl.pallas_call(
        sum_kernel,
        out_shape=jax.ShapeDtypeStruct((XH * Z,) + got.shape[1:], jnp.float32),
        in_specs=[vmem],
        out_specs=vmem,
        compiler_params=pltpu.CompilerParams(vmem_limit_bytes=SMALL_BYTES),
    )(got)


def cut_kernel(fout, pieces, token):
    token[...] = jnp.zeros_like(token)
    half = fout.shape[1] // XH
    run = pieces.shape[1] // XH
    for h in range(XH):
        for k in range(Z):
            cols = pl.ds(h * half + k * run, run)
            pieces[k, pl.ds(h * run, run), :] = jnp.transpose(fout[:, cols])


def cut_factors(fout):
    members, out_width = fout.shape
    vmem = pl.BlockSpec(memory_space=pltpu.VMEM)
    return pl.pallas_call(
        cut_kernel,
        out_shape=(
            jax.ShapeDtypeStruct((Z, out_width // Z, members), fout.dtype),
            jax.ShapeDtypeStruct((8, 128), jnp.float32),
        ),
        in_specs=[vmem],
        out_specs=(vmem, vmem),
        compiler_params=pltpu.CompilerParams(vmem_limit_bytes=LARGE_BYTES),
        cost_estimate=pl.CostEstimate(flops=0, bytes_accessed=4 * 1024 * 1024, transcendentals=0),
    )(fout)


def low_kernel(x, fin, out, x_buf, f_buf, sems):
    tiles, rows, tile, width = x_buf.shape
    copies = []
    for t in range(tiles):
        span = pl.ds(t * tile, tile)
        pair = (
            pltpu.make_async_copy(x.at[:, span, :], x_buf.at[t], sems.at[t, 0]),
            pltpu.make_async_copy(fin.at[span, :], f_buf.at[t], sems.at[t, 1]),
        )
        for copy in pair:
            copy.start()
        copies.append(pair)
    chunk = 128
    for t in range(tiles):
        for copy in copies[t]:
            copy.wait()
        totals = [None] * rows
        for j in range(0, width, chunk):
            cols = pl.ds(j, chunk)
            f = f_buf[t, :, cols].astype(jnp.float32)
            for r in range(rows):
                term = x_buf[t, r, :, cols].astype(jnp.float32) * f
                totals[r] = term if totals[r] is None else totals[r] + term
        for r in range(rows):
            out[r, pl.ds(t * tile, tile), :] = perturb_scale * jnp.sum(totals[r], axis=1, keepdims=True)


def low_term(x, fin):
    rows, members, width = x.shape
    tile = 64
    tiles = members // tile
    hbm = pl.BlockSpec(memory_space=pl.ANY)
    return pl.pallas_call(
        low_kernel,
        out_shape=jax.ShapeDtypeStruct((rows, members, 1), jnp.float32),
        in_specs=[hbm, hbm],
        out_specs=pl.BlockSpec(memory_space=pltpu.VMEM),
        scratch_shapes=[
            pltpu.VMEM((tiles, rows, tile, width), jnp.bfloat16),
            pltpu.VMEM((tiles, tile, width), jnp.bfloat16),
            pltpu.SemaphoreType.DMA((tiles, 2)),
        ],
        compiler_params=pltpu.CompilerParams(vmem_limit_bytes=VMEM_BYTES),
        cost_estimate=pl.CostEstimate(
            flops=2 * rows * members * width, bytes_accessed=9 * 1024 * 1024, transcendentals=0
        ),
    )(x, fin)


def step_kernel(place, fit, fout_all, fin_all, keep, give, util, fout, fin, sems):
    copies = []
    for k in range(Z):
        pair = (
            pltpu.make_async_copy(fout_all.at[k], fout.at[k], sems.at[k, 0]),
            pltpu.make_async_copy(fin_all.at[k], fin.at[k], sems.at[k, 1]),
        )
        for copy in pair:
            copy.start()
        copies.append(pair)
    values = fit[...]
    members = fin.shape[1]
    count = values.shape[0] * values.shape[2]
    mean = jnp.sum(values) / count
    spread = jnp.sum((values - mean) ** 2) / count
    root = jnp.sqrt(jnp.full((1, 1), spread + epsilon, jnp.float32))
    c, xh, z = place[8], place[9], place[10]
    at = pl.ds(pl.multiple_of(c * members, members), members)
    util[...] = (fit[xh * Z + z, :, at] - mean) / root
    total = None
    for k in range(Z):
        for copy in copies[k]:
            copy.wait()
        row = (fit[xh * Z + k, :, at] - mean) / root
        scaled = (fout[k].astype(jnp.float32) * row).astype(jnp.bfloat16)
        one = jnp.dot(scaled, fin[k], preferred_element_type=jnp.float32)
        total = one if total is None else total + one
    total = total * (1.0 / np.sqrt(float(count)))
    rows = keep.shape[1]
    total = total.reshape(XH, CORE, rows, total.shape[1])
    for h in range(XH):
        to = jnp.bitwise_xor(xh, h)
        keep[to] = jnp.where(c == 0, total[h, 0], total[h, 1])
        give[to] = jnp.where(c == 0, total[h, 1], total[h, 0])


def weight_part(place, fit, fout, fin):
    rows, members = fout.shape[1], fout.shape[2]
    cols = fin.shape[2]
    vmem = pl.BlockSpec(memory_space=pltpu.VMEM)
    hbm = pl.BlockSpec(memory_space=pl.ANY)
    block = jax.ShapeDtypeStruct((XH, rows // (XH * CORE), cols), jnp.float32)
    return pl.pallas_call(
        step_kernel,
        out_shape=(block, block, jax.ShapeDtypeStruct((1, members), jnp.float32)),
        in_specs=[pl.BlockSpec(memory_space=pltpu.SMEM), vmem, hbm, hbm],
        out_specs=(vmem, vmem, vmem),
        scratch_shapes=[
            pltpu.VMEM(fout.shape, fout.dtype),
            pltpu.VMEM(fin.shape, fin.dtype),
            pltpu.SemaphoreType.DMA((Z, 2)),
        ],
        compiler_params=pltpu.CompilerParams(vmem_limit_bytes=STEP_BYTES),
        cost_estimate=pl.CostEstimate(
            flops=2 * rows * Z * members * cols, bytes_accessed=4 * 1024 * 1024, transcendentals=0
        ),
    )(place, fit, fout, fin)


def share(x, axes):
    return lax.all_to_all(x, axes, 0, 0, tiled=True)


def shards(inputs, weight, factor_in, factor_out, readout):
    members, rows_here, width = inputs.shape
    out_width, block = weight.shape
    half = out_width // 2
    xh, z, c, xl, y = (lax.axis_index(a) for a in AXES)
    wa = xl * Y + y
    sign = 1 - 2 * c
    y_fwd, y_bwd, x_go, core_go = go_y(1), go_y(-1), go_x(), go_core()

    def send(v, pairs):
        return lax.ppermute(v, AXES, pairs)

    def col(xl_at, off):
        return xl_at * Y + lax.rem(y + off + Y, Y)

    xo = 1 - xl
    k_own, k_a, k_b, k_c = col(xl, 0), col(xl, -sign), col(xl, sign), col(xl, 2)
    k_d, k_e, k_f, k_g = col(xo, 0), col(xo, -sign), col(xo, sign), col(xo, 2)

    x_own = inputs.transpose(1, 0, 2)
    def col(xl_at, off):
        return xl_at * Y + lax.rem(y + off + Y, Y)

    xo = 1 - xl
    k_own, k_a, k_b, k_c = col(xl, 0), col(xl, -sign), col(xl, sign), col(xl, 2)
    k_d, k_e, k_f, k_g = col(xo, 0), col(xo, -sign), col(xo, sign), col(xo, 2)

    x_own = inputs.transpose(1, 0, 2)
    w_own = lax.dynamic_slice_in_dim(weight, c * half, half, 0)

    places = jnp.stack([k_own, k_a, k_d, k_b, k_e, k_f, k_c, k_g, c, xh, z]).astype(jnp.int32)

    part = half // CHAINS
    chains = range(CHAINS)
    own = [lax.dynamic_slice_in_dim(weight, c * half + h * part, part, 0) for h in chains]
    w_a = [send(w, y_fwd) for w in own]
    w_d = [send(w, x_go) for w in own]
    x_oth = send(x_own, core_go)

    fin_here = lax.dynamic_slice_in_dim(factor_in, wa * block, block, 1)
    fin_all = lax.all_gather(fin_here, "z", axis=0)
    pieces_here, cut_done = cut_factors(factor_out)
    pieces = lax.all_to_all(pieces_here, "z", 0, 0, tiled=True)
    fout_oth = send(factor_out, core_go)
    low_own = low_term(x_own, factor_in)
    low_oth = send(low_own, core_go)

    w_b, w_e, w_c, w_f, w_g = ([None] * CHAINS for _ in range(5))
    for h in chains:
        own[h], w_a[h], w_d[h] = after((own[h], w_a[h], w_d[h]))
        w_b[h] = send(own[h], y_bwd)
        w_e[h] = send(w_a[h], x_go)
    acc, token = group_matmul(0, places, x_own, x_oth, [own, w_a, w_d], None)
    for h in chains:
        w_a[h], w_b[h], w_e[h] = after((w_a[h], w_b[h], w_e[h]), token)
        w_c[h] = send(w_a[h], y_fwd)
        w_f[h] = send(w_b[h], x_go)
    acc, token = group_matmul(3, places, x_own, x_oth, [w_b, w_e], acc, extra=(low_own,))
    for h in chains:
        w_c[h], w_f[h], w_e[h] = after((w_c[h], w_f[h], w_e[h]), token)
        w_g[h] = send(w_c[h], x_go) if h == 0 else send(w_e[h], y_fwd)
    acc, token, x_last = group_matmul(5, places, x_own, x_oth, [w_f, w_c], acc, ahead=True)
    partial = last_matmul(
        places, *w_g, factor_out, fout_oth, x_last, acc, low_own, low_oth, readout[None]
    )
    (partial,) = after((partial,), pieces)

    fit = share(sum_and_copy(share(partial, ("core", "xl", "y"))), ("xh", "z"))

    keep, give, util = weight_part(places, fit, pieces, fin_all)
    summed = keep + send(give, core_go)
    weight_step = summed[0] + send(summed[1], go_xh())
    return weight_step, util.reshape(members)


def solution(mesh):
    fine = Mesh(mesh.devices.reshape(SIZES), AXES)
    pop, wa = ("xh", "z", "core"), ("xl", "y")
    placed = (P(pop, wa, None), P(None, wa), P(pop, None), P(pop, None), P())
    return jax.shard_map(
        shards, mesh=fine, in_specs=placed, out_specs=(P(pop, wa), P(pop)), check_vma=False
    )
```
